32 devices in a mesh: rows: 4 (over z), cols: 8 (over y, x, core).
Axes of the slice: x: 2, y: 2, z: 4, core: 2. Of those that a mesh axis runs over, the one named last changes fastest.
Arguments:
- global_in: bfloat16 [8, 32, 1024], P('rows', None, 'cols'), may hold values from -6 to 6
- global_first: bfloat16 [3, 3, 1024, 1024], P(None, None, None, 'cols'), may hold values from -0.0625 to 0.0625
- global_second: bfloat16 [3, 3, 1024, 1024], P(None, None, None, 'cols'), may hold values from -0.0625 to 0.0625
- project_weight: bfloat16 [1024, 128], replicated, may hold values from -0.1875 to 0.1875
- enhancer_input: bfloat16 [128, 512, 128], P('rows', 'cols'), may hold values from -6 to 6
- instance_map: int32 [128, 512], P('rows', 'cols'), may hold values from 0 to 255, as said below
- encoder_features: float32 [16, 128, 512], P(None, 'rows', 'cols'), may hold values from -5 to 5
- instance_weight: float32 [16, 128], replicated, may hold values from -4 to 4
- enhancer_first: bfloat16 [3, 3, 128, 128], replicated, may hold values from -0.1875 to 0.1875
- enhancer_second: bfloat16 [3, 3, 128, 128], replicated, may hold values from -0.1875 to 0.1875
- output_cotangent: bfloat16 [128, 512, 128], P('rows', 'cols'), may hold values from -6 to 6
Outputs:
- enhanced: bfloat16 [128, 512, 128], P('rows', 'cols')
- gradient_first: float32 [3, 3, 128, 128], replicated
- gradient_second: float32 [3, 3, 128, 128], replicated
- global_gradient: float32 [8, 32, 128], P('rows', 'cols')
The draws below stay inside these ranges and needn't reach their ends.
Inputs may be any that keep to these rules, and one draw needn't show every extreme that they name: `instance_map`: constant on each aligned 16 x 16 block of fine pixels.
All inputs are finite; a program needn't handle non-finite values.
Results may differ from the reference program's by a relative error of at most 0.0075.
Values may be sent and summed in bfloat16 or wider, within the bound.
No kernel may reach another device: no remote copies, remote signals or barrier semaphores. Data moves between devices by JAX's collectives and lax.ppermute only.
A program may use at most 64 MiB of HBM per device.

```python
import math
import jax
import jax.numpy as jnp
from jax import lax

GLOBAL_WIDTH = 1024
LOCAL_WIDTH = 128
ENCODER_WIDTH = 16
INSTANCES = 256
UPSCALE = 16
MAP_ROWS = 128
MAP_COLS = 512
COARSE_ROWS = 8
COARSE_COLS = 32


def draw_instance_map(key, part):
    block_rows = MAP_ROWS // UPSCALE
    block_cols = MAP_COLS // UPSCALE
    first_draw = jax.random.randint(jax.random.fold_in(key, 11), (block_rows, block_cols), 0, INSTANCES)
    second_draw = jax.random.randint(jax.random.fold_in(key, 12), (block_rows, block_cols), 0, INSTANCES)
    labels = jnp.minimum(first_draw, second_draw)
    half_rows = block_rows // 2
    copied = jax.random.randint(jax.random.fold_in(key, 13), (half_rows, block_cols), 0, 2)
    upper = labels[:half_rows]
    lower = jnp.where(copied == 1, upper, labels[half_rows:2 * half_rows])
    labels = jnp.concatenate([upper, lower, labels[2 * half_rows:]], axis=0)
    labels = labels.at[0, 0].set(INSTANCES - 1)
    return jnp.repeat(jnp.repeat(labels, UPSCALE, 0), UPSCALE, 1).astype(jnp.int32)


def draw_encoder_features(key, part):
    base_key = jax.random.fold_in(key, 21)
    noise_key = jax.random.fold_in(key, 22)
    base = jnp.clip(jax.random.normal(base_key, (ENCODER_WIDTH, MAP_ROWS // UPSCALE, MAP_COLS // UPSCALE), jnp.float32), -4.0, 4.0)
    noise = jnp.clip(0.3 * jax.random.normal(noise_key, (ENCODER_WIDTH, MAP_ROWS, MAP_COLS), jnp.float32), -1.0, 1.0)
    return (jnp.repeat(jnp.repeat(base, UPSCALE, 1), UPSCALE, 2) + noise).astype(jnp.float32)


def block_scale(stream_key, dims, cuts, least, top_value):
    def one(position, shards_of):
        steps = jax.random.uniform(jax.random.fold_in(jax.random.fold_in(stream_key, 6), position), (shards_of,), jnp.float32, least / len(cuts), top_value / len(cuts))
        return jnp.repeat(jnp.exp(steps), dims[position] // shards_of).reshape((-1,) + (1,) * (len(dims) - position - 1))

    loudness = one(*cuts[0])
    for cut in cuts[1:]:
        loudness = loudness * one(*cut)
    return loudness


def normal_values(key, extent, width, reach, cuts=(), kind=jnp.bfloat16):
    values = width * jax.random.normal(key, extent, jnp.float32)
    if cuts:
        values = values * block_scale(key, extent, cuts, -0.22, 0.18)
    return jnp.clip(values, -reach, reach).astype(kind)


def setup_inputs(seed: int = 0) -> dict:
    arg_keys = jax.random.split(jax.random.key(seed), 12)
    global_in = normal_values(arg_keys[0], (COARSE_ROWS, COARSE_COLS, GLOBAL_WIDTH), 1.0, 6.0, ((0, 4), (2, 8)))
    global_first = normal_values(arg_keys[1], (3, 3, GLOBAL_WIDTH, GLOBAL_WIDTH), (9 * GLOBAL_WIDTH) ** -0.5, 0.0625, ((3, 8),))
    global_second = normal_values(arg_keys[2], (3, 3, GLOBAL_WIDTH, GLOBAL_WIDTH), (9 * GLOBAL_WIDTH) ** -0.5, 0.0625, ((3, 8),))
    project_weight = normal_values(arg_keys[3], (GLOBAL_WIDTH, LOCAL_WIDTH), GLOBAL_WIDTH ** -0.5, 0.1875)
    enhancer_input = normal_values(arg_keys[4], (MAP_ROWS, MAP_COLS, LOCAL_WIDTH), 1.0, 6.0, ((0, 4), (1, 8)))
    instance_map = draw_instance_map(jax.random.fold_in(arg_keys[11], 71), 0)
    encoder_features = draw_encoder_features(jax.random.fold_in(arg_keys[11], 71), 0)
    instance_weight = normal_values(arg_keys[7], (ENCODER_WIDTH, LOCAL_WIDTH), 1.0, 4.0, (), jnp.float32)
    enhancer_first = normal_values(arg_keys[8], (3, 3, LOCAL_WIDTH, LOCAL_WIDTH), (9 * LOCAL_WIDTH) ** -0.5, 0.1875)
    enhancer_second = normal_values(arg_keys[9], (3, 3, LOCAL_WIDTH, LOCAL_WIDTH), (9 * LOCAL_WIDTH) ** -0.5, 0.1875)
    output_cotangent = normal_values(arg_keys[10], (MAP_ROWS, MAP_COLS, LOCAL_WIDTH), 1.0, 6.0, ((0, 4), (1, 8)))
    return {"global_in": global_in, "global_first": global_first, "global_second": global_second, "project_weight": project_weight, "enhancer_input": enhancer_input, "instance_map": instance_map, "encoder_features": encoder_features, "instance_weight": instance_weight, "enhancer_first": enhancer_first, "enhancer_second": enhancer_second, "output_cotangent": output_cotangent}


norm_eps = 1e-05

def pad_map(field):
    return jnp.pad(field, ((1, 1), (1, 1), (0, 0)))

def conv_taps(padded, weight, row_count, col_count):
    summed = jnp.zeros((row_count * col_count, weight.shape[3]), jnp.float32)
    for tap_row in range(3):
        for tap_col in range(3):
            window = padded[tap_row:tap_row + row_count, tap_col:tap_col + col_count]
            summed = summed + jnp.dot(window.reshape(row_count * col_count, window.shape[2]), weight[tap_row, tap_col], preferred_element_type=jnp.float32)
    return summed

def back_taps(padded, weight, row_count, col_count):
    summed = jnp.zeros((row_count * col_count, weight.shape[2]), jnp.float32)
    for tap_row in range(3):
        for tap_col in range(3):
            window = padded[2 - tap_row:2 - tap_row + row_count, 2 - tap_col:2 - tap_col + col_count]
            summed = summed + jnp.dot(window.reshape(row_count * col_count, window.shape[2]), weight[tap_row, tap_col].T, preferred_element_type=jnp.float32)
    return summed

def weight_taps(padded, gradient, row_count, col_count):
    flattened = gradient.reshape(row_count * col_count, gradient.shape[2])
    stacked = []
    for tap_row in range(3):
        line = []
        for tap_col in range(3):
            window = padded[tap_row:tap_row + row_count, tap_col:tap_col + col_count]
            line.append(lax.dot_general(window.reshape(row_count * col_count, window.shape[2]), flattened, (((0,), (0,)), ((), ())), preferred_element_type=jnp.float32))
        stacked.append(jnp.stack(line))
    return jnp.stack(stacked)

def reference(global_in, global_first, global_second, project_weight, enhancer_input, instance_map, encoder_features, instance_weight, enhancer_first, enhancer_second, output_cotangent):
    coarse_rows, coarse_cols, global_width = global_in.shape
    map_rows, map_cols, local_width = enhancer_input.shape
    first_raw = conv_taps(pad_map(global_in), global_first, coarse_rows, coarse_cols)
    band_total = coarse_rows * coarse_cols
    band_mean = lax.optimization_barrier(jnp.sum(first_raw, 0)) / band_total
    band_var = lax.optimization_barrier(jnp.sum(first_raw * first_raw, 0)) / band_total - band_mean * band_mean
    normed = (first_raw - band_mean) * lax.rsqrt(band_var + norm_eps)
    hidden = jnp.maximum(normed, 0.0).astype(jnp.bfloat16).reshape(coarse_rows, coarse_cols, global_width)
    second_raw = conv_taps(pad_map(hidden), global_second, coarse_rows, coarse_cols)
    global_out = (global_in.astype(jnp.float32).reshape(-1, global_width) + second_raw).astype(jnp.bfloat16)
    coarse = jnp.dot(global_out, project_weight, preferred_element_type=jnp.float32).astype(jnp.bfloat16)
    coarse = coarse.reshape(coarse_rows, coarse_cols, local_width)
    pixel_labels = instance_map.reshape(-1)
    flat_features = encoder_features.reshape(encoder_features.shape[0], -1).T
    feature_sums = jax.ops.segment_sum(flat_features, pixel_labels, num_segments=INSTANCES)
    member_counts = jax.ops.segment_sum(jnp.ones(pixel_labels.shape, jnp.float32), pixel_labels, num_segments=INSTANCES)
    averages = feature_sums / jnp.maximum(member_counts, 1.0)[:, None]
    lookup = jnp.dot(averages, instance_weight, precision=lax.Precision.HIGHEST)
    pooled = jnp.take(lookup, pixel_labels, axis=0).reshape(map_rows, map_cols, local_width)
    upsampled = jnp.repeat(jnp.repeat(coarse, UPSCALE, 0), UPSCALE, 1)
    mixed = (enhancer_input.astype(jnp.float32) + upsampled.astype(jnp.float32) + pooled).astype(jnp.bfloat16)
    mixed_padded = pad_map(mixed)
    first_act = conv_taps(mixed_padded, enhancer_first, map_rows, map_cols)
    pixel_total = map_rows * map_cols
    act_mean = lax.optimization_barrier(jnp.sum(first_act, 0)) / pixel_total
    act_var = lax.optimization_barrier(jnp.sum(first_act * first_act, 0)) / pixel_total - act_mean * act_mean
    inverse_dev = lax.rsqrt(act_var + norm_eps)
    normed_act = (first_act - act_mean) * inverse_dev
    activated = jax.nn.silu(normed_act).astype(jnp.bfloat16).reshape(map_rows, map_cols, local_width)
    active_padded = pad_map(activated)
    second_act = conv_taps(active_padded, enhancer_second, map_rows, map_cols)
    enhanced = (mixed.astype(jnp.float32).reshape(-1, local_width) + second_act).astype(jnp.bfloat16).reshape(map_rows, map_cols, local_width)
    second_sum = weight_taps(active_padded, output_cotangent, map_rows, map_cols)
    act_grad = back_taps(pad_map(output_cotangent), enhancer_second, map_rows, map_cols)
    gate_value = jax.nn.sigmoid(normed_act)
    normed_grad = act_grad * gate_value * (1.0 + normed_act * (1.0 - gate_value))
    grad_mean = lax.optimization_barrier(jnp.sum(normed_grad, 0)) / pixel_total
    cross_mean = lax.optimization_barrier(jnp.sum(normed_grad * normed_act, 0)) / pixel_total
    first_grad = (inverse_dev * (normed_grad - grad_mean - normed_act * cross_mean)).astype(jnp.bfloat16).reshape(map_rows, map_cols, local_width)
    first_sum = weight_taps(mixed_padded, first_grad, map_rows, map_cols)
    mixed_grad = output_cotangent.astype(jnp.float32).reshape(-1, local_width) + back_taps(pad_map(first_grad), enhancer_first, map_rows, map_cols)
    rescale = 1.0 / math.sqrt(pixel_total)
    global_gradient = mixed_grad.reshape(coarse_rows, UPSCALE, coarse_cols, UPSCALE, local_width).sum(axis=(1, 3)) / UPSCALE
    return (enhanced, first_sum * rescale, second_sum * rescale, global_gradient)
```

```python
import math

import jax
import jax.numpy as jnp
from jax import lax
from jax.sharding import PartitionSpec as P

INSTANCES = 256
UPSCALE = 16
BOTH = ("rows", "cols")

norm_eps = 1e-05


def halo_2(array, axis, dim, width):
    devices, length = (lax.axis_size(axis), array.shape[dim])
    up = [(i, i + 1) for i in range(devices - 1)]
    down = [(j, i) for i, j in up]
    last = lax.slice_in_dim(array, length - width, length, axis=dim)
    initial = lax.slice_in_dim(array, 0, width, axis=dim)
    before = lax.ppermute(last, axis, up)
    after = lax.ppermute(initial, axis, down)
    return jnp.concatenate([before, array, after], axis=dim)


def conv_taps(padded, weight, row_count, col_count):
    summed = jnp.zeros((row_count * col_count, weight.shape[3]), jnp.float32)
    for tap_row in range(3):
        for tap_col in range(3):
            window = padded[tap_row : tap_row + row_count, tap_col : tap_col + col_count]
            summed = summed + jnp.dot(
                window.reshape(row_count * col_count, window.shape[2]),
                weight[tap_row, tap_col],
                preferred_element_type=jnp.float32,
            )
    return summed


def back_taps(padded, weight, row_count, col_count):
    summed = jnp.zeros((row_count * col_count, weight.shape[2]), jnp.float32)
    for tap_row in range(3):
        for tap_col in range(3):
            window = padded[
                2 - tap_row : 2 - tap_row + row_count, 2 - tap_col : 2 - tap_col + col_count
            ]
            summed = summed + jnp.dot(
                window.reshape(row_count * col_count, window.shape[2]),
                weight[tap_row, tap_col].T,
                preferred_element_type=jnp.float32,
            )
    return summed


def weight_taps(padded, gradient, row_count, col_count):
    flattened = gradient.reshape(row_count * col_count, gradient.shape[2])
    stacked = []
    for tap_row in range(3):
        for tap_col in range(3):
            window = padded[tap_row : tap_row + row_count, tap_col : tap_col + col_count]
            stacked.append(
                lax.dot_general(
                    window.reshape(row_count * col_count, window.shape[2]),
                    flattened,
                    (((0,), (0,)), ((), ())),
                    preferred_element_type=jnp.float32,
                )
            )
    return jnp.concatenate(stacked)


def pieces(array):
    high = array.astype(jnp.bfloat16)
    rest = array - high.astype(jnp.float32)
    middle = rest.astype(jnp.bfloat16)
    return high, middle, (rest - middle.astype(jnp.float32)).astype(jnp.bfloat16)


def per_device(
    global_in,
    global_first,
    global_second,
    project_weight,
    enhancer_input,
    instance_map,
    encoder_features,
    instance_weight,
    enhancer_first,
    enhancer_second,
    output_cotangent,
):
    row_devices, col_devices = lax.axis_size("rows"), lax.axis_size("cols")
    devices = row_devices * col_devices
    my_row, my_col = lax.axis_index("rows"), lax.axis_index("cols")
    band_rows, band_cols, width_share = global_in.shape
    tile_rows, tile_cols, local_width = enhancer_input.shape
    coarse_rows = band_rows * row_devices
    block_rows = tile_rows // UPSCALE
    block_cols = tile_cols // UPSCALE
    blocks = block_rows * block_cols
    encoder_width = encoder_features.shape[0]

    block_labels = instance_map[::UPSCALE, ::UPSCALE].reshape(-1)
    block_sums = (
        encoder_features.reshape(encoder_width, block_rows, UPSCALE, block_cols, UPSCALE)
        .sum(axis=(2, 4))
        .reshape(-1)
    )
    extra = jnp.concatenate([*pieces(block_sums), block_labels.astype(jnp.bfloat16)])
    extra_rows = -(-extra.shape[0] // 2048) * 16
    extra = jnp.pad(extra, (0, extra_rows * 128 - extra.shape[0])).reshape(extra_rows, 128)
    packed = jnp.concatenate([global_in.reshape(-1, 128), extra])
    everything = lax.all_gather(packed, BOTH, axis=0)
    main_rows = packed.shape[0] - extra_rows
    gathered = everything[:, :main_rows].reshape(
        row_devices, col_devices, band_rows, band_cols, width_share
    )
    tail = everything[:, main_rows:].reshape(devices, -1)
    sums = blocks * encoder_width
    all_sums = sum(tail[:, k * sums : (k + 1) * sums].astype(jnp.float32) for k in (2, 1, 0))
    all_sums = (
        all_sums.reshape(row_devices, col_devices, encoder_width, block_rows, block_cols)
        .transpose(0, 3, 1, 4, 2)
        .reshape(-1, encoder_width)
    )
    all_labels = (
        tail[:, 3 * sums : 3 * sums + blocks]
        .reshape(row_devices, col_devices, block_rows, block_cols)
        .transpose(0, 2, 1, 3)
    )
    label_map = jnp.pad(
        all_labels.reshape(coarse_rows, band_cols), 1, constant_values=-1.0
    )
    near_labels = lax.dynamic_slice(
        label_map,
        (my_row * block_rows, my_col * block_cols),
        (block_rows + 2, block_cols + 2),
    ).reshape(-1)
    same = (near_labels[:, None] == all_labels.reshape(-1)[None, :]).astype(jnp.float32)
    near_sums = jnp.dot(same, all_sums, precision=lax.Precision.HIGHEST)
    near_counts = jnp.sum(same, 1, keepdims=True) * float(UPSCALE * UPSCALE)
    pooled = jnp.dot(
        near_sums / jnp.maximum(near_counts, 1.0),
        instance_weight,
        precision=lax.Precision.HIGHEST,
    ).reshape(block_rows + 2, block_cols + 2, local_width)

    both = jnp.stack([enhancer_input, output_cotangent])
    both = halo_2(both, "rows", 1, 2)
    both = halo_2(both, "cols", 2, 2)
    input_padded, cotangent_padded = both[0], both[1]

    whole_in = gathered.transpose(0, 2, 3, 1, 4).reshape(coarse_rows, band_cols, -1)
    rimmed = jnp.pad(whole_in, ((1, 1), (1, 1), (0, 0)))
    first_raw = conv_taps(rimmed, global_first, coarse_rows, band_cols)
    band_total = coarse_rows * band_cols
    band_mean = jnp.sum(first_raw, 0) / band_total
    band_var = jnp.sum(first_raw * first_raw, 0) / band_total - band_mean * band_mean
    normed = (first_raw - band_mean) * lax.rsqrt(band_var + norm_eps)
    hidden = (
        jnp.maximum(normed, 0.0).astype(jnp.bfloat16).reshape(coarse_rows, band_cols, width_share)
    )
    hidden = jnp.pad(hidden, ((2, 2), (0, 0), (0, 0)))
    near_hidden = lax.dynamic_slice_in_dim(hidden, my_row * band_rows, band_rows + 4, 0)
    near_hidden = lax.all_gather(near_hidden, "cols", axis=2, tiled=True)
    second_raw = conv_taps(
        jnp.pad(near_hidden, ((0, 0), (1, 1), (0, 0))), global_second, band_rows + 2, band_cols
    )
    mine = lax.dynamic_index_in_dim(gathered, my_col, 1, keepdims=False)
    mine = jnp.pad(
        mine.reshape(coarse_rows, band_cols, width_share), ((1, 1), (0, 0), (0, 0))
    )
    near_in = lax.dynamic_slice_in_dim(mine, my_row * band_rows, band_rows + 2, 0)
    global_out = (
        near_in.astype(jnp.float32).reshape(-1, width_share) + second_raw
    ).astype(jnp.bfloat16)
    weight_rows = lax.dynamic_slice_in_dim(project_weight, my_col * width_share, width_share, 0)
    partial = jnp.dot(global_out, weight_rows, preferred_element_type=jnp.float32)
    partial = jnp.pad(
        partial.reshape(band_rows + 2, band_cols, local_width), ((0, 0), (1, 1), (0, 0))
    )
    outgoing = jnp.stack(
        [partial[:, j * block_cols : (j + 1) * block_cols + 2] for j in range(col_devices)]
    )
    incoming = lax.all_to_all(outgoing, "cols", 0, 0)
    coarse = jnp.sum(incoming, 0).astype(jnp.bfloat16)

    block_terms = coarse.astype(jnp.float32) + pooled
    upsampled = jnp.repeat(jnp.repeat(block_terms, UPSCALE, 0), UPSCALE, 1)
    cut = UPSCALE - 2
    upsampled = upsampled[cut:-cut, cut:-cut]
    row_ids = my_row * tile_rows - 2 + jnp.arange(tile_rows + 4)
    col_ids = my_col * tile_cols - 2 + jnp.arange(tile_cols + 4)
    inside = (
        ((row_ids >= 0) & (row_ids < tile_rows * row_devices))[:, None]
        & ((col_ids >= 0) & (col_ids < tile_cols * col_devices))[None, :]
    )[:, :, None]
    mixed = jnp.where(inside, input_padded.astype(jnp.float32) + upsampled, 0.0).astype(
        jnp.bfloat16
    )
    near_rows, near_cols = tile_rows + 2, tile_cols + 2
    inside = inside[1:-1, 1:-1]
    first_act = conv_taps(mixed, enhancer_first, near_rows, near_cols).reshape(
        near_rows, near_cols, local_width
    )
    pixel_total = tile_rows * tile_cols * devices
    own_act = first_act[1:-1, 1:-1]
    act_sums = jnp.stack([jnp.sum(own_act, (0, 1)), jnp.sum(own_act * own_act, (0, 1))])
    act_sums = jnp.sum(lax.all_gather(act_sums, BOTH, axis=0), 0)
    act_mean = act_sums[0] / pixel_total
    inverse_dev = lax.rsqrt(act_sums[1] / pixel_total - act_mean * act_mean + norm_eps)
    normed_act = (first_act - act_mean) * inverse_dev
    activated = jnp.where(inside, jax.nn.silu(normed_act), 0.0).astype(jnp.bfloat16)
    second_act = conv_taps(activated, enhancer_second, tile_rows, tile_cols)
    own_mixed = mixed[2:-2, 2:-2]
    enhanced = (
        (own_mixed.astype(jnp.float32).reshape(-1, local_width) + second_act)
        .astype(jnp.bfloat16)
        .reshape(tile_rows, tile_cols, local_width)
    )
    second_local = weight_taps(activated, output_cotangent, tile_rows, tile_cols)
    act_grad = back_taps(cotangent_padded, enhancer_second, near_rows, near_cols).reshape(
        near_rows, near_cols, local_width
    )
    gate_value = jax.nn.sigmoid(normed_act)
    normed_grad = act_grad * gate_value * (1.0 + normed_act * (1.0 - gate_value))
    own_grad = normed_grad[1:-1, 1:-1]
    grad_sums = jnp.stack(
        [jnp.sum(own_grad, (0, 1)), jnp.sum(own_grad * normed_act[1:-1, 1:-1], (0, 1))]
    )
    grad_sums = jnp.sum(
        lax.all_to_all(
            jnp.broadcast_to(grad_sums, (devices, 2, local_width)), BOTH, 0, 0
        ),
        0,
    )
    first_grad = jnp.where(
        inside,
        inverse_dev
        * (normed_grad - grad_sums[0] / pixel_total - normed_act * (grad_sums[1] / pixel_total)),
        0.0,
    ).astype(jnp.bfloat16)
    first_local = weight_taps(mixed[1:-1, 1:-1], first_grad[1:-1, 1:-1], tile_rows, tile_cols)
    windows = []
    for tap_row in range(3):
        for tap_col in range(3):
            window = first_grad[
                2 - tap_row : 2 - tap_row + tile_rows, 2 - tap_col : 2 - tap_col + tile_cols
            ].astype(jnp.float32)
            windows.append(
                window.reshape(block_rows, UPSCALE, block_cols, UPSCALE, local_width)
                .sum(axis=(1, 3))
                .reshape(blocks, local_width)
            )
    cot_blocks = (
        output_cotangent.astype(jnp.float32)
        .reshape(block_rows, UPSCALE, block_cols, UPSCALE, local_width)
        .sum(axis=(1, 3))
    )
    turned = jnp.swapaxes(enhancer_first, 2, 3).reshape(-1, local_width)
    spread = jnp.dot(
        jnp.concatenate(windows, 1), turned.astype(jnp.float32), precision=lax.Precision.HIGHEST
    )
    global_gradient = (
        cot_blocks + spread.reshape(block_rows, block_cols, local_width)
    ) / UPSCALE

    rescale = 1.0 / math.sqrt(pixel_total)
    locals_both = jnp.concatenate([first_local, second_local]).astype(jnp.bfloat16)
    share = locals_both.shape[0] // devices
    received = lax.all_to_all(
        locals_both.reshape(devices, share, local_width), BOTH, 0, 0
    )
    summed = jnp.sum(received.astype(jnp.float32), 0) * rescale
    totals = lax.all_gather(summed.astype(jnp.bfloat16), BOTH, axis=0, tiled=True).astype(
        jnp.float32
    )
    totals = totals.reshape(2, 3, 3, local_width, local_width)
    return (enhanced, totals[0], totals[1], global_gradient)


def solution(mesh):
    return jax.shard_map(
        per_device,
        mesh=mesh,
        in_specs=(
            P("rows", None, "cols"),
            P(None, None, None, "cols"),
            P(None, None, None, "cols"),
            P(),
            P("rows", "cols", None),
            P("rows", "cols"),
            P(None, "rows", "cols"),
            P(),
            P(),
            P(),
            P("rows", "cols", None),
        ),
        out_specs=(P("rows", "cols", None), P(), P(), P("rows", "cols", None)),
        check_vma=False,
    )
```

```python
import math

import jax
import jax.numpy as jnp
from jax import lax
from jax.sharding import PartitionSpec as P

INSTANCES = 256
UPSCALE = 16
BOTH = ("rows", "cols")

norm_eps = 1e-05


def spread_to(array, axis):
    devices = lax.axis_size(axis)
    return lax.all_to_all(jnp.broadcast_to(array, (devices, *array.shape)), axis, 0, 0)


def halo_2(array, axis, dim, width):
    devices, length = (lax.axis_size(axis), array.shape[dim])
    up = [(i, i + 1) for i in range(devices - 1)]
    down = [(j, i) for i, j in up]
    last = lax.slice_in_dim(array, length - width, length, axis=dim)
    initial = lax.slice_in_dim(array, 0, width, axis=dim)
    before = lax.ppermute(last, axis, up)
    after = lax.ppermute(initial, axis, down)
    return jnp.concatenate([before, array, after], axis=dim)


def conv_taps(padded, weight, row_count, col_count):
    summed = jnp.zeros((row_count * col_count, weight.shape[3]), jnp.float32)
    for tap_row in range(3):
        for tap_col in range(3):
            window = padded[tap_row : tap_row + row_count, tap_col : tap_col + col_count]
            summed = summed + jnp.dot(
                window.reshape(row_count * col_count, window.shape[2]),
                weight[tap_row, tap_col],
                preferred_element_type=jnp.float32,
            )
    return summed


def back_taps(padded, weight, row_count, col_count):
    summed = jnp.zeros((row_count * col_count, weight.shape[2]), jnp.float32)
    for tap_row in range(3):
        for tap_col in range(3):
            window = padded[
                2 - tap_row : 2 - tap_row + row_count, 2 - tap_col : 2 - tap_col + col_count
            ]
            summed = summed + jnp.dot(
                window.reshape(row_count * col_count, window.shape[2]),
                weight[tap_row, tap_col].T,
                preferred_element_type=jnp.float32,
            )
    return summed


def weight_taps(padded, gradient, row_count, col_count):
    flattened = gradient.reshape(row_count * col_count, gradient.shape[2])
    stacked = []
    for tap_row in range(3):
        for tap_col in range(3):
            window = padded[tap_row : tap_row + row_count, tap_col : tap_col + col_count]
            stacked.append(
                lax.dot_general(
                    window.reshape(row_count * col_count, window.shape[2]),
                    flattened,
                    (((0,), (0,)), ((), ())),
                    preferred_element_type=jnp.float32,
                )
            )
    return jnp.concatenate(stacked)


def pieces(array):
    high = array.astype(jnp.bfloat16)
    rest = array - high.astype(jnp.float32)
    middle = rest.astype(jnp.bfloat16)
    return high, middle, (rest - middle.astype(jnp.float32)).astype(jnp.bfloat16)


def per_device(
    global_in,
    global_first,
    global_second,
    project_weight,
    enhancer_input,
    instance_map,
    encoder_features,
    instance_weight,
    enhancer_first,
    enhancer_second,
    output_cotangent,
):
    row_devices, col_devices = lax.axis_size("rows"), lax.axis_size("cols")
    devices = row_devices * col_devices
    my_row, my_col = lax.axis_index("rows"), lax.axis_index("cols")
    band_rows, band_cols, width_share = global_in.shape
    tile_rows, tile_cols, local_width = enhancer_input.shape
    coarse_rows = band_rows * row_devices
    block_rows = tile_rows // UPSCALE
    block_cols = tile_cols // UPSCALE
    blocks = block_rows * block_cols
    encoder_width = encoder_features.shape[0]

    block_labels = instance_map[::UPSCALE, ::UPSCALE].reshape(-1)
    block_sums = (
        encoder_features.reshape(encoder_width, block_rows, UPSCALE, block_cols, UPSCALE)
        .sum(axis=(2, 4))
        .reshape(-1)
    )
    extra = jnp.concatenate([*pieces(block_sums), block_labels.astype(jnp.bfloat16)])
    extra_rows = -(-extra.shape[0] // 2048) * 16
    extra = jnp.pad(extra, (0, extra_rows * 128 - extra.shape[0])).reshape(extra_rows, 128)
    packed = jnp.concatenate([global_in.reshape(-1, 128), extra])
    everything = spread_to(packed, BOTH)
    main_rows = packed.shape[0] - extra_rows
    gathered = everything[:, :main_rows].reshape(
        row_devices, col_devices, band_rows, band_cols, width_share
    )
    tail = everything[:, main_rows:].reshape(devices, -1)
    sums = blocks * encoder_width
    all_sums = sum(tail[:, k * sums : (k + 1) * sums].astype(jnp.float32) for k in (2, 1, 0))
    all_sums = (
        all_sums.reshape(row_devices, col_devices, encoder_width, block_rows, block_cols)
        .transpose(0, 3, 1, 4, 2)
        .reshape(-1, encoder_width)
    )
    all_labels = (
        tail[:, 3 * sums : 3 * sums + blocks]
        .reshape(row_devices, col_devices, block_rows, block_cols)
        .transpose(0, 2, 1, 3)
    )
    label_map = jnp.pad(
        all_labels.reshape(coarse_rows, band_cols), 1, constant_values=-1.0
    )
    near_labels = lax.dynamic_slice(
        label_map,
        (my_row * block_rows, my_col * block_cols),
        (block_rows + 2, block_cols + 2),
    ).reshape(-1)
    same = (near_labels[:, None] == all_labels.reshape(-1)[None, :]).astype(jnp.float32)
    near_sums = jnp.dot(same, all_sums, precision=lax.Precision.HIGHEST)
    near_counts = jnp.sum(same, 1, keepdims=True) * float(UPSCALE * UPSCALE)
    pooled = jnp.dot(
        near_sums / jnp.maximum(near_counts, 1.0),
        instance_weight,
        precision=lax.Precision.HIGHEST,
    ).reshape(block_rows + 2, block_cols + 2, local_width)

    both = jnp.stack([enhancer_input, output_cotangent])
    both = halo_2(both, "rows", 1, 2)
    both = halo_2(both, "cols", 2, 2)
    input_padded, cotangent_padded = both[0], both[1]

    whole_in = gathered.transpose(0, 2, 3, 1, 4).reshape(coarse_rows, band_cols, -1)
    rimmed = jnp.pad(whole_in, ((1, 1), (1, 1), (0, 0)))
    first_raw = conv_taps(rimmed, global_first, coarse_rows, band_cols)
    band_total = coarse_rows * band_cols
    band_mean = jnp.sum(first_raw, 0) / band_total
    band_var = jnp.sum(first_raw * first_raw, 0) / band_total - band_mean * band_mean
    normed = (first_raw - band_mean) * lax.rsqrt(band_var + norm_eps)
    hidden = (
        jnp.maximum(normed, 0.0).astype(jnp.bfloat16).reshape(coarse_rows, band_cols, width_share)
    )
    hidden = jnp.pad(hidden, ((2, 2), (0, 0), (0, 0)))
    near_hidden = lax.dynamic_slice_in_dim(hidden, my_row * band_rows, band_rows + 4, 0)
    near_hidden = spread_to(near_hidden, "cols")
    near_hidden = near_hidden.transpose(1, 2, 0, 3).reshape(band_rows + 4, band_cols, -1)
    second_raw = conv_taps(
        jnp.pad(near_hidden, ((0, 0), (1, 1), (0, 0))), global_second, band_rows + 2, band_cols
    )
    mine = lax.dynamic_index_in_dim(gathered, my_col, 1, keepdims=False)
    mine = jnp.pad(
        mine.reshape(coarse_rows, band_cols, width_share), ((1, 1), (0, 0), (0, 0))
    )
    near_in = lax.dynamic_slice_in_dim(mine, my_row * band_rows, band_rows + 2, 0)
    global_out = (
        near_in.astype(jnp.float32).reshape(-1, width_share) + second_raw
    ).astype(jnp.bfloat16)
    weight_rows = lax.dynamic_slice_in_dim(project_weight, my_col * width_share, width_share, 0)
    partial = jnp.dot(global_out, weight_rows, preferred_element_type=jnp.float32)
    partial = jnp.pad(
        partial.reshape(band_rows + 2, band_cols, local_width), ((0, 0), (1, 1), (0, 0))
    )
    outgoing = jnp.stack(
        [partial[:, j * block_cols : (j + 1) * block_cols + 2] for j in range(col_devices)]
    )
    incoming = lax.all_to_all(outgoing, "cols", 0, 0)
    coarse = jnp.sum(incoming, 0).astype(jnp.bfloat16)

    block_terms = coarse.astype(jnp.float32) + pooled
    upsampled = jnp.repeat(jnp.repeat(block_terms, UPSCALE, 0), UPSCALE, 1)
    cut = UPSCALE - 2
    upsampled = upsampled[cut:-cut, cut:-cut]
    row_ids = my_row * tile_rows - 2 + jnp.arange(tile_rows + 4)
    col_ids = my_col * tile_cols - 2 + jnp.arange(tile_cols + 4)
    inside = (
        ((row_ids >= 0) & (row_ids < tile_rows * row_devices))[:, None]
        & ((col_ids >= 0) & (col_ids < tile_cols * col_devices))[None, :]
    )[:, :, None]
    mixed = jnp.where(inside, input_padded.astype(jnp.float32) + upsampled, 0.0).astype(
        jnp.bfloat16
    )
    near_rows, near_cols = tile_rows + 2, tile_cols + 2
    inside = inside[1:-1, 1:-1]
    first_act = conv_taps(mixed, enhancer_first, near_rows, near_cols).reshape(
        near_rows, near_cols, local_width
    )
    pixel_total = tile_rows * tile_cols * devices
    own_act = first_act[1:-1, 1:-1]
    act_sums = jnp.stack([jnp.sum(own_act, (0, 1)), jnp.sum(own_act * own_act, (0, 1))])
    act_sums = jnp.sum(spread_to(act_sums, BOTH), 0)
    act_mean = act_sums[0] / pixel_total
    inverse_dev = lax.rsqrt(act_sums[1] / pixel_total - act_mean * act_mean + norm_eps)
    normed_act = (first_act - act_mean) * inverse_dev
    activated = jnp.where(inside, jax.nn.silu(normed_act), 0.0).astype(jnp.bfloat16)
    second_act = conv_taps(activated, enhancer_second, tile_rows, tile_cols)
    own_mixed = mixed[2:-2, 2:-2]
    enhanced = (
        (own_mixed.astype(jnp.float32).reshape(-1, local_width) + second_act)
        .astype(jnp.bfloat16)
        .reshape(tile_rows, tile_cols, local_width)
    )
    second_local = weight_taps(activated, output_cotangent, tile_rows, tile_cols)
    act_grad = back_taps(cotangent_padded, enhancer_second, near_rows, near_cols).reshape(
        near_rows, near_cols, local_width
    )
    gate_value = jax.nn.sigmoid(normed_act)
    normed_grad = act_grad * gate_value * (1.0 + normed_act * (1.0 - gate_value))
    own_grad = normed_grad[1:-1, 1:-1]
    grad_sums = jnp.stack(
        [jnp.sum(own_grad, (0, 1)), jnp.sum(own_grad * normed_act[1:-1, 1:-1], (0, 1))]
    )
    grad_sums = jnp.sum(spread_to(grad_sums, BOTH), 0)
    first_grad = jnp.where(
        inside,
        inverse_dev
        * (normed_grad - grad_sums[0] / pixel_total - normed_act * (grad_sums[1] / pixel_total)),
        0.0,
    ).astype(jnp.bfloat16)
    first_local = weight_taps(mixed[1:-1, 1:-1], first_grad[1:-1, 1:-1], tile_rows, tile_cols)
    windows = []
    for tap_row in range(3):
        for tap_col in range(3):
            window = first_grad[
                2 - tap_row : 2 - tap_row + tile_rows, 2 - tap_col : 2 - tap_col + tile_cols
            ].astype(jnp.float32)
            windows.append(
                window.reshape(block_rows, UPSCALE, block_cols, UPSCALE, local_width)
                .sum(axis=(1, 3))
                .reshape(blocks, local_width)
            )
    cot_blocks = (
        output_cotangent.astype(jnp.float32)
        .reshape(block_rows, UPSCALE, block_cols, UPSCALE, local_width)
        .sum(axis=(1, 3))
    )
    turned = jnp.swapaxes(enhancer_first, 2, 3).reshape(-1, local_width)
    spread = jnp.dot(
        jnp.concatenate(windows, 1), turned.astype(jnp.float32), precision=lax.Precision.HIGHEST
    )
    global_gradient = (
        cot_blocks + spread.reshape(block_rows, block_cols, local_width)
    ) / UPSCALE

    rescale = 1.0 / math.sqrt(pixel_total)
    locals_both = jnp.concatenate([first_local, second_local]).astype(jnp.bfloat16)
    share = locals_both.shape[0] // devices
    received = lax.all_to_all(
        locals_both.reshape(devices, share, local_width), BOTH, 0, 0
    )
    summed = jnp.sum(received.astype(jnp.float32), 0) * rescale
    totals = spread_to(summed.astype(jnp.bfloat16), BOTH).astype(jnp.float32)
    totals = totals.reshape(2, 3, 3, local_width, local_width)
    return (enhanced, totals[0], totals[1], global_gradient)


def solution(mesh):
    return jax.shard_map(
        per_device,
        mesh=mesh,
        in_specs=(
            P("rows", None, "cols"),
            P(None, None, None, "cols"),
            P(None, None, None, "cols"),
            P(),
            P("rows", "cols", None),
            P("rows", "cols"),
            P(None, "rows", "cols"),
            P(),
            P(),
            P(),
            P("rows", "cols", None),
        ),
        out_specs=(P("rows", "cols", None), P(), P(), P("rows", "cols", None)),
        check_vma=False,
    )
```

```python
import functools
import math

import jax
import jax.numpy as jnp
import numpy as np
from jax import lax
from jax.experimental import pallas as pl
from jax.experimental.pallas import tpu as pltpu
from jax.sharding import PartitionSpec as P

INSTANCES = 256
UPSCALE = 16
BOTH = ("rows", "cols")

norm_eps = 1e-05


def spread_to(array, axis):
    devices = lax.axis_size(axis)
    return lax.all_to_all(jnp.broadcast_to(array, (devices, *array.shape)), axis, 0, 0)


def conv_taps(padded, weight, row_count, col_count):
    summed = jnp.zeros((row_count * col_count, weight.shape[3]), jnp.float32)
    for tap_row in range(3):
        for tap_col in range(3):
            window = padded[tap_row : tap_row + row_count, tap_col : tap_col + col_count]
            summed = summed + jnp.dot(
                window.reshape(row_count * col_count, window.shape[2]),
                weight[tap_row, tap_col],
                preferred_element_type=jnp.float32,
            )
    return summed


RIM = 8
MARGIN = 16
KERNEL_VMEM = 40 * 1024 * 1024


class Layout:
    def __init__(self, tile_rows, tile_cols):
        self.rows, self.cols = tile_rows, tile_cols
        self.wide = tile_cols + 2 * RIM
        self.flat = (tile_rows + 6) * self.wide + 2 * MARGIN
        self.out_rows = tile_rows + 3
        self.out = self.out_rows * self.wide
        self.z = self.out + 2 * MARGIN
        self.own = tile_rows * self.wide + 2 * MARGIN
        self.kept = -(-self.out // 128) * 128


def vmem(count):
    return [pl.BlockSpec(memory_space=pltpu.VMEM)] * count


def call(body, outs, ins, scratch=(), flops=0, **fixed):
    return pl.pallas_call(
        functools.partial(body, **fixed),
        out_shape=outs,
        in_specs=vmem(len(ins)),
        out_specs=jax.tree.map(lambda _: pl.BlockSpec(memory_space=pltpu.VMEM), outs),
        scratch_shapes=list(scratch),
        compiler_params=pltpu.CompilerParams(vmem_limit_bytes=KERNEL_VMEM),
        cost_estimate=pl.CostEstimate(flops=flops, bytes_accessed=4 << 20, transcendentals=0),
    )(*ins)


def put_tiles(flat_ref, lay, main_ref, top_ref, bottom_ref, strip_ref):
    flat_ref[...] = jnp.zeros_like(flat_ref)
    for k in range(lay.rows + 5):
        base = MARGIN + k * lay.wide
        i = k - 3
        if i >= -2:
            if i < 0:
                row = top_ref[i + 2]
            elif i < lay.rows:
                row = main_ref[i]
            else:
                row = bottom_ref[i - lay.rows]
            flat_ref[base : base + lay.cols] = row
        flat_ref[base + lay.cols : base + lay.wide] = strip_ref[k]


def taps_matmul(flat_ref, square_ref, z_refs, lay, turned):
    count = z_refs[0].shape[0]
    chunks = 3
    step = count // chunks
    width = z_refs[0].shape[1]

    @pl.loop(0, chunks)
    def _(c):
        begin = pl.multiple_of(c * step, 16)
        parts = [flat_ref[pl.ds(begin + shift, step)] for shift in (0, lay.wide, 2 * lay.wide)]
        if turned:
            left = jnp.concatenate(parts[::-1], 1)
            result = lax.dot_general(
                left, square_ref[...], (((1,), (1,)), ((), ())), preferred_element_type=jnp.float32
            )
        else:
            left = jnp.concatenate(parts, 1)
            result = jnp.dot(left, square_ref[...], preferred_element_type=jnp.float32)
        for b in range(3):
            z_refs[b][pl.ds(begin, step)] = result[:, b * width : (b + 1) * width]


def put_square(square_ref, weight_ref, turned):
    width = weight_ref.shape[2]
    for a in range(3):
        for b in range(3):
            r, c = (b, a) if turned else (a, b)
            square_ref[r * width : (r + 1) * width, c * width : (c + 1) * width] = weight_ref[a, b]


def taken(z_refs, begin, count, turned):
    early, late = (2, 0) if turned else (0, 2)
    return (
        z_refs[early][pl.ds(begin + MARGIN - 1, count)]
        + z_refs[1][pl.ds(begin + MARGIN, count)]
        + z_refs[late][pl.ds(begin + MARGIN + 1, count)]
    )


def folded(value):
    return value.reshape(-1, 8, value.shape[-1]).sum(0)


def send_stats(out_ref, first, second):
    sums = jnp.concatenate(
        [jnp.sum(first, 0, keepdims=True), jnp.sum(second, 0, keepdims=True)], 0
    )
    out_ref[...] = jnp.zeros_like(out_ref)
    for d in range(out_ref.shape[0]):
        out_ref[d, 0:2] = sums


def cot_kernel(main, top, bottom, strip, weight, grad_out, flat, square, z0, z1, z2, *, lay):
    put_tiles(flat, lay, main, top, bottom, strip)
    put_square(square, weight, True)
    taps_matmul(flat, square, (z0, z1, z2), lay, True)

    @pl.loop(0, lay.out_rows)
    def _(r):
        begin = pl.multiple_of(r * lay.wide, 16)
        grad_out[pl.ds(begin, lay.wide)] = taken((z0, z1, z2), begin, lay.wide, True)


def mixed_kernel(
    main, top, bottom, strip, terms, weight, flat, act_out, stats, square, z0, z1, z2, *, lay
):
    width = main.shape[2]
    flat[...] = jnp.zeros_like(flat)
    blocks = lay.cols // UPSCALE
    for k in range(lay.rows + 5):
        base = MARGIN + k * lay.wide
        i = k - 3
        own, following = (i + UPSCALE) // UPSCALE, (i + 1 + UPSCALE) // UPSCALE

        def spread(block_row, block_col, rows):
            return jnp.broadcast_to(
                terms[block_row, block_col : block_col + 1], (rows, width)
            )

        if i >= -2:
            if i < 0:
                row = top[i + 2]
            elif i < lay.rows:
                row = main[i]
            else:
                row = bottom[i - lay.rows]
            added = jnp.concatenate([spread(own, b + 2, UPSCALE) for b in range(blocks)], 0)
            flat[base : base + lay.cols] = (row.astype(jnp.float32) + added).astype(jnp.bfloat16)
        zero = jnp.zeros((RIM, width), jnp.float32)
        right = spread(own, blocks + 2, RIM) if i >= -2 else zero
        left = spread(following, 1, RIM) if i + 1 < lay.rows + 2 else zero
        flat[base + lay.cols : base + lay.wide] = (
            strip[k].astype(jnp.float32) + jnp.concatenate([right, left], 0)
        ).astype(jnp.bfloat16)
    put_square(square, weight, False)
    taps_matmul(flat, square, (z0, z1, z2), lay, False)

    def step(r, sums):
        begin = pl.multiple_of(r * lay.wide, 16)
        value = taken((z0, z1, z2), begin, lay.wide, False)
        act_out[pl.ds(begin, lay.wide)] = value
        mine = ((r >= 2) & (r < lay.rows + 2)).astype(jnp.float32)
        own_value = value[: lay.cols] * mine
        return sums[0] + folded(own_value), sums[1] + folded(own_value * own_value)

    zero = jnp.zeros((8, width), jnp.float32)
    sums = lax.fori_loop(0, lay.out_rows, step, (zero, zero))
    send_stats(stats, *sums)


def act_moments(stats, pixel_total):
    sums = jnp.sum(stats[...], 0)
    mean = sums[0:1] / pixel_total
    return mean, lax.rsqrt(sums[1:2] / pixel_total - mean * mean + norm_eps)


def inside_masks(lay, width, row_devices, col_devices):
    my_row, my_col = lax.axis_index("rows"), lax.axis_index("cols")
    column = lax.broadcasted_iota(jnp.int32, (lay.wide, width), 0)
    has_right = (my_col < col_devices - 1).astype(jnp.float32)
    has_left = (my_col > 0).astype(jnp.float32)
    near = jnp.where(
        column < lay.cols, 1.0, jnp.where(column < lay.cols + RIM, has_right, 0.0)
    )
    following = jnp.where(column >= lay.cols + RIM, has_left, 0.0)

    def row_inside(i):
        row = my_row * lay.rows + i
        return ((row >= 0) & (row < lay.rows * row_devices)).astype(jnp.float32)

    return lambda r: near * row_inside(r - 2) + following * row_inside(r - 1)


def norm_kernel(
    act, stats, act_grad, activated, normed_out, grad_out, grad_stats, *, lay, grid, pixel_total
):
    width = act.shape[1]
    mean, inverse = act_moments(stats, pixel_total)
    mask = inside_masks(lay, width, *grid)
    activated[...] = jnp.zeros_like(activated)

    def step(r, sums):
        begin = pl.multiple_of(r * lay.wide, 16)
        normed = (act[pl.ds(begin, lay.wide)] - mean) * inverse
        gate = 1.0 / (1.0 + jnp.exp(-normed))
        inside = mask(r)
        activated[pl.ds(pl.multiple_of(begin + MARGIN + lay.wide, 16), lay.wide)] = (
            normed * gate * inside
        ).astype(jnp.bfloat16)
        grad = act_grad[pl.ds(begin, lay.wide)] * gate * (1.0 + normed * (1.0 - gate))
        normed_out[pl.ds(begin, lay.wide)] = normed
        grad_out[pl.ds(begin, lay.wide)] = grad
        mine = ((r >= 2) & (r < lay.rows + 2)).astype(jnp.float32)
        own_grad = grad[: lay.cols] * mine
        return sums[0] + folded(own_grad), sums[1] + folded(own_grad * normed[: lay.cols])

    zero = jnp.zeros((8, width), jnp.float32)
    sums = lax.fori_loop(0, lay.out_rows, step, (zero, zero))
    send_stats(grad_stats, *sums)


def weight_matmul(flat_ref, own_ref, total_ref, sent_ref, lay, chunk):
    count = lay.own
    first = MARGIN + 3 * lay.wide - MARGIN
    chunks = 3
    step = count // chunks
    width = own_ref.shape[1]
    total = None
    for c in range(chunks):
        begin = c * step
        left = jnp.concatenate(
            [
                flat_ref[first + begin + a * lay.wide : first + begin + a * lay.wide + step]
                for a in (-1, 0, 1)
            ],
            1,
        )
        right = jnp.concatenate(
            [
                own_ref[MARGIN + begin - b : MARGIN + begin - b + step].astype(jnp.bfloat16)
                for b in (-1, 0, 1)
            ],
            1,
        )
        part = lax.dot_general(
            left, right, (((0,), (0,)), ((), ())), preferred_element_type=jnp.float32
        )
        total = part if total is None else total + part
    for a in range(3):
        for b in range(3):
            total_ref[(a * 3 + b) * width : (a * 3 + b + 1) * width] = total[
                a * width : (a + 1) * width, b * width : (b + 1) * width
            ]
    padded = sent_ref.shape[1]
    for d in range(sent_ref.shape[0]):
        sent_ref[d] = total_ref[d * chunk : d * chunk + padded].astype(jnp.bfloat16)


def second_kernel(
    activated, mixed, main, weight, enhanced, sent, square, z0, z1, z2, own, total, *, lay, chunk
):
    put_square(square, weight, False)
    taps_matmul(activated, square, (z0, z1, z2), lay, False)

    @pl.loop(0, lay.rows)
    def _(i):
        begin = pl.multiple_of((i + 2) * lay.wide, 16)
        value = taken((z0, z1, z2), begin, lay.cols, False)
        place = pl.multiple_of((i + 3) * lay.wide + MARGIN, 16)
        enhanced[i] = (mixed[pl.ds(place, lay.cols)].astype(jnp.float32) + value).astype(
            jnp.bfloat16
        )

    own[...] = jnp.zeros_like(own)

    @pl.loop(0, lay.rows)
    def _(i):
        place = pl.multiple_of(i * lay.wide + 2 * MARGIN, 16)
        own[pl.ds(place, lay.cols)] = main[i].astype(jnp.float32)

    weight_matmul(activated, own, total, sent, lay, chunk)


def first_kernel(
    stats, grad_stats, normed_ref, grad_ref, mixed, sent, kept, own, total, *, lay, grid, chunk,
    pixel_total
):
    width = normed_ref.shape[1]
    _, inverse = act_moments(stats, pixel_total)
    sums = jnp.sum(grad_stats[...], 0)
    grad_mean, cross_mean = sums[0:1] / pixel_total, sums[1:2] / pixel_total
    mask = inside_masks(lay, width, *grid)
    own[...] = jnp.zeros_like(own)
    kept[...] = jnp.zeros_like(kept)

    @pl.loop(0, lay.out_rows)
    def _(r):
        begin = pl.multiple_of(r * lay.wide, 16)
        value = inverse * (
            grad_ref[pl.ds(begin, lay.wide)]
            - grad_mean
            - normed_ref[pl.ds(begin, lay.wide)] * cross_mean
        )
        value = (value * mask(r)).astype(jnp.bfloat16)
        kept[pl.ds(begin, lay.wide)] = value

        @pl.when((r >= 2) & (r < lay.rows + 2))
        def _():
            place = pl.multiple_of((r - 2) * lay.wide + 2 * MARGIN, 16)
            own[pl.ds(place, lay.cols)] = value[: lay.cols].astype(jnp.float32)

    weight_matmul(mixed, own, total, sent, lay, chunk)


def coarse_kernel(kept, picked, main, weight, out, *, lay):
    width = weight.shape[2]
    windows = jnp.dot(picked[...], kept[...], preferred_element_type=jnp.float32)
    block_rows, block_cols = lay.rows // UPSCALE, lay.cols // UPSCALE
    blocks = block_rows * block_cols
    summed = jnp.zeros((blocks, width), jnp.float32)
    for tap in range(9):
        summed = summed + lax.dot_general(
            windows[tap * blocks : (tap + 1) * blocks],
            weight[tap // 3, tap % 3].astype(jnp.float32),
            (((1,), (1,)), ((), ())),
            precision=lax.Precision.HIGHEST,
            preferred_element_type=jnp.float32,
        )
    for bi in range(block_rows):
        rows = jnp.zeros((lay.cols, width), jnp.float32)
        for i in range(UPSCALE):
            rows = rows + main[bi * UPSCALE + i].astype(jnp.float32)
        for bj in range(block_cols):
            k = bi * block_cols + bj
            cot = jnp.sum(rows[bj * UPSCALE : (bj + 1) * UPSCALE], 0, keepdims=True)
            out[k : k + 1] = (cot + summed[k : k + 1]) / UPSCALE


def share_kernel(received, sent, *, rescale):
    total = received[0].astype(jnp.float32)
    for d in range(1, received.shape[0]):
        total = total + received[d].astype(jnp.float32)
    total = (total * rescale).astype(jnp.bfloat16)
    for d in range(sent.shape[0]):
        sent[d] = total


def join_kernel(received, out, *, chunk):
    for d in range(received.shape[0]):
        out[d * chunk : (d + 1) * chunk] = received[d].astype(jnp.float32)[:chunk]


def window_picks(lay):
    place = np.arange(lay.kept)
    slot, column = place // lay.wide + 1, place % lay.wide
    behind = column >= lay.cols + RIM
    i = np.where(behind, slot - 2, slot - 3)
    j = np.where(behind, column - lay.wide, column)
    rows = []
    for a in range(3):
        for b in range(3):
            y, x = i + a - 1, j + b - 1
            for bi in range(lay.rows // UPSCALE):
                for bj in range(lay.cols // UPSCALE):
                    rows.append((y // UPSCALE == bi) & (x // UPSCALE == bj) & (place < lay.out))
    return jnp.asarray(np.stack(rows), jnp.bfloat16)


def to_all(payload, axis):
    return lax.all_to_all(payload, axis, 0, 0)


def pieces(array):
    high = array.astype(jnp.bfloat16)
    rest = array - high.astype(jnp.float32)
    middle = rest.astype(jnp.bfloat16)
    return high, middle, (rest - middle.astype(jnp.float32)).astype(jnp.bfloat16)


def per_device(
    global_in,
    global_first,
    global_second,
    project_weight,
    enhancer_input,
    instance_map,
    encoder_features,
    instance_weight,
    enhancer_first,
    enhancer_second,
    output_cotangent,
):
    row_devices, col_devices = lax.axis_size("rows"), lax.axis_size("cols")
    devices = row_devices * col_devices
    my_row, my_col = lax.axis_index("rows"), lax.axis_index("cols")
    band_rows, band_cols, width_share = global_in.shape
    tile_rows, tile_cols, local_width = enhancer_input.shape
    coarse_rows = band_rows * row_devices
    block_rows = tile_rows // UPSCALE
    block_cols = tile_cols // UPSCALE
    blocks = block_rows * block_cols
    encoder_width = encoder_features.shape[0]

    block_labels = instance_map[::UPSCALE, ::UPSCALE].reshape(-1)
    block_sums = (
        encoder_features.reshape(encoder_width, block_rows, UPSCALE, block_cols, UPSCALE)
        .sum(axis=(2, 4))
        .reshape(-1)
    )
    extra = jnp.concatenate([*pieces(block_sums), block_labels.astype(jnp.bfloat16)])
    extra_rows = -(-extra.shape[0] // 2048) * 16
    extra = jnp.pad(extra, (0, extra_rows * 128 - extra.shape[0])).reshape(extra_rows, 128)
    packed = jnp.concatenate([global_in.reshape(-1, 128), extra])
    everything = spread_to(packed, BOTH)
    main_rows = packed.shape[0] - extra_rows
    gathered = everything[:, :main_rows].reshape(
        row_devices, col_devices, band_rows, band_cols, width_share
    )
    tail = everything[:, main_rows:].reshape(devices, -1)
    sums = blocks * encoder_width
    all_sums = sum(tail[:, k * sums : (k + 1) * sums].astype(jnp.float32) for k in (2, 1, 0))
    all_sums = (
        all_sums.reshape(row_devices, col_devices, encoder_width, block_rows, block_cols)
        .transpose(0, 3, 1, 4, 2)
        .reshape(-1, encoder_width)
    )
    all_labels = (
        tail[:, 3 * sums : 3 * sums + blocks]
        .reshape(row_devices, col_devices, block_rows, block_cols)
        .transpose(0, 2, 1, 3)
    )
    label_map = jnp.pad(
        all_labels.reshape(coarse_rows, band_cols), 1, constant_values=-1.0
    )
    near_labels = lax.dynamic_slice(
        label_map,
        (my_row * block_rows, my_col * block_cols),
        (block_rows + 2, block_cols + 2),
    ).reshape(-1)
    same = (near_labels[:, None] == all_labels.reshape(-1)[None, :]).astype(jnp.float32)
    near_sums = jnp.dot(same, all_sums, precision=lax.Precision.HIGHEST)
    near_counts = jnp.sum(same, 1, keepdims=True) * float(UPSCALE * UPSCALE)
    pooled = jnp.dot(
        near_sums / jnp.maximum(near_counts, 1.0),
        instance_weight,
        precision=lax.Precision.HIGHEST,
    ).reshape(block_rows + 2, block_cols + 2, local_width)

    row_up = [(i, i + 1) for i in range(row_devices - 1)]
    row_down = [(j, i) for i, j in row_up]
    col_up = [(i, i + 1) for i in range(col_devices - 1)]
    col_down = [(j, i) for i, j in col_up]
    top = lax.ppermute(
        jnp.stack([enhancer_input[-2:], output_cotangent[-2:]]), "rows", row_up
    )
    bottom = lax.ppermute(
        jnp.stack([enhancer_input[:2], output_cotangent[:2]]), "rows", row_down
    )
    both = jnp.stack([enhancer_input, output_cotangent])
    tall_last = jnp.concatenate([top[:, :, -RIM:], both[:, :, -RIM:], bottom[:, :, -RIM:]], 1)
    tall_first = jnp.concatenate([top[:, :, :RIM], both[:, :, :RIM], bottom[:, :, :RIM]], 1)
    left = lax.ppermute(tall_last, "cols", col_up)
    right = lax.ppermute(tall_first, "cols", col_down)
    strip = jnp.concatenate(
        [
            jnp.pad(right, ((0, 0), (1, 0), (0, 0), (0, 0))),
            jnp.pad(left, ((0, 0), (0, 1), (0, 0), (0, 0))),
        ],
        2,
    )
    lay = Layout(tile_rows, tile_cols)
    width = local_width
    grid = (row_devices, col_devices)
    pixel_total = float(tile_rows * tile_cols * devices)
    chunk = 9 * width // devices
    padded_chunk = -(-chunk // 8) * 8
    square = pltpu.VMEM((3 * width, 3 * width), jnp.bfloat16)
    z = [pltpu.VMEM((lay.z, width), jnp.float32)] * 3
    own = pltpu.VMEM((lay.own + 2 * MARGIN, width), jnp.float32)
    total = pltpu.VMEM((9 * width + 64, width), jnp.float32)
    flat_shape = jax.ShapeDtypeStruct((lay.flat, width), jnp.bfloat16)
    out_shape = jax.ShapeDtypeStruct((lay.out, width), jnp.float32)
    stats_shape = jax.ShapeDtypeStruct((devices, 8, width), jnp.float32)
    sent_shape = jax.ShapeDtypeStruct((devices, padded_chunk, width), jnp.bfloat16)
    conv_flops = 18 * width * width * lay.out

    act_grad = call(
        cot_kernel,
        out_shape,
        (output_cotangent, top[1], bottom[1], strip[1], enhancer_second),
        [pltpu.VMEM((lay.flat, width), jnp.bfloat16), square, *z],
        conv_flops,
        lay=lay,
    )

    whole_in = gathered.transpose(0, 2, 3, 1, 4).reshape(coarse_rows, band_cols, -1)
    rimmed = jnp.pad(whole_in, ((1, 1), (1, 1), (0, 0)))
    first_raw = conv_taps(rimmed, global_first, coarse_rows, band_cols)
    band_total = coarse_rows * band_cols
    band_mean = jnp.sum(first_raw, 0) / band_total
    band_var = jnp.sum(first_raw * first_raw, 0) / band_total - band_mean * band_mean
    normed = (first_raw - band_mean) * lax.rsqrt(band_var + norm_eps)
    hidden = (
        jnp.maximum(normed, 0.0).astype(jnp.bfloat16).reshape(coarse_rows, band_cols, width_share)
    )
    hidden = jnp.pad(hidden, ((2, 2), (0, 0), (0, 0)))
    near_hidden = lax.dynamic_slice_in_dim(hidden, my_row * band_rows, band_rows + 4, 0)
    near_hidden = spread_to(near_hidden, "cols")
    near_hidden = near_hidden.transpose(1, 2, 0, 3).reshape(band_rows + 4, band_cols, -1)
    second_raw = conv_taps(
        jnp.pad(near_hidden, ((0, 0), (1, 1), (0, 0))), global_second, band_rows + 2, band_cols
    )
    mine = lax.dynamic_index_in_dim(gathered, my_col, 1, keepdims=False)
    mine = jnp.pad(
        mine.reshape(coarse_rows, band_cols, width_share), ((1, 1), (0, 0), (0, 0))
    )
    near_in = lax.dynamic_slice_in_dim(mine, my_row * band_rows, band_rows + 2, 0)
    global_out = (
        near_in.astype(jnp.float32).reshape(-1, width_share) + second_raw
    ).astype(jnp.bfloat16)
    weight_rows = lax.dynamic_slice_in_dim(project_weight, my_col * width_share, width_share, 0)
    partial = jnp.dot(global_out, weight_rows, preferred_element_type=jnp.float32)
    partial = jnp.pad(
        partial.reshape(band_rows + 2, band_cols, local_width), ((0, 0), (1, 1), (0, 0))
    )
    outgoing = jnp.stack(
        [partial[:, j * block_cols : (j + 1) * block_cols + 2] for j in range(col_devices)]
    )
    incoming = lax.all_to_all(outgoing, "cols", 0, 0)
    coarse = jnp.sum(incoming, 0).astype(jnp.bfloat16)

    block_terms = coarse.astype(jnp.float32) + pooled
    row_ids = my_row * block_rows - 1 + jnp.arange(block_rows + 2)
    col_ids = my_col * block_cols - 1 + jnp.arange(block_cols + 2)
    inside = ((row_ids >= 0) & (row_ids < coarse_rows))[:, None] & (
        (col_ids >= 0) & (col_ids < band_cols)
    )[None, :]
    terms = jnp.where(inside[:, :, None], block_terms, 0.0)
    terms = jnp.pad(terms, ((0, 0), (1, 1), (0, 0)))

    mixed, first_act, stats = call(
        mixed_kernel,
        (flat_shape, out_shape, stats_shape),
        (enhancer_input, top[0], bottom[0], strip[0], terms, enhancer_first),
        [square, *z],
        conv_flops,
        lay=lay,
    )
    stats = to_all(stats, BOTH)
    activated, normed_act, normed_grad, grad_stats = call(
        norm_kernel,
        (flat_shape, out_shape, out_shape, stats_shape),
        (first_act, stats, act_grad),
        lay=lay,
        grid=grid,
        pixel_total=pixel_total,
    )
    grad_stats = to_all(grad_stats, BOTH)
    enhanced, second_sent = call(
        second_kernel,
        (jax.ShapeDtypeStruct((tile_rows, tile_cols, width), jnp.bfloat16), sent_shape),
        (activated, mixed, output_cotangent, enhancer_second),
        [square, *z, own, total],
        2 * conv_flops,
        lay=lay,
        chunk=chunk,
    )
    second_part = to_all(second_sent, BOTH)
    first_sent, kept = call(
        first_kernel,
        (sent_shape, jax.ShapeDtypeStruct((lay.kept, width), jnp.bfloat16)),
        (stats, grad_stats, normed_act, normed_grad, mixed),
        [own, total],
        conv_flops,
        lay=lay,
        grid=grid,
        chunk=chunk,
        pixel_total=pixel_total,
    )
    first_part = to_all(first_sent, BOTH)
    rescale = 1.0 / math.sqrt(pixel_total)
    second_share = to_all(call(share_kernel, sent_shape, (second_part,), rescale=rescale), BOTH)
    global_gradient = call(
        coarse_kernel,
        jax.ShapeDtypeStruct((blocks, width), jnp.float32),
        (kept, window_picks(lay), output_cotangent, enhancer_first),
        (),
        lay=lay,
    )
    first_share = to_all(call(share_kernel, sent_shape, (first_part,), rescale=rescale), BOTH)
    whole_shape = jax.ShapeDtypeStruct((9 * width, width), jnp.float32)
    second_total = call(join_kernel, whole_shape, (second_share,), chunk=chunk)
    first_total = call(join_kernel, whole_shape, (first_share,), chunk=chunk)
    return (
        enhanced,
        first_total.reshape(3, 3, width, width),
        second_total.reshape(3, 3, width, width),
        global_gradient.reshape(block_rows, block_cols, width),
    )


def solution(mesh):
    return jax.shard_map(
        per_device,
        mesh=mesh,
        in_specs=(
            P("rows", None, "cols"),
            P(None, None, None, "cols"),
            P(None, None, None, "cols"),
            P(),
            P("rows", "cols", None),
            P("rows", "cols"),
            P(None, "rows", "cols"),
            P(),
            P(),
            P(),
            P("rows", "cols", None),
        ),
        out_specs=(P("rows", "cols", None), P(), P(), P("rows", "cols", None)),
        check_vma=False,
    )
```

```python
import functools
import math

import jax
import jax.numpy as jnp
import numpy as np
from jax import lax
from jax.experimental import pallas as pl
from jax.experimental.pallas import tpu as pltpu
from jax.sharding import PartitionSpec as P

INSTANCES = 256
UPSCALE = 16
BOTH = ("rows", "cols")

norm_eps = 1e-05


RIM = 8
MARGIN = 16
KERNEL_VMEM = 20 * 1024 * 1024


class Layout:
    def __init__(self, tile_rows, tile_cols):
        self.rows, self.cols = tile_rows, tile_cols
        self.wide = tile_cols + 2 * RIM
        self.flat = (tile_rows + 6) * self.wide + 2 * MARGIN
        self.out_rows = tile_rows + 3
        self.out = self.out_rows * self.wide
        self.z = self.out + 2 * MARGIN
        self.own = tile_rows * self.wide + 2 * MARGIN
        self.kept = -(-self.out // 128) * 128


def vmem(count):
    return [pl.BlockSpec(memory_space=pltpu.VMEM)] * count


def call(body, outs, ins, scratch=(), flops=0, **fixed):
    return pl.pallas_call(
        functools.partial(body, **fixed),
        out_shape=outs,
        in_specs=vmem(len(ins)),
        out_specs=jax.tree.map(lambda _: pl.BlockSpec(memory_space=pltpu.VMEM), outs),
        scratch_shapes=list(scratch),
        compiler_params=pltpu.CompilerParams(vmem_limit_bytes=KERNEL_VMEM),
        cost_estimate=pl.CostEstimate(flops=flops, bytes_accessed=4 << 20, transcendentals=0),
    )(*ins)


def put_tiles(flat_ref, lay, main_ref, top_ref, bottom_ref, strip_ref):
    flat_ref[...] = jnp.zeros_like(flat_ref)
    for k in range(lay.rows + 5):
        base = MARGIN + k * lay.wide
        i = k - 3
        if i >= -2:
            if i < 0:
                row = top_ref[i + 2]
            elif i < lay.rows:
                row = main_ref[i]
            else:
                row = bottom_ref[i - lay.rows]
            flat_ref[base : base + lay.cols] = row
        flat_ref[base + lay.cols : base + lay.wide] = strip_ref[k]


def taps_matmul(flat_ref, square_ref, z_refs, lay, turned):
    count = z_refs[0].shape[0]
    chunks = 3
    step = count // chunks
    width = z_refs[0].shape[1]

    @pl.loop(0, chunks)
    def _(c):
        begin = pl.multiple_of(c * step, 16)
        parts = [flat_ref[pl.ds(begin + shift, step)] for shift in (0, lay.wide, 2 * lay.wide)]
        if turned:
            left = jnp.concatenate(parts[::-1], 1)
            result = lax.dot_general(
                left, square_ref[...], (((1,), (1,)), ((), ())), preferred_element_type=jnp.float32
            )
        else:
            left = jnp.concatenate(parts, 1)
            result = jnp.dot(left, square_ref[...], preferred_element_type=jnp.float32)
        for b in range(3):
            z_refs[b][pl.ds(begin, step)] = result[:, b * width : (b + 1) * width]


def put_square(square_ref, weight_ref, turned):
    width = weight_ref.shape[2]
    for a in range(3):
        for b in range(3):
            r, c = (b, a) if turned else (a, b)
            square_ref[r * width : (r + 1) * width, c * width : (c + 1) * width] = weight_ref[a, b]


def taken(z_refs, begin, count, turned):
    early, late = (2, 0) if turned else (0, 2)
    return (
        z_refs[early][pl.ds(begin + MARGIN - 1, count)]
        + z_refs[1][pl.ds(begin + MARGIN, count)]
        + z_refs[late][pl.ds(begin + MARGIN + 1, count)]
    )


def folded(value):
    return value.reshape(-1, 8, value.shape[-1]).sum(0)


def send_stats(out_ref, first, second):
    sums = jnp.concatenate(
        [jnp.sum(first, 0, keepdims=True), jnp.sum(second, 0, keepdims=True)], 0
    )
    out_ref[...] = jnp.zeros_like(out_ref)
    for d in range(out_ref.shape[0]):
        out_ref[d, 0:2] = sums


def cot_kernel(main, top, bottom, strip, weight, grad_out, flat, square, z0, z1, z2, *, lay):
    put_tiles(flat, lay, main, top, bottom, strip)
    put_square(square, weight, True)
    taps_matmul(flat, square, (z0, z1, z2), lay, True)

    @pl.loop(0, lay.out_rows)
    def _(r):
        begin = pl.multiple_of(r * lay.wide, 16)
        grad_out[pl.ds(begin, lay.wide)] = taken((z0, z1, z2), begin, lay.wide, True)


def mixed_kernel(
    main, top, bottom, strip, coarse, pooled, valid, weight, flat, act_out, stats, square, terms, z0,
    z1, z2, *, lay
):
    width = main.shape[2]
    flat[...] = jnp.zeros_like(flat)
    blocks = lay.cols // UPSCALE
    near = coarse[0]
    for c in range(1, coarse.shape[0]):
        near = near + coarse[c]
    terms[...] = near.astype(jnp.bfloat16).astype(jnp.float32) * valid[...] + pooled[...]
    for k in range(lay.rows + 5):
        base = MARGIN + k * lay.wide
        i = k - 3
        own, following = (i + UPSCALE) // UPSCALE, (i + 1 + UPSCALE) // UPSCALE

        def spread(block_row, block_col, rows):
            return jnp.broadcast_to(
                terms[block_row, block_col : block_col + 1], (rows, width)
            )

        if i >= -2:
            if i < 0:
                row = top[i + 2]
            elif i < lay.rows:
                row = main[i]
            else:
                row = bottom[i - lay.rows]
            added = jnp.concatenate([spread(own, b + 2, UPSCALE) for b in range(blocks)], 0)
            flat[base : base + lay.cols] = (row.astype(jnp.float32) + added).astype(jnp.bfloat16)
        zero = jnp.zeros((RIM, width), jnp.float32)
        right = spread(own, blocks + 2, RIM) if i >= -2 else zero
        left = spread(following, 1, RIM) if i + 1 < lay.rows + 2 else zero
        flat[base + lay.cols : base + lay.wide] = (
            strip[k].astype(jnp.float32) + jnp.concatenate([right, left], 0)
        ).astype(jnp.bfloat16)
    put_square(square, weight, False)
    taps_matmul(flat, square, (z0, z1, z2), lay, False)

    def step(r, sums):
        begin = pl.multiple_of(r * lay.wide, 16)
        value = taken((z0, z1, z2), begin, lay.wide, False)
        act_out[pl.ds(begin, lay.wide)] = value
        mine = ((r >= 2) & (r < lay.rows + 2)).astype(jnp.float32)
        own_value = value[: lay.cols] * mine
        return sums[0] + folded(own_value), sums[1] + folded(own_value * own_value)

    zero = jnp.zeros((8, width), jnp.float32)
    sums = lax.fori_loop(0, lay.out_rows, step, (zero, zero))
    send_stats(stats, *sums)


def act_moments(stats, pixel_total):
    sums = jnp.sum(stats[...], 0)
    mean = sums[0:1] / pixel_total
    return mean, lax.rsqrt(sums[1:2] / pixel_total - mean * mean + norm_eps)


def inside_masks(lay, width, row_devices, col_devices):
    my_row, my_col = lax.axis_index("rows"), lax.axis_index("cols")
    column = lax.broadcasted_iota(jnp.int32, (lay.wide, width), 0)
    has_right = (my_col < col_devices - 1).astype(jnp.float32)
    has_left = (my_col > 0).astype(jnp.float32)
    near = jnp.where(
        column < lay.cols, 1.0, jnp.where(column < lay.cols + RIM, has_right, 0.0)
    )
    following = jnp.where(column >= lay.cols + RIM, has_left, 0.0)

    def row_inside(i):
        row = my_row * lay.rows + i
        return ((row >= 0) & (row < lay.rows * row_devices)).astype(jnp.float32)

    return lambda r: near * row_inside(r - 2) + following * row_inside(r - 1)


def norm_kernel(
    act, stats, act_grad, activated, normed_out, grad_out, grad_stats, *, lay, grid, pixel_total
):
    width = act.shape[1]
    mean, inverse = act_moments(stats, pixel_total)
    mask = inside_masks(lay, width, *grid)
    activated[...] = jnp.zeros_like(activated)

    def step(r, sums):
        begin = pl.multiple_of(r * lay.wide, 16)
        normed = (act[pl.ds(begin, lay.wide)] - mean) * inverse
        gate = 1.0 / (1.0 + jnp.exp(-normed))
        inside = mask(r)
        activated[pl.ds(pl.multiple_of(begin + MARGIN + lay.wide, 16), lay.wide)] = (
            normed * gate * inside
        ).astype(jnp.bfloat16)
        grad = act_grad[pl.ds(begin, lay.wide)] * gate * (1.0 + normed * (1.0 - gate))
        normed_out[pl.ds(begin, lay.wide)] = normed
        grad_out[pl.ds(begin, lay.wide)] = grad
        mine = ((r >= 2) & (r < lay.rows + 2)).astype(jnp.float32)
        own_grad = grad[: lay.cols] * mine
        return sums[0] + folded(own_grad), sums[1] + folded(own_grad * normed[: lay.cols])

    zero = jnp.zeros((8, width), jnp.float32)
    sums = lax.fori_loop(0, lay.out_rows, step, (zero, zero))
    send_stats(grad_stats, *sums)


def weight_matmul(flat_ref, own_ref, total_ref, sent_ref, lay, chunk):
    count = lay.own
    first = MARGIN + 3 * lay.wide - MARGIN
    chunks = 3
    step = count // chunks
    width = own_ref.shape[1]
    total = None
    for c in range(chunks):
        begin = c * step
        left = jnp.concatenate(
            [
                flat_ref[first + begin + a * lay.wide : first + begin + a * lay.wide + step]
                for a in (-1, 0, 1)
            ],
            1,
        )
        right = jnp.concatenate(
            [
                own_ref[MARGIN + begin - b : MARGIN + begin - b + step].astype(jnp.bfloat16)
                for b in (-1, 0, 1)
            ],
            1,
        )
        part = lax.dot_general(
            left, right, (((0,), (0,)), ((), ())), preferred_element_type=jnp.float32
        )
        total = part if total is None else total + part
    for a in range(3):
        for b in range(3):
            total_ref[(a * 3 + b) * width : (a * 3 + b + 1) * width] = total[
                a * width : (a + 1) * width, b * width : (b + 1) * width
            ]
    padded = sent_ref.shape[1]
    for d in range(9 * width // chunk):
        sent_ref[d] = total_ref[d * chunk : d * chunk + padded].astype(jnp.bfloat16)


def second_kernel(
    activated, mixed, main, weight, enhanced, sent, square, z0, z1, z2, own, total, *, lay, chunk
):
    put_square(square, weight, False)
    taps_matmul(activated, square, (z0, z1, z2), lay, False)

    @pl.loop(0, lay.rows)
    def _(i):
        begin = pl.multiple_of((i + 2) * lay.wide, 16)
        value = taken((z0, z1, z2), begin, lay.cols, False)
        place = pl.multiple_of((i + 3) * lay.wide + MARGIN, 16)
        enhanced[i] = (mixed[pl.ds(place, lay.cols)].astype(jnp.float32) + value).astype(
            jnp.bfloat16
        )

    own[...] = jnp.zeros_like(own)

    @pl.loop(0, lay.rows)
    def _(i):
        place = pl.multiple_of(i * lay.wide + 2 * MARGIN, 16)
        own[pl.ds(place, lay.cols)] = main[i].astype(jnp.float32)

    weight_matmul(activated, own, total, sent, lay, chunk)


def first_kernel(
    stats, grad_stats, normed_ref, grad_ref, mixed, second, sent, kept, own, total, *, lay, grid,
    chunk, pixel_total
):
    width = normed_ref.shape[1]
    _, inverse = act_moments(stats, pixel_total)
    sums = jnp.sum(grad_stats[...], 0)
    grad_mean, cross_mean = sums[0:1] / pixel_total, sums[1:2] / pixel_total
    mask = inside_masks(lay, width, *grid)
    own[...] = jnp.zeros_like(own)
    kept[...] = jnp.zeros_like(kept)

    @pl.loop(0, lay.out_rows)
    def _(r):
        begin = pl.multiple_of(r * lay.wide, 16)
        value = inverse * (
            grad_ref[pl.ds(begin, lay.wide)]
            - grad_mean
            - normed_ref[pl.ds(begin, lay.wide)] * cross_mean
        )
        value = (value * mask(r)).astype(jnp.bfloat16)
        kept[pl.ds(begin, lay.wide)] = value

        @pl.when((r >= 2) & (r < lay.rows + 2))
        def _():
            place = pl.multiple_of((r - 2) * lay.wide + 2 * MARGIN, 16)
            own[pl.ds(place, lay.cols)] = value[: lay.cols].astype(jnp.float32)

    weight_matmul(mixed, own, total, sent, lay, chunk)
    for d in range(second.shape[0]):
        sent[second.shape[0] + d] = second[d]


def coarse_kernel(kept, picked, main, weight, out, *, lay):
    width = weight.shape[2]
    windows = jnp.dot(picked[...], kept[...], preferred_element_type=jnp.float32)
    block_rows, block_cols = lay.rows // UPSCALE, lay.cols // UPSCALE
    blocks = block_rows * block_cols
    summed = jnp.zeros((blocks, width), jnp.float32)
    for tap in range(9):
        summed = summed + lax.dot_general(
            windows[tap * blocks : (tap + 1) * blocks],
            weight[tap // 3, tap % 3].astype(jnp.float32),
            (((1,), (1,)), ((), ())),
            precision=lax.Precision.HIGHEST,
            preferred_element_type=jnp.float32,
        )
    for bi in range(block_rows):
        rows = jnp.zeros((lay.cols, width), jnp.float32)
        for i in range(UPSCALE):
            rows = rows + main[bi * UPSCALE + i].astype(jnp.float32)
        for bj in range(block_cols):
            k = bi * block_cols + bj
            cot = jnp.sum(rows[bj * UPSCALE : (bj + 1) * UPSCALE], 0, keepdims=True)
            out[k : k + 1] = (cot + summed[k : k + 1]) / UPSCALE


def share_kernel(received, sent, *, rescale):
    total = received[0].astype(jnp.float32)
    for d in range(1, received.shape[0]):
        total = total + received[d].astype(jnp.float32)
    total = (total * rescale).astype(jnp.bfloat16)
    for d in range(sent.shape[0]):
        sent[d] = total


def join_kernel(received, first, second, *, chunk):
    half = received.shape[0] // 2
    for out, begin in ((first, 0), (second, half)):
        for d in range(half):
            out[d * chunk : (d + 1) * chunk] = received[begin + d].astype(jnp.float32)[:chunk]


def window_picks(lay):
    place = np.arange(lay.kept)
    slot, column = place // lay.wide + 1, place % lay.wide
    behind = column >= lay.cols + RIM
    i = np.where(behind, slot - 2, slot - 3)
    j = np.where(behind, column - lay.wide, column)
    rows = []
    for a in range(3):
        for b in range(3):
            y, x = i + a - 1, j + b - 1
            for bi in range(lay.rows // UPSCALE):
                for bj in range(lay.cols // UPSCALE):
                    rows.append((y // UPSCALE == bi) & (x // UPSCALE == bj) & (place < lay.out))
    return jnp.asarray(np.stack(rows), jnp.bfloat16)


def to_all(payload, axis):
    return lax.all_to_all(payload, axis, 0, 0)


def pieces(array):
    high = array.astype(jnp.bfloat16)
    rest = array - high.astype(jnp.float32)
    middle = rest.astype(jnp.bfloat16)
    return high, middle, (rest - middle.astype(jnp.float32)).astype(jnp.bfloat16)


def lane_roll(value, shift):
    return pltpu.roll(value, shift % value.shape[1], 1)


def pack_kernel(features, labels, band, sent, sums):
    encoder_width, tile_rows, tile_cols = features.shape
    block_rows, block_cols = tile_rows // UPSCALE, tile_cols // UPSCALE
    blocks = block_rows * block_cols
    sums[...] = jnp.zeros_like(sums)
    slot = lax.broadcasted_iota(jnp.int32, (blocks, tile_cols), 0)
    column = lax.broadcasted_iota(jnp.int32, (blocks, tile_cols), 1)
    total = jnp.zeros((blocks, 128), jnp.float32)
    for r in range(block_rows):
        sums[0:encoder_width] = jnp.sum(features[:, r * UPSCALE : (r + 1) * UPSCALE], 1)
        sums[encoder_width : encoder_width + 1] = (
            labels[r * UPSCALE : r * UPSCALE + 1].astype(jnp.float32) / UPSCALE
        )
        low = (slot - r * block_cols) * UPSCALE
        picked = ((column >= low) & (column < low + UPSCALE)).astype(jnp.float32)
        total = total + lax.dot_general(
            picked,
            sums[...],
            (((1,), (1,)), ((), ())),
            precision=lax.Precision.HIGHEST,
            preferred_element_type=jnp.float32,
        )
    high, middle, low = pieces(total)
    packed = (
        high.astype(jnp.float32)
        + lane_roll(middle.astype(jnp.float32), 32)
        + lane_roll(low.astype(jnp.float32), 64)
    )
    value = jnp.concatenate([band[...].astype(jnp.float32), packed], 0).astype(jnp.bfloat16)
    for d in range(sent.shape[0]):
        sent[d] = value


def pool_kernel(received, places, weight, pooled, valid, table, *, near, coarse):
    block_rows, block_cols = near
    coarse_rows, coarse_cols = coarse
    encoder_width = weight.shape[0]
    devices, rows, _ = received.shape
    lane = lax.broadcasted_iota(jnp.int32, (8, 128), 1)
    for d in range(devices):
        packed = received[d].astype(jnp.float32)[rows - 8 :]
        value = packed + lane_roll(packed, -32) + lane_roll(packed, -64)
        table[d * 8 : (d + 1) * 8] = jnp.where(lane <= encoder_width, value, 0.0)
    exact = dict(precision=lax.Precision.HIGHEST, preferred_element_type=jnp.float32)
    row0 = lax.axis_index("rows") * block_rows - 1
    col0 = lax.axis_index("cols") * block_cols - 2

    def position(shape):
        q = lax.broadcasted_iota(jnp.int32, shape, 0)
        return row0 + (q >> 3), col0 + (q & 7)

    count = pooled.shape[0]
    row, col = position((count, devices * 8))
    chosen = ((row == places[0:1]) & (col == places[1:2])).astype(jnp.float32)
    mine = jnp.dot(chosen, table[...], **exact)[:, encoder_width : encoder_width + 1]
    pick = (lane == encoder_width).astype(jnp.float32)
    every = lax.dot_general(pick, table[...], (((1,), (1,)), ((), ())), **exact)[0:1]
    same = (mine == every).astype(jnp.float32)
    sums = jnp.dot(same, table[...], **exact)
    members = jnp.sum(same, 1, keepdims=True) * float(UPSCALE * UPSCALE)
    averages = sums / jnp.maximum(members, 1.0)
    result = jnp.dot(averages[:, :encoder_width], weight[...], **exact)
    row, col = position(pooled.shape)
    inside = (row >= 0) & (row < coarse_rows) & (col >= 0) & (col < coarse_cols)
    pooled[...] = jnp.where(inside, result, 0.0)
    valid[...] = inside.astype(jnp.float32)


def channel_conv(rows_ref, weight, shifted, out_rows, cols):
    width = weight.shape[3]
    count = out_rows * cols
    sums = None
    for a in range(3):
        left = rows_ref[a * cols : a * cols + count]
        if width % 128:
            part = [
                jnp.dot(left, weight[a, b], preferred_element_type=jnp.float32) for b in range(3)
            ]
        else:
            right = jnp.concatenate([weight[a, b] for b in range(3)], 1)
            part = jnp.dot(left, right, preferred_element_type=jnp.float32)
            part = [part[:, b * width : (b + 1) * width] for b in range(3)]
        sums = part if sums is None else [s + p for s, p in zip(sums, part)]
    shifted[...] = jnp.zeros_like(shifted)
    total = sums[1]
    for b in (0, 2):
        shifted[:, 8 : 8 + cols] = sums[b].reshape(out_rows, cols, width)
        total = total + shifted[:, 7 + b : 7 + b + cols].reshape(count, width)
    return total


def hidden_kernel(source, weight, sent, rows_ref, shifted, kept, *, grid, band, direct):
    row_devices, col_devices = grid
    band_rows, cols = band
    coarse_rows = row_devices * band_rows
    width = weight.shape[3]
    rows_ref[...] = jnp.zeros_like(rows_ref)
    if direct:
        for d in range(row_devices * col_devices):
            r, c = d // col_devices, d % col_devices
            begin = (1 + r * band_rows) * cols
            rows_ref[begin : begin + band_rows * cols, c * width : (c + 1) * width] = source[
                d, : band_rows * cols
            ]
    else:
        rows_ref[cols : cols + coarse_rows * cols] = source[...]
    raw = channel_conv(rows_ref, weight, shifted, coarse_rows, cols)
    pixels = coarse_rows * cols
    mean = jnp.sum(raw, 0, keepdims=True) / pixels
    variance = jnp.sum(raw * raw, 0, keepdims=True) / pixels - mean * mean
    hidden = jnp.maximum((raw - mean) * lax.rsqrt(variance + norm_eps), 0.0)
    kept[...] = jnp.zeros_like(kept)
    kept[2 : 2 + coarse_rows] = hidden.astype(jnp.bfloat16).reshape(coarse_rows, cols, width)
    near = kept[pl.ds(lax.axis_index("rows") * band_rows, band_rows + 4)]
    near = near.reshape((band_rows + 4) * cols, width)
    for d in range(sent.shape[0]):
        sent[d] = near


def project_kernel(
    received, weight, source, project, sent, rows_ref, shifted, residual, spread, *, grid, band,
    direct
):
    row_devices, col_devices = grid
    band_rows, cols = band
    width = weight.shape[3]
    my_col = lax.axis_index("cols")
    for c in range(col_devices):
        rows_ref[:, c * width : (c + 1) * width] = received[c]
    raw = channel_conv(rows_ref, weight, shifted, band_rows + 2, cols)
    count = (band_rows + 2) * cols
    if direct:
        residual[...] = jnp.zeros_like(residual)
        for r in range(row_devices):
            piece = source[r * col_devices + my_col, : band_rows * cols]
            residual[1 + r * band_rows : 1 + (r + 1) * band_rows] = piece.reshape(
                band_rows, cols, width
            )
        base = residual[pl.ds(lax.axis_index("rows") * band_rows, band_rows + 2)]
        base = base.reshape(count, width)
    else:
        base = source[...]
    result = (base.astype(jnp.float32) + raw).astype(jnp.bfloat16)
    rows = project[pl.ds(pl.multiple_of(my_col * width, width), width)]
    partial = jnp.dot(result, rows, preferred_element_type=jnp.float32)
    spread[...] = jnp.zeros_like(spread)
    spread[:, 8 : 8 + cols] = partial.reshape(band_rows + 2, cols, partial.shape[1])
    step = cols // col_devices
    for j in range(col_devices):
        sent[j] = spread[:, 6 + j * step : 6 + j * step + sent.shape[2]]


def per_device(
    global_in,
    global_first,
    global_second,
    project_weight,
    enhancer_input,
    instance_map,
    encoder_features,
    instance_weight,
    enhancer_first,
    enhancer_second,
    output_cotangent,
):
    row_devices, col_devices = lax.axis_size("rows"), lax.axis_size("cols")
    devices = row_devices * col_devices
    my_row, my_col = lax.axis_index("rows"), lax.axis_index("cols")
    band_rows, band_cols, width_share = global_in.shape
    tile_rows, tile_cols, local_width = enhancer_input.shape
    coarse_rows = band_rows * row_devices
    block_rows = tile_rows // UPSCALE
    block_cols = tile_cols // UPSCALE
    blocks = block_rows * block_cols
    encoder_width = encoder_features.shape[0]

    lay = Layout(tile_rows, tile_cols)
    width = local_width
    grid = (row_devices, col_devices)
    band = (band_rows, band_cols)
    direct = width_share == 128
    main = global_in.reshape(-1, 128)
    main_rows = main.shape[0]
    sent_input = call(
        pack_kernel,
        jax.ShapeDtypeStruct((devices, main_rows + 8, 128), jnp.bfloat16),
        (encoder_features, instance_map, main),
        [pltpu.VMEM((128, tile_cols), jnp.float32)],
    )
    tops = jnp.stack([enhancer_input[-2:], output_cotangent[-2:]])
    bottoms = jnp.stack([enhancer_input[:2], output_cotangent[:2]])
    sent_input, tops, bottoms = lax.optimization_barrier((sent_input, tops, bottoms))
    everything = to_all(sent_input, BOTH)

    row_up = [(i, i + 1) for i in range(row_devices - 1)]
    row_down = [(j, i) for i, j in row_up]
    col_up = [(i, i + 1) for i in range(col_devices - 1)]
    col_down = [(j, i) for i, j in col_up]
    top = lax.ppermute(tops, "rows", row_up)
    bottom = lax.ppermute(bottoms, "rows", row_down)
    both = jnp.stack([enhancer_input, output_cotangent])
    tall_last = jnp.concatenate([top[:, :, -RIM:], both[:, :, -RIM:], bottom[:, :, -RIM:]], 1)
    tall_first = jnp.concatenate([top[:, :, :RIM], both[:, :, :RIM], bottom[:, :, :RIM]], 1)
    left = lax.ppermute(tall_last, "cols", col_up)
    right = lax.ppermute(tall_first, "cols", col_down)
    strip = jnp.concatenate(
        [
            jnp.pad(right, ((0, 0), (1, 0), (0, 0), (0, 0))),
            jnp.pad(left, ((0, 0), (0, 1), (0, 0), (0, 0))),
        ],
        2,
    )
    pixel_total = float(tile_rows * tile_cols * devices)
    chunk = 18 * width // devices
    padded_chunk = -(-chunk // 8) * 8
    square = pltpu.VMEM((3 * width, 3 * width), jnp.bfloat16)
    z = [pltpu.VMEM((lay.z, width), jnp.float32)] * 3
    own = pltpu.VMEM((lay.own + 2 * MARGIN, width), jnp.float32)
    total = pltpu.VMEM((9 * width + 64, width), jnp.float32)
    flat_shape = jax.ShapeDtypeStruct((lay.flat, width), jnp.bfloat16)
    out_shape = jax.ShapeDtypeStruct((lay.out, width), jnp.float32)
    stats_shape = jax.ShapeDtypeStruct((devices, 8, width), jnp.float32)
    sent_shape = jax.ShapeDtypeStruct((devices, padded_chunk, width), jnp.bfloat16)
    half_shape = jax.ShapeDtypeStruct((devices // 2, padded_chunk, width), jnp.bfloat16)
    conv_flops = 18 * width * width * lay.out

    act_grad = call(
        cot_kernel,
        out_shape,
        (output_cotangent, top[1], bottom[1], strip[1], enhancer_second),
        [pltpu.VMEM((lay.flat, width), jnp.bfloat16), square, *z],
        conv_flops,
        lay=lay,
    )

    place = np.arange(devices * blocks)
    owner, slot = place // blocks, place % blocks
    places = np.zeros((8, devices * blocks), np.int32)
    places[0] = owner // col_devices * block_rows + slot // block_cols
    places[1] = owner % col_devices * block_cols + slot % block_cols
    near_shape = jax.ShapeDtypeStruct(((block_rows + 2) * 8, width), jnp.float32)
    pooled, valid = call(
        pool_kernel,
        (near_shape, near_shape),
        (everything, jnp.asarray(places), instance_weight),
        [pltpu.VMEM((devices * 8, 128), jnp.float32)],
        near=(block_rows, block_cols),
        coarse=(coarse_rows, band_cols),
    )
    channels = width_share * col_devices
    if direct:
        source = base = everything
    else:
        gathered = everything[:, :main_rows].reshape(
            row_devices, col_devices, band_rows, band_cols, width_share
        )
        source = gathered.transpose(0, 2, 3, 1, 4).reshape(coarse_rows * band_cols, channels)
        mine = lax.dynamic_index_in_dim(gathered, my_col, 1, keepdims=False)
        mine = jnp.pad(
            mine.reshape(coarse_rows, band_cols, width_share), ((1, 1), (0, 0), (0, 0))
        )
        base = lax.dynamic_slice_in_dim(mine, my_row * band_rows, band_rows + 2, 0)
        base = base.reshape(-1, width_share)
    near_rows = band_rows + 4
    sent_hidden = call(
        hidden_kernel,
        jax.ShapeDtypeStruct((col_devices, near_rows * band_cols, width_share), jnp.bfloat16),
        (source, global_first),
        [
            pltpu.VMEM(((coarse_rows + 2) * band_cols, channels), jnp.bfloat16),
            pltpu.VMEM((coarse_rows, band_cols + 16, width_share), jnp.float32),
            pltpu.VMEM((coarse_rows + 4, band_cols, width_share), jnp.bfloat16),
        ],
        18 * coarse_rows * band_cols * channels * width_share,
        grid=grid,
        band=band,
        direct=direct,
    )
    near_hidden = to_all(sent_hidden, "cols")
    sent_coarse = call(
        project_kernel,
        jax.ShapeDtypeStruct((col_devices, band_rows + 2, 8, width), jnp.float32),
        (near_hidden, global_second, base, project_weight),
        [
            pltpu.VMEM((near_rows * band_cols, channels), jnp.bfloat16),
            pltpu.VMEM((band_rows + 2, band_cols + 16, width_share), jnp.float32),
            pltpu.VMEM((coarse_rows + 2, band_cols, width_share), jnp.bfloat16),
            pltpu.VMEM((band_rows + 2, band_cols + 16, width), jnp.float32),
        ],
        18 * (band_rows + 2) * band_cols * channels * width_share,
        grid=grid,
        band=band,
        direct=direct,
    )
    near_coarse = to_all(sent_coarse, "cols")
    terms = (near_coarse, pooled.reshape(-1, 8, width), valid.reshape(-1, 8, width))

    mixed, first_act, stats = call(
        mixed_kernel,
        (flat_shape, out_shape, stats_shape),
        (enhancer_input, top[0], bottom[0], strip[0], *terms, enhancer_first),
        [square, pltpu.VMEM((block_rows + 2, 8, width), jnp.float32), *z],
        conv_flops,
        lay=lay,
    )
    stats = to_all(stats, BOTH)
    activated, normed_act, normed_grad, grad_stats = call(
        norm_kernel,
        (flat_shape, out_shape, out_shape, stats_shape),
        (first_act, stats, act_grad),
        lay=lay,
        grid=grid,
        pixel_total=pixel_total,
    )
    grad_stats = to_all(grad_stats, BOTH)
    enhanced, second_sent = call(
        second_kernel,
        (jax.ShapeDtypeStruct((tile_rows, tile_cols, width), jnp.bfloat16), half_shape),
        (activated, mixed, output_cotangent, enhancer_second),
        [square, *z, own, total],
        2 * conv_flops,
        lay=lay,
        chunk=chunk,
    )
    sent_both, kept = call(
        first_kernel,
        (sent_shape, jax.ShapeDtypeStruct((lay.kept, width), jnp.bfloat16)),
        (stats, grad_stats, normed_act, normed_grad, mixed, second_sent),
        [own, total],
        conv_flops,
        lay=lay,
        grid=grid,
        chunk=chunk,
        pixel_total=pixel_total,
    )
    part = to_all(sent_both, BOTH)
    rescale = 1.0 / math.sqrt(pixel_total)
    global_gradient = call(
        coarse_kernel,
        jax.ShapeDtypeStruct((blocks, width), jnp.float32),
        (kept, window_picks(lay), output_cotangent, enhancer_first),
        (),
        lay=lay,
    )
    share = to_all(call(share_kernel, sent_shape, (part,), rescale=rescale), BOTH)
    whole_shape = jax.ShapeDtypeStruct((9 * width, width), jnp.float32)
    first_total, second_total = call(
        join_kernel, (whole_shape, whole_shape), (share,), chunk=chunk
    )
    return (
        enhanced,
        first_total.reshape(3, 3, width, width),
        second_total.reshape(3, 3, width, width),
        global_gradient.reshape(block_rows, block_cols, width),
    )


def solution(mesh):
    return jax.shard_map(
        per_device,
        mesh=mesh,
        in_specs=(
            P("rows", None, "cols"),
            P(None, None, None, "cols"),
            P(None, None, None, "cols"),
            P(),
            P("rows", "cols", None),
            P("rows", "cols"),
            P(None, "rows", "cols"),
            P(),
            P(),
            P(),
            P("rows", "cols", None),
        ),
        out_specs=(P("rows", "cols", None), P(), P(), P("rows", "cols", None)),
        check_vma=False,
    )
```

```python
import functools
import math

import jax
import jax.numpy as jnp
import numpy as np
from jax import lax
from jax.experimental import pallas as pl
from jax.experimental.pallas import tpu as pltpu
from jax.sharding import PartitionSpec as P

INSTANCES = 256
UPSCALE = 16
BOTH = ("rows", "cols")

norm_eps = 1e-05


RIM = 8
MARGIN = 16
KERNEL_VMEM = 20 * 1024 * 1024


class Layout:
    def __init__(self, tile_rows, tile_cols):
        self.rows, self.cols = tile_rows, tile_cols
        self.wide = tile_cols + 2 * RIM
        self.flat = (tile_rows + 6) * self.wide + 2 * MARGIN
        self.out_rows = tile_rows + 3
        self.out = self.out_rows * self.wide
        self.z = self.out + 2 * MARGIN
        self.own = tile_rows * self.wide + 2 * MARGIN
        self.kept = -(-self.out // 128) * 128


def vmem(count):
    return [pl.BlockSpec(memory_space=pltpu.VMEM)] * count


def call(body, outs, ins, scratch=(), flops=0, **fixed):
    return pl.pallas_call(
        functools.partial(body, **fixed),
        out_shape=outs,
        in_specs=vmem(len(ins)),
        out_specs=jax.tree.map(lambda _: pl.BlockSpec(memory_space=pltpu.VMEM), outs),
        scratch_shapes=list(scratch),
        compiler_params=pltpu.CompilerParams(vmem_limit_bytes=KERNEL_VMEM),
        cost_estimate=pl.CostEstimate(flops=flops, bytes_accessed=4 << 20, transcendentals=0),
    )(*ins)


def put_tiles(flat_ref, lay, main_ref, top_ref, bottom_ref, strip_ref):
    flat_ref[...] = jnp.zeros_like(flat_ref)
    for k in range(lay.rows + 5):
        base = MARGIN + k * lay.wide
        i = k - 3
        if i >= -2:
            if i < 0:
                row = top_ref[i + 2]
            elif i < lay.rows:
                row = main_ref[i]
            else:
                row = bottom_ref[i - lay.rows]
            flat_ref[base : base + lay.cols] = row
        flat_ref[base + lay.cols : base + lay.wide] = strip_ref[k]


def taps_matmul(flat_ref, square_ref, z_refs, lay, turned):
    count = z_refs[0].shape[0]
    chunks = 3
    step = count // chunks
    width = z_refs[0].shape[1]

    @pl.loop(0, chunks)
    def _(c):
        begin = pl.multiple_of(c * step, 16)
        parts = [flat_ref[pl.ds(begin + shift, step)] for shift in (0, lay.wide, 2 * lay.wide)]
        if turned:
            left = jnp.concatenate(parts[::-1], 1)
            result = lax.dot_general(
                left, square_ref[...], (((1,), (1,)), ((), ())), preferred_element_type=jnp.float32
            )
        else:
            left = jnp.concatenate(parts, 1)
            result = jnp.dot(left, square_ref[...], preferred_element_type=jnp.float32)
        for b in range(3):
            z_refs[b][pl.ds(begin, step)] = result[:, b * width : (b + 1) * width]


def put_square(square_ref, weight_ref, turned):
    width = weight_ref.shape[2]
    for a in range(3):
        for b in range(3):
            r, c = (b, a) if turned else (a, b)
            square_ref[r * width : (r + 1) * width, c * width : (c + 1) * width] = weight_ref[a, b]


def taken(z_refs, begin, count, turned):
    early, late = (2, 0) if turned else (0, 2)
    return (
        z_refs[early][pl.ds(begin + MARGIN - 1, count)]
        + z_refs[1][pl.ds(begin + MARGIN, count)]
        + z_refs[late][pl.ds(begin + MARGIN + 1, count)]
    )


def folded(value):
    return value.reshape(-1, 8, value.shape[-1]).sum(0)


def send_stats(out_ref, first, second):
    sums = jnp.concatenate(
        [jnp.sum(first, 0, keepdims=True), jnp.sum(second, 0, keepdims=True)], 0
    )
    out_ref[...] = jnp.zeros_like(out_ref)
    for d in range(out_ref.shape[0]):
        out_ref[d, 0:2] = sums


def cot_kernel(main, top, bottom, strip, weight, grad_out, flat, square, z0, z1, z2, *, lay):
    put_tiles(flat, lay, main, top, bottom, strip)
    put_square(square, weight, True)
    taps_matmul(flat, square, (z0, z1, z2), lay, True)

    @pl.loop(0, lay.out_rows)
    def _(r):
        begin = pl.multiple_of(r * lay.wide, 16)
        grad_out[pl.ds(begin, lay.wide)] = taken((z0, z1, z2), begin, lay.wide, True)


def mixed_kernel(
    main, top, bottom, strip, coarse, pooled, valid, weight, flat, act_out, stats, square, terms, z0,
    z1, z2, *, lay
):
    width = main.shape[2]
    flat[...] = jnp.zeros_like(flat)
    blocks = lay.cols // UPSCALE
    near = coarse[0]
    for c in range(1, coarse.shape[0]):
        near = near + coarse[c]
    terms[...] = near.astype(jnp.bfloat16).astype(jnp.float32) * valid[...] + pooled[...]
    for k in range(lay.rows + 5):
        base = MARGIN + k * lay.wide
        i = k - 3
        own, following = (i + UPSCALE) // UPSCALE, (i + 1 + UPSCALE) // UPSCALE

        def spread(block_row, block_col, rows):
            return jnp.broadcast_to(
                terms[block_row, block_col : block_col + 1], (rows, width)
            )

        if i >= -2:
            if i < 0:
                row = top[i + 2]
            elif i < lay.rows:
                row = main[i]
            else:
                row = bottom[i - lay.rows]
            added = jnp.concatenate([spread(own, b + 2, UPSCALE) for b in range(blocks)], 0)
            flat[base : base + lay.cols] = (row.astype(jnp.float32) + added).astype(jnp.bfloat16)
        zero = jnp.zeros((RIM, width), jnp.float32)
        right = spread(own, blocks + 2, RIM) if i >= -2 else zero
        left = spread(following, 1, RIM) if i + 1 < lay.rows + 2 else zero
        flat[base + lay.cols : base + lay.wide] = (
            strip[k].astype(jnp.float32) + jnp.concatenate([right, left], 0)
        ).astype(jnp.bfloat16)
    put_square(square, weight, False)
    taps_matmul(flat, square, (z0, z1, z2), lay, False)

    def step(r, sums):
        begin = pl.multiple_of(r * lay.wide, 16)
        value = taken((z0, z1, z2), begin, lay.wide, False)
        act_out[pl.ds(begin, lay.wide)] = value
        mine = ((r >= 2) & (r < lay.rows + 2)).astype(jnp.float32)
        own_value = value[: lay.cols] * mine
        return sums[0] + folded(own_value), sums[1] + folded(own_value * own_value)

    zero = jnp.zeros((8, width), jnp.float32)
    sums = lax.fori_loop(0, lay.out_rows, step, (zero, zero))
    send_stats(stats, *sums)


def act_moments(stats, pixel_total):
    sums = jnp.sum(stats[...], 0)
    mean = sums[0:1] / pixel_total
    return mean, lax.rsqrt(sums[1:2] / pixel_total - mean * mean + norm_eps)


def inside_masks(lay, width, row_devices, col_devices):
    my_row, my_col = lax.axis_index("rows"), lax.axis_index("cols")
    column = lax.broadcasted_iota(jnp.int32, (lay.wide, width), 0)
    has_right = (my_col < col_devices - 1).astype(jnp.float32)
    has_left = (my_col > 0).astype(jnp.float32)
    near = jnp.where(
        column < lay.cols, 1.0, jnp.where(column < lay.cols + RIM, has_right, 0.0)
    )
    following = jnp.where(column >= lay.cols + RIM, has_left, 0.0)

    def row_inside(i):
        row = my_row * lay.rows + i
        return ((row >= 0) & (row < lay.rows * row_devices)).astype(jnp.float32)

    return lambda r: near * row_inside(r - 2) + following * row_inside(r - 1)


def norm_kernel(
    act, stats, act_grad, activated, normed_out, grad_out, grad_stats, *, lay, grid, pixel_total
):
    width = act.shape[1]
    mean, inverse = act_moments(stats, pixel_total)
    mask = inside_masks(lay, width, *grid)
    activated[...] = jnp.zeros_like(activated)

    def step(r, sums):
        begin = pl.multiple_of(r * lay.wide, 16)
        normed = (act[pl.ds(begin, lay.wide)] - mean) * inverse
        gate = 1.0 / (1.0 + jnp.exp(-normed))
        inside = mask(r)
        activated[pl.ds(pl.multiple_of(begin + MARGIN + lay.wide, 16), lay.wide)] = (
            normed * gate * inside
        ).astype(jnp.bfloat16)
        grad = act_grad[pl.ds(begin, lay.wide)] * gate * (1.0 + normed * (1.0 - gate))
        normed_out[pl.ds(begin, lay.wide)] = normed
        grad_out[pl.ds(begin, lay.wide)] = grad
        mine = ((r >= 2) & (r < lay.rows + 2)).astype(jnp.float32)
        own_grad = grad[: lay.cols] * mine
        return sums[0] + folded(own_grad), sums[1] + folded(own_grad * normed[: lay.cols])

    zero = jnp.zeros((8, width), jnp.float32)
    sums = lax.fori_loop(0, lay.out_rows, step, (zero, zero))
    send_stats(grad_stats, *sums)


def weight_matmul(flat_ref, own_ref, total_ref, sent_ref, lay, chunk):
    count = lay.own
    first = MARGIN + 3 * lay.wide - MARGIN
    chunks = 3
    step = count // chunks
    width = own_ref.shape[1]
    total = None
    for c in range(chunks):
        begin = c * step
        left = jnp.concatenate(
            [
                flat_ref[first + begin + a * lay.wide : first + begin + a * lay.wide + step]
                for a in (-1, 0, 1)
            ],
            1,
        )
        right = jnp.concatenate(
            [
                own_ref[MARGIN + begin - b : MARGIN + begin - b + step].astype(jnp.bfloat16)
                for b in (-1, 0, 1)
            ],
            1,
        )
        part = lax.dot_general(
            left, right, (((0,), (0,)), ((), ())), preferred_element_type=jnp.float32
        )
        total = part if total is None else total + part
    for a in range(3):
        for b in range(3):
            total_ref[(a * 3 + b) * width : (a * 3 + b + 1) * width] = total[
                a * width : (a + 1) * width, b * width : (b + 1) * width
            ]
    padded = sent_ref.shape[1]
    for d in range(9 * width // chunk):
        sent_ref[d] = total_ref[d * chunk : d * chunk + padded].astype(jnp.bfloat16)


def second_kernel(
    activated, mixed, main, weight, enhanced, sent, square, z0, z1, z2, own, total, *, lay, chunk
):
    put_square(square, weight, False)
    taps_matmul(activated, square, (z0, z1, z2), lay, False)

    @pl.loop(0, lay.rows)
    def _(i):
        begin = pl.multiple_of((i + 2) * lay.wide, 16)
        value = taken((z0, z1, z2), begin, lay.cols, False)
        place = pl.multiple_of((i + 3) * lay.wide + MARGIN, 16)
        enhanced[i] = (mixed[pl.ds(place, lay.cols)].astype(jnp.float32) + value).astype(
            jnp.bfloat16
        )

    own[...] = jnp.zeros_like(own)

    @pl.loop(0, lay.rows)
    def _(i):
        place = pl.multiple_of(i * lay.wide + 2 * MARGIN, 16)
        own[pl.ds(place, lay.cols)] = main[i].astype(jnp.float32)

    weight_matmul(activated, own, total, sent, lay, chunk)


def first_kernel(
    stats, grad_stats, normed_ref, grad_ref, mixed, second, sent, kept, own, total, *, lay, grid,
    chunk, pixel_total
):
    width = normed_ref.shape[1]
    _, inverse = act_moments(stats, pixel_total)
    sums = jnp.sum(grad_stats[...], 0)
    grad_mean, cross_mean = sums[0:1] / pixel_total, sums[1:2] / pixel_total
    mask = inside_masks(lay, width, *grid)
    own[...] = jnp.zeros_like(own)
    kept[...] = jnp.zeros_like(kept)

    @pl.loop(0, lay.out_rows)
    def _(r):
        begin = pl.multiple_of(r * lay.wide, 16)
        value = inverse * (
            grad_ref[pl.ds(begin, lay.wide)]
            - grad_mean
            - normed_ref[pl.ds(begin, lay.wide)] * cross_mean
        )
        value = (value * mask(r)).astype(jnp.bfloat16)
        kept[pl.ds(begin, lay.wide)] = value

        @pl.when((r >= 2) & (r < lay.rows + 2))
        def _():
            place = pl.multiple_of((r - 2) * lay.wide + 2 * MARGIN, 16)
            own[pl.ds(place, lay.cols)] = value[: lay.cols].astype(jnp.float32)

    weight_matmul(mixed, own, total, sent, lay, chunk)
    for d in range(second.shape[0]):
        sent[second.shape[0] + d] = second[d]


def coarse_kernel(kept, picked, main, weight, out, *, lay):
    width = weight.shape[2]
    windows = jnp.dot(picked[...], kept[...], preferred_element_type=jnp.float32)
    block_rows, block_cols = lay.rows // UPSCALE, lay.cols // UPSCALE
    blocks = block_rows * block_cols
    summed = jnp.zeros((blocks, width), jnp.float32)
    for tap in range(9):
        summed = summed + lax.dot_general(
            windows[tap * blocks : (tap + 1) * blocks],
            weight[tap // 3, tap % 3].astype(jnp.float32),
            (((1,), (1,)), ((), ())),
            precision=lax.Precision.HIGHEST,
            preferred_element_type=jnp.float32,
        )
    for bi in range(block_rows):
        rows = jnp.zeros((lay.cols, width), jnp.float32)
        for i in range(UPSCALE):
            rows = rows + main[bi * UPSCALE + i].astype(jnp.float32)
        for bj in range(block_cols):
            k = bi * block_cols + bj
            cot = jnp.sum(rows[bj * UPSCALE : (bj + 1) * UPSCALE], 0, keepdims=True)
            out[k : k + 1] = (cot + summed[k : k + 1]) / UPSCALE


def share_kernel(received, sent, *, rescale):
    total = received[0].astype(jnp.float32)
    for d in range(1, received.shape[0]):
        total = total + received[d].astype(jnp.float32)
    total = (total * rescale).astype(jnp.bfloat16)
    for d in range(sent.shape[0]):
        sent[d] = total


def join_kernel(mine, other, first, second, *, chunk, grid):
    row_devices, col_devices = grid
    half, pairs = row_devices * col_devices // 2, col_devices // 2
    core = lax.axis_index("cols") & 1
    for k in range(2):

        @pl.when(core == k)
        def _():
            for source, side in ((mine, k), (other, 1 - k)):
                for d in range(half):
                    owner = d // pairs * col_devices + d % pairs * 2 + side
                    out = first if owner < half else second
                    begin = owner % half * chunk
                    out[begin : begin + chunk] = source[d].astype(jnp.float32)[:chunk]


def window_picks(lay):
    place = np.arange(lay.kept)
    slot, column = place // lay.wide + 1, place % lay.wide
    behind = column >= lay.cols + RIM
    i = np.where(behind, slot - 2, slot - 3)
    j = np.where(behind, column - lay.wide, column)
    rows = []
    for a in range(3):
        for b in range(3):
            y, x = i + a - 1, j + b - 1
            for bi in range(lay.rows // UPSCALE):
                for bj in range(lay.cols // UPSCALE):
                    rows.append((y // UPSCALE == bi) & (x // UPSCALE == bj) & (place < lay.out))
    return jnp.asarray(np.stack(rows), jnp.bfloat16)


def to_all(payload, axis):
    return lax.all_to_all(payload, axis, 0, 0)


def from_all(payload, row_devices, col_devices):
    groups = [
        [r * col_devices + 2 * h + k for r in range(row_devices) for h in range(col_devices // 2)]
        for k in range(2)
    ]
    mine = lax.all_to_all(payload, BOTH, 0, 0, axis_index_groups=groups)
    swap = [(c, c ^ 1) for c in range(col_devices)]
    return mine, lax.ppermute(mine, "cols", swap)


def pieces(array):
    high = array.astype(jnp.bfloat16)
    rest = array - high.astype(jnp.float32)
    middle = rest.astype(jnp.bfloat16)
    return high, middle, (rest - middle.astype(jnp.float32)).astype(jnp.bfloat16)


def lane_roll(value, shift):
    return pltpu.roll(value, shift % value.shape[1], 1)


def pack_kernel(features, labels, band, sent, sums):
    encoder_width, tile_rows, tile_cols = features.shape
    block_rows, block_cols = tile_rows // UPSCALE, tile_cols // UPSCALE
    blocks = block_rows * block_cols
    sums[...] = jnp.zeros_like(sums)
    slot = lax.broadcasted_iota(jnp.int32, (blocks, tile_cols), 0)
    column = lax.broadcasted_iota(jnp.int32, (blocks, tile_cols), 1)
    total = jnp.zeros((blocks, 128), jnp.float32)
    for r in range(block_rows):
        sums[0:encoder_width] = jnp.sum(features[:, r * UPSCALE : (r + 1) * UPSCALE], 1)
        sums[encoder_width : encoder_width + 1] = (
            labels[r * UPSCALE : r * UPSCALE + 1].astype(jnp.float32) / UPSCALE
        )
        low = (slot - r * block_cols) * UPSCALE
        picked = ((column >= low) & (column < low + UPSCALE)).astype(jnp.float32)
        total = total + lax.dot_general(
            picked,
            sums[...],
            (((1,), (1,)), ((), ())),
            precision=lax.Precision.HIGHEST,
            preferred_element_type=jnp.float32,
        )
    high, middle, low = pieces(total)
    packed = (
        high.astype(jnp.float32)
        + lane_roll(middle.astype(jnp.float32), 32)
        + lane_roll(low.astype(jnp.float32), 64)
    )
    value = jnp.concatenate([band[...].astype(jnp.float32), packed], 0).astype(jnp.bfloat16)
    for d in range(sent.shape[0]):
        sent[d] = value


def pool_kernel(mine_ref, other_ref, places, weight, pooled, valid, table, *, near, coarse):
    block_rows, block_cols = near
    coarse_rows, coarse_cols = coarse
    encoder_width = weight.shape[0]
    half, rows, _ = mine_ref.shape
    devices = 2 * half
    lane = lax.broadcasted_iota(jnp.int32, (8, 128), 1)
    for d in range(devices):
        part = mine_ref[d] if d < half else other_ref[d - half]
        packed = part.astype(jnp.float32)[rows - 8 :]
        value = packed + lane_roll(packed, -32) + lane_roll(packed, -64)
        table[d * 8 : (d + 1) * 8] = jnp.where(lane <= encoder_width, value, 0.0)
    exact = dict(precision=lax.Precision.HIGHEST, preferred_element_type=jnp.float32)
    row0 = lax.axis_index("rows") * block_rows - 1
    col0 = lax.axis_index("cols") * block_cols - 2

    def position(shape):
        q = lax.broadcasted_iota(jnp.int32, shape, 0)
        return row0 + (q >> 3), col0 + (q & 7)

    count = pooled.shape[0]
    row, col = position((count, devices * 8))
    core = lax.axis_index("cols") & 1
    column = places[1:2] + block_cols * jnp.where(places[2:3] == 1, core, 1 - core)
    chosen = ((row == places[0:1]) & (col == column)).astype(jnp.float32)
    mine = jnp.dot(chosen, table[...], **exact)[:, encoder_width : encoder_width + 1]
    pick = (lane == encoder_width).astype(jnp.float32)
    every = lax.dot_general(pick, table[...], (((1,), (1,)), ((), ())), **exact)[0:1]
    same = (mine == every).astype(jnp.float32)
    sums = jnp.dot(same, table[...], **exact)
    members = jnp.sum(same, 1, keepdims=True) * float(UPSCALE * UPSCALE)
    averages = sums / jnp.maximum(members, 1.0)
    result = jnp.dot(averages[:, :encoder_width], weight[...], **exact)
    row, col = position(pooled.shape)
    inside = (row >= 0) & (row < coarse_rows) & (col >= 0) & (col < coarse_cols)
    pooled[...] = jnp.where(inside, result, 0.0)
    valid[...] = inside.astype(jnp.float32)


def channel_conv(rows_ref, weight, shifted, out_rows, cols):
    width = weight.shape[3]
    count = out_rows * cols
    sums = None
    for a in range(3):
        left = rows_ref[a * cols : a * cols + count]
        if width % 128:
            part = [
                jnp.dot(left, weight[a, b], preferred_element_type=jnp.float32) for b in range(3)
            ]
        else:
            right = jnp.concatenate([weight[a, b] for b in range(3)], 1)
            part = jnp.dot(left, right, preferred_element_type=jnp.float32)
            part = [part[:, b * width : (b + 1) * width] for b in range(3)]
        sums = part if sums is None else [s + p for s, p in zip(sums, part)]
    shifted[...] = jnp.zeros_like(shifted)
    total = sums[1]
    for b in (0, 2):
        shifted[:, 8 : 8 + cols] = sums[b].reshape(out_rows, cols, width)
        total = total + shifted[:, 7 + b : 7 + b + cols].reshape(count, width)
    return total


def hidden_kernel(mine, other, weight, sent, rows_ref, shifted, kept, *, grid, band, direct):
    row_devices, col_devices = grid
    band_rows, cols = band
    coarse_rows = row_devices * band_rows
    width = weight.shape[3]
    rows_ref[...] = jnp.zeros_like(rows_ref)
    if direct:
        pairs = col_devices // 2
        core = lax.axis_index("cols") & 1
        for source, side in ((mine, core), (other, 1 - core)):
            for d in range(row_devices * pairs):
                begin = (1 + d // pairs * band_rows) * cols
                lanes = pl.multiple_of((d % pairs * 2 + side) * width, width)
                rows_ref[begin : begin + band_rows * cols, pl.ds(lanes, width)] = source[
                    d, : band_rows * cols
                ]
    else:
        rows_ref[cols : cols + coarse_rows * cols] = mine[...]
    raw = channel_conv(rows_ref, weight, shifted, coarse_rows, cols)
    pixels = coarse_rows * cols
    mean = jnp.sum(raw, 0, keepdims=True) / pixels
    variance = jnp.sum(raw * raw, 0, keepdims=True) / pixels - mean * mean
    hidden = jnp.maximum((raw - mean) * lax.rsqrt(variance + norm_eps), 0.0)
    kept[...] = jnp.zeros_like(kept)
    kept[2 : 2 + coarse_rows] = hidden.astype(jnp.bfloat16).reshape(coarse_rows, cols, width)
    near = kept[pl.ds(lax.axis_index("rows") * band_rows, band_rows + 4)]
    near = near.reshape((band_rows + 4) * cols, width)
    for d in range(sent.shape[0]):
        sent[d] = near


def project_kernel(
    received, weight, source, project, sent, rows_ref, shifted, residual, spread, *, grid, band,
    direct
):
    row_devices, col_devices = grid
    band_rows, cols = band
    width = weight.shape[3]
    my_col = lax.axis_index("cols")
    for c in range(col_devices):
        rows_ref[:, c * width : (c + 1) * width] = received[c]
    raw = channel_conv(rows_ref, weight, shifted, band_rows + 2, cols)
    count = (band_rows + 2) * cols
    if direct:
        residual[...] = jnp.zeros_like(residual)
        for r in range(row_devices):
            piece = source[r * (col_devices // 2) + (my_col >> 1), : band_rows * cols]
            residual[1 + r * band_rows : 1 + (r + 1) * band_rows] = piece.reshape(
                band_rows, cols, width
            )
        base = residual[pl.ds(lax.axis_index("rows") * band_rows, band_rows + 2)]
        base = base.reshape(count, width)
    else:
        base = source[...]
    result = (base.astype(jnp.float32) + raw).astype(jnp.bfloat16)
    rows = project[pl.ds(pl.multiple_of(my_col * width, width), width)]
    partial = jnp.dot(result, rows, preferred_element_type=jnp.float32)
    spread[...] = jnp.zeros_like(spread)
    spread[:, 8 : 8 + cols] = partial.reshape(band_rows + 2, cols, partial.shape[1])
    step = cols // col_devices
    for j in range(col_devices):
        sent[j] = spread[:, 6 + j * step : 6 + j * step + sent.shape[2]]


def per_device(
    global_in,
    global_first,
    global_second,
    project_weight,
    enhancer_input,
    instance_map,
    encoder_features,
    instance_weight,
    enhancer_first,
    enhancer_second,
    output_cotangent,
):
    row_devices, col_devices = lax.axis_size("rows"), lax.axis_size("cols")
    devices = row_devices * col_devices
    my_row, my_col = lax.axis_index("rows"), lax.axis_index("cols")
    band_rows, band_cols, width_share = global_in.shape
    tile_rows, tile_cols, local_width = enhancer_input.shape
    coarse_rows = band_rows * row_devices
    block_rows = tile_rows // UPSCALE
    block_cols = tile_cols // UPSCALE
    blocks = block_rows * block_cols
    encoder_width = encoder_features.shape[0]

    lay = Layout(tile_rows, tile_cols)
    width = local_width
    grid = (row_devices, col_devices)
    band = (band_rows, band_cols)
    direct = width_share == 128
    main = global_in.reshape(-1, 128)
    main_rows = main.shape[0]
    sent_input = call(
        pack_kernel,
        jax.ShapeDtypeStruct((devices // 2, main_rows + 8, 128), jnp.bfloat16),
        (encoder_features, instance_map, main),
        [pltpu.VMEM((128, tile_cols), jnp.float32)],
    )
    mine, other = from_all(sent_input, row_devices, col_devices)
    late_input, late_cotangent, _ = lax.optimization_barrier(
        (enhancer_input, output_cotangent, sent_input)
    )
    tops = jnp.stack([late_input[-2:], late_cotangent[-2:]])
    bottoms = jnp.stack([late_input[:2], late_cotangent[:2]])

    row_up = [(i, i + 1) for i in range(row_devices - 1)]
    row_down = [(j, i) for i, j in row_up]
    col_up = [(i, i + 1) for i in range(col_devices - 1)]
    col_down = [(j, i) for i, j in col_up]
    top = lax.ppermute(tops, "rows", row_up)
    bottom = lax.ppermute(bottoms, "rows", row_down)
    pixel_total = float(tile_rows * tile_cols * devices)
    chunk = 18 * width // devices
    padded_chunk = -(-chunk // 8) * 8
    square = pltpu.VMEM((3 * width, 3 * width), jnp.bfloat16)
    z = [pltpu.VMEM((lay.z, width), jnp.float32)] * 3
    own = pltpu.VMEM((lay.own + 2 * MARGIN, width), jnp.float32)
    total = pltpu.VMEM((9 * width + 64, width), jnp.float32)
    flat_shape = jax.ShapeDtypeStruct((lay.flat, width), jnp.bfloat16)
    out_shape = jax.ShapeDtypeStruct((lay.out, width), jnp.float32)
    stats_shape = jax.ShapeDtypeStruct((devices, 8, width), jnp.float32)
    sent_shape = jax.ShapeDtypeStruct((devices, padded_chunk, width), jnp.bfloat16)
    half_shape = jax.ShapeDtypeStruct((devices // 2, padded_chunk, width), jnp.bfloat16)
    conv_flops = 18 * width * width * lay.out

    place = np.arange(devices * blocks)
    owner, slot = place // blocks % (devices // 2), place % blocks
    pairs = col_devices // 2
    places = np.zeros((8, devices * blocks), np.int32)
    places[0] = owner // pairs * block_rows + slot // block_cols
    places[1] = owner % pairs * 2 * block_cols + slot % block_cols
    places[2] = place // blocks < devices // 2
    near_shape = jax.ShapeDtypeStruct(((block_rows + 2) * 8, width), jnp.float32)
    pooled, valid = call(
        pool_kernel,
        (near_shape, near_shape),
        (mine, other, jnp.asarray(places), instance_weight),
        [pltpu.VMEM((devices * 8, 128), jnp.float32)],
        near=(block_rows, block_cols),
        coarse=(coarse_rows, band_cols),
    )
    channels = width_share * col_devices
    if direct:
        sources, base = (mine, other), mine
    else:
        even = my_col % 2 == 0
        sides = [jnp.where(even, mine, other), jnp.where(even, other, mine)]
        gathered = jnp.stack([side[:, :main_rows] for side in sides], 1).reshape(
            row_devices, col_devices, band_rows, band_cols, width_share
        )
        source = gathered.transpose(0, 2, 3, 1, 4).reshape(coarse_rows * band_cols, channels)
        sources = (source, source)
        column = lax.dynamic_index_in_dim(gathered, my_col, 1, keepdims=False)
        column = jnp.pad(
            column.reshape(coarse_rows, band_cols, width_share), ((1, 1), (0, 0), (0, 0))
        )
        base = lax.dynamic_slice_in_dim(column, my_row * band_rows, band_rows + 2, 0)
        base = base.reshape(-1, width_share)
    near_rows = band_rows + 4
    sent_hidden = call(
        hidden_kernel,
        jax.ShapeDtypeStruct((col_devices, near_rows * band_cols, width_share), jnp.bfloat16),
        (*sources, global_first),
        [
            pltpu.VMEM(((coarse_rows + 2) * band_cols, channels), jnp.bfloat16),
            pltpu.VMEM((coarse_rows, band_cols + 16, width_share), jnp.float32),
            pltpu.VMEM((coarse_rows + 4, band_cols, width_share), jnp.bfloat16),
        ],
        18 * coarse_rows * band_cols * channels * width_share,
        grid=grid,
        band=band,
        direct=direct,
    )
    near_hidden = to_all(sent_hidden, "cols")
    late_input, late_cotangent, top, bottom, _ = lax.optimization_barrier(
        (enhancer_input, output_cotangent, top, bottom, sent_hidden)
    )
    both = jnp.stack([late_input, late_cotangent])
    tall_last = jnp.concatenate([top[:, :, -RIM:], both[:, :, -RIM:], bottom[:, :, -RIM:]], 1)
    tall_first = jnp.concatenate([top[:, :, :RIM], both[:, :, :RIM], bottom[:, :, :RIM]], 1)
    left = lax.ppermute(tall_last, "cols", col_up)
    right = lax.ppermute(tall_first, "cols", col_down)
    strip = jnp.concatenate(
        [
            jnp.pad(right, ((0, 0), (1, 0), (0, 0), (0, 0))),
            jnp.pad(left, ((0, 0), (0, 1), (0, 0), (0, 0))),
        ],
        2,
    )
    act_grad = call(
        cot_kernel,
        out_shape,
        (output_cotangent, top[1], bottom[1], strip[1], enhancer_second),
        [pltpu.VMEM((lay.flat, width), jnp.bfloat16), square, *z],
        conv_flops,
        lay=lay,
    )

    sent_coarse = call(
        project_kernel,
        jax.ShapeDtypeStruct((col_devices, band_rows + 2, 8, width), jnp.float32),
        (near_hidden, global_second, base, project_weight),
        [
            pltpu.VMEM((near_rows * band_cols, channels), jnp.bfloat16),
            pltpu.VMEM((band_rows + 2, band_cols + 16, width_share), jnp.float32),
            pltpu.VMEM((coarse_rows + 2, band_cols, width_share), jnp.bfloat16),
            pltpu.VMEM((band_rows + 2, band_cols + 16, width), jnp.float32),
        ],
        18 * (band_rows + 2) * band_cols * channels * width_share,
        grid=grid,
        band=band,
        direct=direct,
    )
    near_coarse = to_all(sent_coarse, "cols")
    terms = (near_coarse, pooled.reshape(-1, 8, width), valid.reshape(-1, 8, width))

    mixed, first_act, stats = call(
        mixed_kernel,
        (flat_shape, out_shape, stats_shape),
        (enhancer_input, top[0], bottom[0], strip[0], *terms, enhancer_first),
        [square, pltpu.VMEM((block_rows + 2, 8, width), jnp.float32), *z],
        conv_flops,
        lay=lay,
    )
    stats = to_all(stats, BOTH)
    activated, normed_act, normed_grad, grad_stats = call(
        norm_kernel,
        (flat_shape, out_shape, out_shape, stats_shape),
        (first_act, stats, act_grad),
        lay=lay,
        grid=grid,
        pixel_total=pixel_total,
    )
    grad_stats = to_all(grad_stats, BOTH)
    enhanced, second_sent = call(
        second_kernel,
        (jax.ShapeDtypeStruct((tile_rows, tile_cols, width), jnp.bfloat16), half_shape),
        (activated, mixed, output_cotangent, enhancer_second),
        [square, *z, own, total],
        2 * conv_flops,
        lay=lay,
        chunk=chunk,
    )
    sent_both, kept = call(
        first_kernel,
        (sent_shape, jax.ShapeDtypeStruct((lay.kept, width), jnp.bfloat16)),
        (stats, grad_stats, normed_act, normed_grad, mixed, second_sent),
        [own, total],
        conv_flops,
        lay=lay,
        grid=grid,
        chunk=chunk,
        pixel_total=pixel_total,
    )
    part = to_all(sent_both, BOTH)
    rescale = 1.0 / math.sqrt(pixel_total)
    global_gradient = call(
        coarse_kernel,
        jax.ShapeDtypeStruct((blocks, width), jnp.float32),
        (kept, window_picks(lay), output_cotangent, enhancer_first),
        (),
        lay=lay,
    )
    share = call(share_kernel, half_shape, (part,), rescale=rescale)
    shares = from_all(share, row_devices, col_devices)
    whole_shape = jax.ShapeDtypeStruct((9 * width, width), jnp.float32)
    first_total, second_total = call(
        join_kernel, (whole_shape, whole_shape), shares, chunk=chunk, grid=grid
    )
    return (
        enhanced,
        first_total.reshape(3, 3, width, width),
        second_total.reshape(3, 3, width, width),
        global_gradient.reshape(block_rows, block_cols, width),
    )


def solution(mesh):
    return jax.shard_map(
        per_device,
        mesh=mesh,
        in_specs=(
            P("rows", None, "cols"),
            P(None, None, None, "cols"),
            P(None, None, None, "cols"),
            P(),
            P("rows", "cols", None),
            P("rows", "cols"),
            P(None, "rows", "cols"),
            P(),
            P(),
            P(),
            P("rows", "cols", None),
        ),
        out_specs=(P("rows", "cols", None), P(), P(), P("rows", "cols", None)),
        check_vma=False,
    )
```

```python
import math

import jax
import jax.numpy as jnp
import numpy as np
from jax import lax
from jax.experimental import pallas as pl
from jax.experimental.pallas import tpu as pltpu
from jax.sharding import PartitionSpec as P

INSTANCES = 256
UPSCALE = 16
BOTH = ("rows", "cols")

norm_eps = 1e-05


RIM = 8
MARGIN = 16
KERNEL_VMEM = 20 * 1024 * 1024


class Layout:
    def __init__(self, tile_rows, tile_cols):
        self.rows, self.cols = tile_rows, tile_cols
        self.wide = tile_cols + 2 * RIM
        self.flat = (tile_rows + 6) * self.wide + 2 * MARGIN
        self.out_rows = tile_rows + 3
        self.out = self.out_rows * self.wide
        self.z = self.out + 2 * MARGIN
        self.own = tile_rows * self.wide + 2 * MARGIN
        self.kept = -(-self.out // 128) * 128


def call(body, outs, ins, scratch=(), flops=0, far=None, late=(), far_out=(), **fixed):
    far = far or {}
    single = not isinstance(outs, tuple)
    outs = (outs,) if single else outs
    n_in, n_out, n_own = len(ins), len(outs), len(scratch)
    near = pl.BlockSpec(memory_space=pltpu.VMEM)
    hbm = pl.BlockSpec(memory_space=pltpu.MemorySpace.HBM)
    landing = [
        pltpu.VMEM(ins[i].shape[0 if k is None else 1 :], ins[i].dtype) for i, k in far.items()
    ]
    leaving = [pltpu.VMEM(outs[j].shape, outs[j].dtype) for j in far_out]

    def kernel(*refs):
        in_refs, out_refs = list(refs[:n_in]), list(refs[n_in : n_in + n_out])
        rest = refs[n_in + n_out :]
        own, rest = rest[:n_own], rest[n_own:]
        buffers, sems = rest[: len(far) + len(far_out)], rest[len(far) + len(far_out) :]
        copies = {}
        for slot, (i, k) in enumerate(far.items()):
            source = in_refs[i] if k is None else in_refs[i].at[k]
            copies[i] = pltpu.make_async_copy(source, buffers[slot], sems[slot])
            copies[i].start()
            in_refs[i] = buffers[slot]
        results = []
        for slot, j in enumerate(far_out, len(far)):
            results.append((buffers[slot], out_refs[j], sems[slot]))
            out_refs[j] = buffers[slot]
        for i, copy in copies.items():
            if i not in late:
                copy.wait()

        def arrive():
            for i in late:
                copies[i].wait()

        extra = {"arrive": arrive} if late else {}
        body(*in_refs, *out_refs, *own, **fixed, **extra)
        ends = [pltpu.make_async_copy(*triple) for triple in results]
        for copy in ends:
            copy.start()
        for copy in ends:
            copy.wait()

    result = pl.pallas_call(
        kernel,
        out_shape=outs,
        in_specs=[hbm if i in far else near for i in range(n_in)],
        out_specs=tuple(hbm if j in far_out else near for j in range(n_out)),
        scratch_shapes=[
            *scratch,
            *landing,
            *leaving,
            *[pltpu.SemaphoreType.DMA] * (len(landing) + len(leaving)),
        ],
        compiler_params=pltpu.CompilerParams(vmem_limit_bytes=KERNEL_VMEM),
        cost_estimate=pl.CostEstimate(flops=flops, bytes_accessed=4 << 20, transcendentals=0),
        name=body.__name__,
    )(*ins)
    return result[0] if single else result


def put_tiles(flat_ref, lay, main_ref, top_ref, bottom_ref, strip_ref):
    flat_ref[...] = jnp.zeros_like(flat_ref)
    for k in range(lay.rows + 5):
        base = MARGIN + k * lay.wide
        i = k - 3
        if i >= -2:
            if i < 0:
                row = top_ref[i + 2]
            elif i < lay.rows:
                row = main_ref[i]
            else:
                row = bottom_ref[i - lay.rows]
            flat_ref[base : base + lay.cols] = row
        flat_ref[base + lay.cols : base + lay.wide] = strip_ref[k]


def taps_matmul(flat_ref, square_ref, z_refs, lay, turned):
    count = z_refs[0].shape[0]
    chunks = 3
    step = count // chunks
    width = z_refs[0].shape[1]

    @pl.loop(0, chunks)
    def _(c):
        begin = pl.multiple_of(c * step, 16)
        parts = [flat_ref[pl.ds(begin + shift, step)] for shift in (0, lay.wide, 2 * lay.wide)]
        if turned:
            left = jnp.concatenate(parts[::-1], 1)
            result = lax.dot_general(
                left, square_ref[...], (((1,), (1,)), ((), ())), preferred_element_type=jnp.float32
            )
        else:
            left = jnp.concatenate(parts, 1)
            result = jnp.dot(left, square_ref[...], preferred_element_type=jnp.float32)
        for b in range(3):
            z_refs[b][pl.ds(begin, step)] = result[:, b * width : (b + 1) * width]


def put_square(square_ref, weight_ref, turned):
    width = weight_ref.shape[2]
    for a in range(3):
        for b in range(3):
            r, c = (b, a) if turned else (a, b)
            square_ref[r * width : (r + 1) * width, c * width : (c + 1) * width] = weight_ref[a, b]


def taken(z_refs, begin, count, turned):
    early, late = (2, 0) if turned else (0, 2)
    return (
        z_refs[early][pl.ds(begin + MARGIN - 1, count)]
        + z_refs[1][pl.ds(begin + MARGIN, count)]
        + z_refs[late][pl.ds(begin + MARGIN + 1, count)]
    )


def folded(value):
    return value.reshape(-1, 8, value.shape[-1]).sum(0)


def send_stats(out_ref, first, second):
    sums = jnp.concatenate(
        [jnp.sum(first, 0, keepdims=True), jnp.sum(second, 0, keepdims=True)], 0
    )
    out_ref[...] = jnp.zeros_like(out_ref)
    for d in range(out_ref.shape[0]):
        out_ref[d, 0:2] = sums


def cot_kernel(main, top, bottom, strip, weight, grad_out, flat, square, z0, z1, z2, *, lay):
    put_tiles(flat, lay, main, top, bottom, strip)
    put_square(square, weight, True)
    taps_matmul(flat, square, (z0, z1, z2), lay, True)

    @pl.loop(0, lay.out_rows)
    def _(r):
        begin = pl.multiple_of(r * lay.wide, 16)
        grad_out[pl.ds(begin, lay.wide)] = taken((z0, z1, z2), begin, lay.wide, True)


def mixed_kernel(
    main, top, bottom, strip, coarse, pooled, valid, weight, flat, act_out, stats, square, terms, z0,
    z1, z2, *, lay, arrive
):
    width = main.shape[2]
    flat[...] = jnp.zeros_like(flat)
    blocks = lay.cols // UPSCALE
    near = coarse[0]
    for c in range(1, coarse.shape[0]):
        near = near + coarse[c]
    terms[...] = near.astype(jnp.bfloat16).astype(jnp.float32) * valid[...] + pooled[...]
    for k in range(lay.rows + 5):
        base = MARGIN + k * lay.wide
        i = k - 3
        own, following = (i + UPSCALE) // UPSCALE, (i + 1 + UPSCALE) // UPSCALE

        def spread(block_row, block_col, rows):
            return jnp.broadcast_to(
                terms[block_row, block_col : block_col + 1], (rows, width)
            )

        if i >= -2:
            if i < 0:
                row = top[i + 2]
            elif i < lay.rows:
                row = main[i]
            else:
                row = bottom[i - lay.rows]
            added = jnp.concatenate([spread(own, b + 2, UPSCALE) for b in range(blocks)], 0)
            flat[base : base + lay.cols] = (row.astype(jnp.float32) + added).astype(jnp.bfloat16)
        zero = jnp.zeros((RIM, width), jnp.float32)
        right = spread(own, blocks + 2, RIM) if i >= -2 else zero
        left = spread(following, 1, RIM) if i + 1 < lay.rows + 2 else zero
        flat[base + lay.cols : base + lay.wide] = (
            strip[k].astype(jnp.float32) + jnp.concatenate([right, left], 0)
        ).astype(jnp.bfloat16)
    arrive()
    put_square(square, weight, False)
    taps_matmul(flat, square, (z0, z1, z2), lay, False)

    def step(r, sums):
        begin = pl.multiple_of(r * lay.wide, 16)
        value = taken((z0, z1, z2), begin, lay.wide, False)
        act_out[pl.ds(begin, lay.wide)] = value
        mine = ((r >= 2) & (r < lay.rows + 2)).astype(jnp.float32)
        own_value = value[: lay.cols] * mine
        return sums[0] + folded(own_value), sums[1] + folded(own_value * own_value)

    zero = jnp.zeros((8, width), jnp.float32)
    sums = lax.fori_loop(0, lay.out_rows, step, (zero, zero))
    send_stats(stats, *sums)


def act_moments(stats, pixel_total):
    sums = jnp.sum(stats[...], 0)
    mean = sums[0:1] / pixel_total
    return mean, lax.rsqrt(sums[1:2] / pixel_total - mean * mean + norm_eps)


def inside_masks(lay, width, row_devices, col_devices):
    my_row, my_col = lax.axis_index("rows"), lax.axis_index("cols")
    column = lax.broadcasted_iota(jnp.int32, (lay.wide, width), 0)
    has_right = (my_col < col_devices - 1).astype(jnp.float32)
    has_left = (my_col > 0).astype(jnp.float32)
    near = jnp.where(
        column < lay.cols, 1.0, jnp.where(column < lay.cols + RIM, has_right, 0.0)
    )
    following = jnp.where(column >= lay.cols + RIM, has_left, 0.0)

    def row_inside(i):
        row = my_row * lay.rows + i
        return ((row >= 0) & (row < lay.rows * row_devices)).astype(jnp.float32)

    return lambda r: near * row_inside(r - 2) + following * row_inside(r - 1)


def norm_kernel(
    act, stats, act_grad, activated, grad_out, grad_stats, *, lay, grid, pixel_total
):
    width = act.shape[1]
    mean, inverse = act_moments(stats, pixel_total)
    mask = inside_masks(lay, width, *grid)
    activated[...] = jnp.zeros_like(activated)

    def step(r, sums):
        begin = pl.multiple_of(r * lay.wide, 16)
        normed = (act[pl.ds(begin, lay.wide)] - mean) * inverse
        gate = 1.0 / (1.0 + jnp.exp(-normed))
        inside = mask(r)
        activated[pl.ds(pl.multiple_of(begin + MARGIN + lay.wide, 16), lay.wide)] = (
            normed * gate * inside
        ).astype(jnp.bfloat16)
        grad = act_grad[pl.ds(begin, lay.wide)] * gate * (1.0 + normed * (1.0 - gate))
        grad_out[pl.ds(begin, lay.wide)] = grad
        mine = ((r >= 2) & (r < lay.rows + 2)).astype(jnp.float32)
        own_grad = grad[: lay.cols] * mine
        return sums[0] + folded(own_grad), sums[1] + folded(own_grad * normed[: lay.cols])

    zero = jnp.zeros((8, width), jnp.float32)
    sums = lax.fori_loop(0, lay.out_rows, step, (zero, zero))
    send_stats(grad_stats, *sums)


def weight_matmul(flat_ref, own_ref, total_ref, sent_ref, lay, chunk):
    count = lay.own
    first = MARGIN + 3 * lay.wide - MARGIN
    chunks = 3
    step = count // chunks
    width = own_ref.shape[1]
    total = None
    for c in range(chunks):
        begin = c * step
        left = jnp.concatenate(
            [
                flat_ref[first + begin + a * lay.wide : first + begin + a * lay.wide + step]
                for a in (-1, 0, 1)
            ],
            1,
        )
        right = jnp.concatenate(
            [
                own_ref[MARGIN + begin - b : MARGIN + begin - b + step].astype(jnp.bfloat16)
                for b in (-1, 0, 1)
            ],
            1,
        )
        part = lax.dot_general(
            left, right, (((0,), (0,)), ((), ())), preferred_element_type=jnp.float32
        )
        total = part if total is None else total + part
    for a in range(3):
        for b in range(3):
            total_ref[(a * 3 + b) * width : (a * 3 + b + 1) * width] = total[
                a * width : (a + 1) * width, b * width : (b + 1) * width
            ]
    padded = sent_ref.shape[1]
    for d in range(9 * width // chunk):
        sent_ref[d] = total_ref[d * chunk : d * chunk + padded].astype(jnp.bfloat16)


def second_kernel(
    activated, mixed, main, weight, enhanced, sent, square, z0, z1, z2, own, total, *, lay, chunk,
    arrive
):
    put_square(square, weight, False)
    taps_matmul(activated, square, (z0, z1, z2), lay, False)
    arrive()

    @pl.loop(0, lay.rows)
    def _(i):
        begin = pl.multiple_of((i + 2) * lay.wide, 16)
        value = taken((z0, z1, z2), begin, lay.cols, False)
        place = pl.multiple_of((i + 3) * lay.wide + MARGIN, 16)
        enhanced[i] = (mixed[pl.ds(place, lay.cols)].astype(jnp.float32) + value).astype(
            jnp.bfloat16
        )

    own[...] = jnp.zeros_like(own)

    @pl.loop(0, lay.rows)
    def _(i):
        place = pl.multiple_of(i * lay.wide + 2 * MARGIN, 16)
        own[pl.ds(place, lay.cols)] = main[i].astype(jnp.float32)

    weight_matmul(activated, own, total, sent, lay, chunk)


def first_kernel(
    stats, grad_stats, act, grad_ref, mixed, second, sent, kept, own, total, *, lay, grid,
    chunk, pixel_total, arrive
):
    width = act.shape[1]
    mean, inverse = act_moments(stats, pixel_total)
    sums = jnp.sum(grad_stats[...], 0)
    grad_mean, cross_mean = sums[0:1] / pixel_total, sums[1:2] / pixel_total
    mask = inside_masks(lay, width, *grid)
    own[...] = jnp.zeros_like(own)
    kept[...] = jnp.zeros_like(kept)

    @pl.loop(0, lay.out_rows)
    def _(r):
        begin = pl.multiple_of(r * lay.wide, 16)
        value = inverse * (
            grad_ref[pl.ds(begin, lay.wide)]
            - grad_mean
            - (act[pl.ds(begin, lay.wide)] - mean) * inverse * cross_mean
        )
        value = (value * mask(r)).astype(jnp.bfloat16)
        kept[pl.ds(begin, lay.wide)] = value

        @pl.when((r >= 2) & (r < lay.rows + 2))
        def _():
            place = pl.multiple_of((r - 2) * lay.wide + 2 * MARGIN, 16)
            own[pl.ds(place, lay.cols)] = value[: lay.cols].astype(jnp.float32)

    arrive()
    weight_matmul(mixed, own, total, sent, lay, chunk)
    for d in range(second.shape[0]):
        sent[second.shape[0] + d] = second[d]


def coarse_kernel(kept, picked, main, weight, out, *, lay):
    width = weight.shape[2]
    windows = jnp.dot(picked[...], kept[...], preferred_element_type=jnp.float32)
    block_rows, block_cols = lay.rows // UPSCALE, lay.cols // UPSCALE
    blocks = block_rows * block_cols
    summed = jnp.zeros((blocks, width), jnp.float32)
    for tap in range(9):
        summed = summed + lax.dot_general(
            windows[tap * blocks : (tap + 1) * blocks],
            weight[tap // 3, tap % 3].astype(jnp.float32),
            (((1,), (1,)), ((), ())),
            precision=lax.Precision.HIGHEST,
            preferred_element_type=jnp.float32,
        )
    for bi in range(block_rows):
        rows = jnp.zeros((lay.cols, width), jnp.float32)
        for i in range(UPSCALE):
            rows = rows + main[bi * UPSCALE + i].astype(jnp.float32)
        for bj in range(block_cols):
            k = bi * block_cols + bj
            cot = jnp.sum(rows[bj * UPSCALE : (bj + 1) * UPSCALE], 0, keepdims=True)
            out[k : k + 1] = (cot + summed[k : k + 1]) / UPSCALE


def share_kernel(received, sent, *, rescale):
    total = received[0].astype(jnp.float32)
    for d in range(1, received.shape[0]):
        total = total + received[d].astype(jnp.float32)
    total = (total * rescale).astype(jnp.bfloat16)
    for d in range(sent.shape[0]):
        sent[d] = total


def join_kernel(mine, other, first, second, *, chunk, grid):
    row_devices, col_devices = grid
    half, pairs = row_devices * col_devices // 2, col_devices // 2
    core = lax.axis_index("cols") & 1
    for k in range(2):

        @pl.when(core == k)
        def _():
            for source, side in ((mine, k), (other, 1 - k)):
                for d in range(half):
                    owner = d // pairs * col_devices + d % pairs * 2 + side
                    out = first if owner < half else second
                    begin = owner % half * chunk
                    out[begin : begin + chunk] = source[d].astype(jnp.float32)[:chunk]


def window_picks(lay):
    place = np.arange(lay.kept)
    slot, column = place // lay.wide + 1, place % lay.wide
    behind = column >= lay.cols + RIM
    i = np.where(behind, slot - 2, slot - 3)
    j = np.where(behind, column - lay.wide, column)
    rows = []
    for a in range(3):
        for b in range(3):
            y, x = i + a - 1, j + b - 1
            for bi in range(lay.rows // UPSCALE):
                for bj in range(lay.cols // UPSCALE):
                    rows.append((y // UPSCALE == bi) & (x // UPSCALE == bj) & (place < lay.out))
    return jnp.asarray(np.stack(rows), jnp.bfloat16)


def to_all(payload, axis):
    return lax.all_to_all(payload, axis, 0, 0)


def among_cores(payload, row_devices, col_devices):
    groups = [
        [r * col_devices + 2 * h + k for r in range(row_devices) for h in range(col_devices // 2)]
        for k in range(2)
    ]
    return lax.all_to_all(payload, BOTH, 0, 0, axis_index_groups=groups)


def core_swap(array, col_devices):
    return lax.ppermute(array, "cols", [(c, c ^ 1) for c in range(col_devices)])


def pieces(array):
    high = array.astype(jnp.bfloat16)
    rest = array - high.astype(jnp.float32)
    middle = rest.astype(jnp.bfloat16)
    return high, middle, (rest - middle.astype(jnp.float32)).astype(jnp.bfloat16)


def lane_roll(value, shift):
    return pltpu.roll(value, shift % value.shape[1], 1)


def pack_kernel(features, labels, band, sent, sums):
    encoder_width, tile_rows, tile_cols = features.shape
    block_rows, block_cols = tile_rows // UPSCALE, tile_cols // UPSCALE
    blocks = block_rows * block_cols
    sums[...] = jnp.zeros_like(sums)
    slot = lax.broadcasted_iota(jnp.int32, (blocks, tile_cols), 0)
    column = lax.broadcasted_iota(jnp.int32, (blocks, tile_cols), 1)
    total = jnp.zeros((blocks, 128), jnp.float32)
    for r in range(block_rows):
        sums[0:encoder_width] = jnp.sum(features[:, r * UPSCALE : (r + 1) * UPSCALE], 1)
        sums[encoder_width : encoder_width + 1] = (
            labels[r * UPSCALE : r * UPSCALE + 1].astype(jnp.float32) / UPSCALE
        )
        low = (slot - r * block_cols) * UPSCALE
        picked = ((column >= low) & (column < low + UPSCALE)).astype(jnp.float32)
        total = total + lax.dot_general(
            picked,
            sums[...],
            (((1,), (1,)), ((), ())),
            precision=lax.Precision.HIGHEST,
            preferred_element_type=jnp.float32,
        )
    high, middle, low = pieces(total)
    packed = (
        high.astype(jnp.float32)
        + lane_roll(middle.astype(jnp.float32), 32)
        + lane_roll(low.astype(jnp.float32), 64)
    )
    value = jnp.concatenate([band[...].astype(jnp.float32), packed], 0).astype(jnp.bfloat16)
    for d in range(sent.shape[0]):
        sent[d] = value


def pool_kernel(mine_ref, other_ref, places, weight, pooled, valid, table, *, near, coarse):
    block_rows, block_cols = near
    coarse_rows, coarse_cols = coarse
    encoder_width = weight.shape[0]
    half, rows, _ = mine_ref.shape
    devices = 2 * half
    lane = lax.broadcasted_iota(jnp.int32, (8, 128), 1)
    for d in range(devices):
        part = mine_ref[d] if d < half else other_ref[d - half]
        packed = part.astype(jnp.float32)[rows - 8 :]
        value = packed + lane_roll(packed, -32) + lane_roll(packed, -64)
        table[d * 8 : (d + 1) * 8] = jnp.where(lane <= encoder_width, value, 0.0)
    exact = dict(precision=lax.Precision.HIGHEST, preferred_element_type=jnp.float32)
    row0 = lax.axis_index("rows") * block_rows - 1
    col0 = lax.axis_index("cols") * block_cols - 2

    def position(shape):
        q = lax.broadcasted_iota(jnp.int32, shape, 0)
        return row0 + (q >> 3), col0 + (q & 7)

    count = pooled.shape[0]
    row, col = position((count, devices * 8))
    core = lax.axis_index("cols") & 1
    column = places[1:2] + block_cols * jnp.where(places[2:3] == 1, core, 1 - core)
    chosen = ((row == places[0:1]) & (col == column)).astype(jnp.float32)
    mine = jnp.dot(chosen, table[...], **exact)[:, encoder_width : encoder_width + 1]
    pick = (lane == encoder_width).astype(jnp.float32)
    every = lax.dot_general(pick, table[...], (((1,), (1,)), ((), ())), **exact)[0:1]
    same = (mine == every).astype(jnp.float32)
    sums = jnp.dot(same, table[...], **exact)
    members = jnp.sum(same, 1, keepdims=True) * float(UPSCALE * UPSCALE)
    averages = sums / jnp.maximum(members, 1.0)
    result = jnp.dot(averages[:, :encoder_width], weight[...], **exact)
    row, col = position(pooled.shape)
    inside = (row >= 0) & (row < coarse_rows) & (col >= 0) & (col < coarse_cols)
    pooled[...] = jnp.where(inside, result, 0.0)
    valid[...] = inside.astype(jnp.float32)


def channel_conv(rows_ref, weight, shifted, out_rows, cols):
    width = weight.shape[3]
    count = out_rows * cols
    sums = None
    for a in range(3):
        left = rows_ref[a * cols : a * cols + count]
        if width % 128:
            part = [
                jnp.dot(left, weight[a, b], preferred_element_type=jnp.float32) for b in range(3)
            ]
        else:
            right = jnp.concatenate([weight[a, b] for b in range(3)], 1)
            part = jnp.dot(left, right, preferred_element_type=jnp.float32)
            part = [part[:, b * width : (b + 1) * width] for b in range(3)]
        sums = part if sums is None else [s + p for s, p in zip(sums, part)]
    shifted[...] = jnp.zeros_like(shifted)
    total = sums[1]
    for b in (0, 2):
        shifted[:, 8 : 8 + cols] = sums[b].reshape(out_rows, cols, width)
        total = total + shifted[:, 7 + b : 7 + b + cols].reshape(count, width)
    return total


def hidden_kernel(mine, other, weight, sent, rows_ref, shifted, kept, *, grid, band, direct, arrive):
    row_devices, col_devices = grid
    band_rows, cols = band
    coarse_rows = row_devices * band_rows
    width = weight.shape[3]
    rows_ref[...] = jnp.zeros_like(rows_ref)
    if direct:
        pairs = col_devices // 2
        core = lax.axis_index("cols") & 1
        for source, side in ((mine, core), (other, 1 - core)):
            for d in range(row_devices * pairs):
                begin = (1 + d // pairs * band_rows) * cols
                lanes = pl.multiple_of((d % pairs * 2 + side) * width, width)
                rows_ref[begin : begin + band_rows * cols, pl.ds(lanes, width)] = source[
                    d, : band_rows * cols
                ]
    else:
        rows_ref[cols : cols + coarse_rows * cols] = mine[...]
    arrive()
    raw = channel_conv(rows_ref, weight, shifted, coarse_rows, cols)
    pixels = coarse_rows * cols
    mean = jnp.sum(raw, 0, keepdims=True) / pixels
    variance = jnp.sum(raw * raw, 0, keepdims=True) / pixels - mean * mean
    hidden = jnp.maximum((raw - mean) * lax.rsqrt(variance + norm_eps), 0.0)
    kept[...] = jnp.zeros_like(kept)
    kept[2 : 2 + coarse_rows] = hidden.astype(jnp.bfloat16).reshape(coarse_rows, cols, width)
    near = kept[pl.ds(lax.axis_index("rows") * band_rows, band_rows + 4)]
    near = near.reshape((band_rows + 4) * cols, width)
    for d in range(sent.shape[0]):
        sent[d] = near


def project_kernel(
    received, weight, source, project, sent, rows_ref, shifted, residual, spread, *, grid, band,
    direct, arrive
):
    row_devices, col_devices = grid
    band_rows, cols = band
    width = weight.shape[3]
    my_col = lax.axis_index("cols")
    for c in range(col_devices):
        rows_ref[:, c * width : (c + 1) * width] = received[c]
    arrive()
    raw = channel_conv(rows_ref, weight, shifted, band_rows + 2, cols)
    count = (band_rows + 2) * cols
    if direct:
        residual[...] = jnp.zeros_like(residual)
        for r in range(row_devices):
            piece = source[r * (col_devices // 2) + (my_col >> 1), : band_rows * cols]
            residual[1 + r * band_rows : 1 + (r + 1) * band_rows] = piece.reshape(
                band_rows, cols, width
            )
        base = residual[pl.ds(lax.axis_index("rows") * band_rows, band_rows + 2)]
        base = base.reshape(count, width)
    else:
        base = source[...]
    result = (base.astype(jnp.float32) + raw).astype(jnp.bfloat16)
    rows = project[pl.ds(pl.multiple_of(my_col * width, width), width)]
    partial = jnp.dot(result, rows, preferred_element_type=jnp.float32)
    spread[...] = jnp.zeros_like(spread)
    spread[:, 8 : 8 + cols] = partial.reshape(band_rows + 2, cols, partial.shape[1])
    step = cols // col_devices
    for j in range(col_devices):
        sent[j] = spread[:, 6 + j * step : 6 + j * step + sent.shape[2]]


def per_device(
    global_in,
    global_first,
    global_second,
    project_weight,
    enhancer_input,
    instance_map,
    encoder_features,
    instance_weight,
    enhancer_first,
    enhancer_second,
    output_cotangent,
):
    row_devices, col_devices = lax.axis_size("rows"), lax.axis_size("cols")
    devices = row_devices * col_devices
    my_row, my_col = lax.axis_index("rows"), lax.axis_index("cols")
    band_rows, band_cols, width_share = global_in.shape
    tile_rows, tile_cols, local_width = enhancer_input.shape
    coarse_rows = band_rows * row_devices
    block_rows = tile_rows // UPSCALE
    block_cols = tile_cols // UPSCALE
    blocks = block_rows * block_cols
    encoder_width = encoder_features.shape[0]

    lay = Layout(tile_rows, tile_cols)
    width = local_width
    grid = (row_devices, col_devices)
    band = (band_rows, band_cols)
    direct = width_share == 128
    main = global_in.reshape(-1, 128)
    main_rows = main.shape[0]
    sent_input = call(
        pack_kernel,
        jax.ShapeDtypeStruct((devices // 2, main_rows + 8, 128), jnp.bfloat16),
        (encoder_features, instance_map, main),
        [pltpu.VMEM((128, tile_cols), jnp.float32)],
        far={0: None, 1: None, 2: None},
    )
    mine = among_cores(sent_input, row_devices, col_devices)
    late_input, late_cotangent, _ = lax.optimization_barrier(
        (enhancer_input, output_cotangent, sent_input)
    )
    tops = jnp.stack([late_input[-2:], late_cotangent[-2:]])
    bottoms = jnp.stack([late_input[:2], late_cotangent[:2]])

    row_up = [(i, i + 1) for i in range(row_devices - 1)]
    row_down = [(j, i) for i, j in row_up]
    col_up = [(i, i + 1) for i in range(col_devices - 1)]
    col_down = [(j, i) for i, j in col_up]
    top = lax.ppermute(tops, "rows", row_up)
    bottom = lax.ppermute(bottoms, "rows", row_down)
    both = jnp.stack([late_input, late_cotangent])
    tall_last = jnp.concatenate([top[:, :, -RIM:], both[:, :, -RIM:], bottom[:, :, -RIM:]], 1)
    tall_first = jnp.concatenate([top[:, :, :RIM], both[:, :, :RIM], bottom[:, :, :RIM]], 1)
    mine, tall_last, tall_first = lax.optimization_barrier((mine, tall_last, tall_first))
    other = core_swap(mine, col_devices)
    pixel_total = float(tile_rows * tile_cols * devices)
    chunk = 18 * width // devices
    padded_chunk = -(-chunk // 8) * 8
    square = pltpu.VMEM((3 * width, 3 * width), jnp.bfloat16)
    z = [pltpu.VMEM((lay.z, width), jnp.float32)] * 3
    own = pltpu.VMEM((lay.own + 2 * MARGIN, width), jnp.float32)
    total = pltpu.VMEM((9 * width + 64, width), jnp.float32)
    flat_shape = jax.ShapeDtypeStruct((lay.flat, width), jnp.bfloat16)
    out_shape = jax.ShapeDtypeStruct((lay.out, width), jnp.float32)
    stats_shape = jax.ShapeDtypeStruct((devices, 8, width), jnp.float32)
    sent_shape = jax.ShapeDtypeStruct((devices, padded_chunk, width), jnp.bfloat16)
    half_shape = jax.ShapeDtypeStruct((devices // 2, padded_chunk, width), jnp.bfloat16)
    conv_flops = 18 * width * width * lay.out

    place = np.arange(devices * blocks)
    owner, slot = place // blocks % (devices // 2), place % blocks
    pairs = col_devices // 2
    places = np.zeros((8, devices * blocks), np.int32)
    places[0] = owner // pairs * block_rows + slot // block_cols
    places[1] = owner % pairs * 2 * block_cols + slot % block_cols
    places[2] = place // blocks < devices // 2
    near_shape = jax.ShapeDtypeStruct(((block_rows + 2) * 8, width), jnp.float32)
    pooled, valid = call(
        pool_kernel,
        (near_shape, near_shape),
        (mine, other, jnp.asarray(places), instance_weight),
        [pltpu.VMEM((devices * 8, 128), jnp.float32)],
        near=(block_rows, block_cols),
        coarse=(coarse_rows, band_cols),
    )
    channels = width_share * col_devices
    if direct:
        sources, base = (mine, other), mine
    else:
        even = my_col % 2 == 0
        sides = [jnp.where(even, mine, other), jnp.where(even, other, mine)]
        gathered = jnp.stack([side[:, :main_rows] for side in sides], 1).reshape(
            row_devices, col_devices, band_rows, band_cols, width_share
        )
        source = gathered.transpose(0, 2, 3, 1, 4).reshape(coarse_rows * band_cols, channels)
        sources = (source, source)
        column = lax.dynamic_index_in_dim(gathered, my_col, 1, keepdims=False)
        column = jnp.pad(
            column.reshape(coarse_rows, band_cols, width_share), ((1, 1), (0, 0), (0, 0))
        )
        base = lax.dynamic_slice_in_dim(column, my_row * band_rows, band_rows + 2, 0)
        base = base.reshape(-1, width_share)
    near_rows = band_rows + 4
    sent_hidden = call(
        hidden_kernel,
        jax.ShapeDtypeStruct((col_devices, near_rows * band_cols, width_share), jnp.bfloat16),
        (*sources, global_first),
        [
            pltpu.VMEM(((coarse_rows + 2) * band_cols, channels), jnp.bfloat16),
            pltpu.VMEM((coarse_rows, band_cols + 16, width_share), jnp.float32),
            pltpu.VMEM((coarse_rows + 4, band_cols, width_share), jnp.bfloat16),
        ],
        18 * coarse_rows * band_cols * channels * width_share,
        far={2: None},
        late=(2,),
        far_out=(0,),
        grid=grid,
        band=band,
        direct=direct,
    )
    near_hidden = to_all(sent_hidden, "cols")
    tall_last, tall_first, _ = lax.optimization_barrier((tall_last, tall_first, sent_hidden))
    left = lax.ppermute(tall_last, "cols", col_up)
    right = lax.ppermute(tall_first, "cols", col_down)
    strip = jnp.concatenate(
        [
            jnp.pad(right, ((0, 0), (1, 0), (0, 0), (0, 0))),
            jnp.pad(left, ((0, 0), (0, 1), (0, 0), (0, 0))),
        ],
        2,
    )
    act_grad = call(
        cot_kernel,
        out_shape,
        (output_cotangent, top, bottom, strip, enhancer_second),
        [pltpu.VMEM((lay.flat, width), jnp.bfloat16), square, *z],
        conv_flops,
        far={0: None, 1: 1, 2: 1, 3: 1, 4: None},
        far_out=(0,),
        lay=lay,
    )

    sent_coarse = call(
        project_kernel,
        jax.ShapeDtypeStruct((col_devices, band_rows + 2, 8, width), jnp.float32),
        (near_hidden, global_second, base, project_weight),
        [
            pltpu.VMEM((near_rows * band_cols, channels), jnp.bfloat16),
            pltpu.VMEM((band_rows + 2, band_cols + 16, width_share), jnp.float32),
            pltpu.VMEM((coarse_rows + 2, band_cols, width_share), jnp.bfloat16),
            pltpu.VMEM((band_rows + 2, band_cols + 16, width), jnp.float32),
        ],
        18 * (band_rows + 2) * band_cols * channels * width_share,
        far={1: None, 2: None, 3: None},
        late=(1, 2, 3),
        far_out=(0,),
        grid=grid,
        band=band,
        direct=direct,
    )
    near_coarse = to_all(sent_coarse, "cols")
    terms = (near_coarse, pooled.reshape(-1, 8, width), valid.reshape(-1, 8, width))

    mixed, first_act, stats = call(
        mixed_kernel,
        (flat_shape, out_shape, stats_shape),
        (enhancer_input, top, bottom, strip, *terms, enhancer_first),
        [square, pltpu.VMEM((block_rows + 2, 8, width), jnp.float32), *z],
        conv_flops,
        far={0: None, 1: 0, 2: 0, 3: 0, 5: None, 6: None, 7: None},
        late=(7,),
        far_out=(0, 1, 2),
        lay=lay,
    )
    stats = to_all(stats, BOTH)
    activated, normed_grad, grad_stats = call(
        norm_kernel,
        (flat_shape, out_shape, stats_shape),
        (first_act, stats, act_grad),
        far={0: None, 2: None},
        far_out=(0, 1, 2),
        lay=lay,
        grid=grid,
        pixel_total=pixel_total,
    )
    grad_stats = to_all(grad_stats, BOTH)
    enhanced, second_sent = call(
        second_kernel,
        (jax.ShapeDtypeStruct((tile_rows, tile_cols, width), jnp.bfloat16), half_shape),
        (activated, mixed, output_cotangent, enhancer_second),
        [square, *z, own, total],
        2 * conv_flops,
        far={0: None, 1: None, 2: None, 3: None},
        late=(1, 2),
        lay=lay,
        chunk=chunk,
    )
    sent_both, kept = call(
        first_kernel,
        (sent_shape, jax.ShapeDtypeStruct((lay.kept, width), jnp.bfloat16)),
        (stats, grad_stats, first_act, normed_grad, mixed, second_sent),
        [own, total],
        conv_flops,
        far={2: None, 3: None, 4: None},
        late=(4,),
        lay=lay,
        grid=grid,
        chunk=chunk,
        pixel_total=pixel_total,
    )
    part = to_all(sent_both, BOTH)
    rescale = 1.0 / math.sqrt(pixel_total)
    global_gradient = call(
        coarse_kernel,
        jax.ShapeDtypeStruct((blocks, width), jnp.float32),
        (kept, window_picks(lay), output_cotangent, enhancer_first),
        (),
        lay=lay,
    )
    part, global_gradient = lax.optimization_barrier((part, global_gradient))
    share = call(share_kernel, half_shape, (part,), rescale=rescale)
    share = among_cores(share, row_devices, col_devices)
    shares = (share, core_swap(share, col_devices))
    whole_shape = jax.ShapeDtypeStruct((9 * width, width), jnp.float32)
    first_total, second_total = call(
        join_kernel, (whole_shape, whole_shape), shares, chunk=chunk, grid=grid
    )
    return (
        enhanced,
        first_total.reshape(3, 3, width, width),
        second_total.reshape(3, 3, width, width),
        global_gradient.reshape(block_rows, block_cols, width),
    )


def solution(mesh):
    return jax.shard_map(
        per_device,
        mesh=mesh,
        in_specs=(
            P("rows", None, "cols"),
            P(None, None, None, "cols"),
            P(None, None, None, "cols"),
            P(),
            P("rows", "cols", None),
            P("rows", "cols"),
            P(None, "rows", "cols"),
            P(),
            P(),
            P(),
            P("rows", "cols", None),
        ),
        out_specs=(P("rows", "cols", None), P(), P(), P("rows", "cols", None)),
        check_vma=False,
    )
```

```python
import math

import jax
import jax.numpy as jnp
import numpy as np
from jax import lax
from jax.experimental import pallas as pl
from jax.experimental.pallas import tpu as pltpu
from jax.sharding import PartitionSpec as P

INSTANCES = 256
UPSCALE = 16
BOTH = ("rows", "cols")

norm_eps = 1e-05


RIM = 8
MARGIN = 16
KERNEL_VMEM = 62 * 1024 * 1024


class Layout:
    def __init__(self, tile_rows, tile_cols):
        self.rows, self.cols = tile_rows, tile_cols
        self.wide = tile_cols + 2 * RIM
        self.flat = (tile_rows + 6) * self.wide + 2 * MARGIN
        self.out_rows = tile_rows + 3
        self.out = self.out_rows * self.wide
        self.z = self.out + 2 * MARGIN
        self.own = tile_rows * self.wide + 2 * MARGIN
        self.kept = -(-self.out // 128) * 128


def call(body, outs, ins, scratch=(), flops=0, far=None, late=(), far_out=(), **fixed):
    far = far or {}
    single = not isinstance(outs, tuple)
    outs = (outs,) if single else outs
    n_in, n_out, n_own = len(ins), len(outs), len(scratch)
    near = pl.BlockSpec(memory_space=pltpu.VMEM)
    hbm = pl.BlockSpec(memory_space=pltpu.MemorySpace.HBM)
    landing = [
        pltpu.VMEM(ins[i].shape[0 if k is None else 1 :], ins[i].dtype) for i, k in far.items()
    ]
    leaving = [pltpu.VMEM(outs[j].shape, outs[j].dtype) for j in far_out]

    def kernel(*refs):
        in_refs, out_refs = list(refs[:n_in]), list(refs[n_in : n_in + n_out])
        rest = refs[n_in + n_out :]
        own, rest = rest[:n_own], rest[n_own:]
        buffers, sems = rest[: len(far) + len(far_out)], rest[len(far) + len(far_out) :]
        copies = {}
        for slot, (i, k) in enumerate(far.items()):
            source = in_refs[i] if k is None else in_refs[i].at[k]
            copies[i] = pltpu.make_async_copy(source, buffers[slot], sems[slot])
            copies[i].start()
            in_refs[i] = buffers[slot]
        results = []
        for slot, j in enumerate(far_out, len(far)):
            results.append((buffers[slot], out_refs[j], sems[slot]))
            out_refs[j] = buffers[slot]
        for i, copy in copies.items():
            if i not in late:
                copy.wait()

        def arrive():
            for i in late:
                copies[i].wait()

        extra = {"arrive": arrive} if late else {}
        body(*in_refs, *out_refs, *own, **fixed, **extra)
        ends = [pltpu.make_async_copy(*triple) for triple in results]
        for copy in ends:
            copy.start()
        for copy in ends:
            copy.wait()

    result = pl.pallas_call(
        kernel,
        out_shape=outs,
        in_specs=[hbm if i in far else near for i in range(n_in)],
        out_specs=tuple(hbm if j in far_out else near for j in range(n_out)),
        scratch_shapes=[
            *scratch,
            *landing,
            *leaving,
            *[pltpu.SemaphoreType.DMA] * (len(landing) + len(leaving)),
        ],
        compiler_params=pltpu.CompilerParams(vmem_limit_bytes=KERNEL_VMEM),
        cost_estimate=pl.CostEstimate(flops=flops, bytes_accessed=4 << 20, transcendentals=0),
        name=body.__name__,
    )(*ins)
    return result[0] if single else result


def put_tiles(flat_ref, lay, main_ref, top_ref, bottom_ref, strip_ref):
    flat_ref[...] = jnp.zeros_like(flat_ref)
    for k in range(lay.rows + 5):
        base = MARGIN + k * lay.wide
        i = k - 3
        if i >= -2:
            if i < 0:
                row = top_ref[i + 2]
            elif i < lay.rows:
                row = main_ref[i]
            else:
                row = bottom_ref[i - lay.rows]
            flat_ref[base : base + lay.cols] = row
        flat_ref[base + lay.cols : base + lay.wide] = strip_ref[k]


def taps_matmul(flat_ref, square_ref, z_refs, lay, turned):
    count = z_refs[0].shape[0]
    chunks = 3
    step = count // chunks
    width = z_refs[0].shape[1]

    @pl.loop(0, chunks)
    def _(c):
        begin = pl.multiple_of(c * step, 16)
        parts = [flat_ref[pl.ds(begin + shift, step)] for shift in (0, lay.wide, 2 * lay.wide)]
        if turned:
            left = jnp.concatenate(parts[::-1], 1)
            result = lax.dot_general(
                left, square_ref[...], (((1,), (1,)), ((), ())), preferred_element_type=jnp.float32
            )
        else:
            left = jnp.concatenate(parts, 1)
            result = jnp.dot(left, square_ref[...], preferred_element_type=jnp.float32)
        for b in range(3):
            z_refs[b][pl.ds(begin, step)] = result[:, b * width : (b + 1) * width]


def put_square(square_ref, weight_ref, turned):
    width = weight_ref.shape[2]
    for a in range(3):
        for b in range(3):
            r, c = (b, a) if turned else (a, b)
            square_ref[r * width : (r + 1) * width, c * width : (c + 1) * width] = weight_ref[a, b]


def taken(z_refs, begin, count, turned):
    early, late = (2, 0) if turned else (0, 2)
    return (
        z_refs[early][pl.ds(begin + MARGIN - 1, count)]
        + z_refs[1][pl.ds(begin + MARGIN, count)]
        + z_refs[late][pl.ds(begin + MARGIN + 1, count)]
    )


def folded(value):
    return value.reshape(-1, 8, value.shape[-1]).sum(0)


def send_stats(out_ref, first, second):
    sums = jnp.concatenate(
        [jnp.sum(first, 0, keepdims=True), jnp.sum(second, 0, keepdims=True)], 0
    )
    out_ref[...] = jnp.zeros_like(out_ref)
    for d in range(out_ref.shape[0]):
        out_ref[d, 0:2] = sums


def cot_kernel(main, top, bottom, strip, weight, grad_out, flat, square, z0, z1, z2, *, lay):
    put_tiles(flat, lay, main, top, bottom, strip)
    put_square(square, weight, True)
    taps_matmul(flat, square, (z0, z1, z2), lay, True)

    @pl.loop(0, lay.out_rows)
    def _(r):
        begin = pl.multiple_of(r * lay.wide, 16)
        grad_out[pl.ds(begin, lay.wide)] = taken((z0, z1, z2), begin, lay.wide, True)


def mixed_kernel(
    main, top, bottom, strip, coarse, pooled, valid, weight, flat, act_out, stats, square, terms, z0,
    z1, z2, *, lay, arrive
):
    width = main.shape[2]
    flat[...] = jnp.zeros_like(flat)
    blocks = lay.cols // UPSCALE
    near = coarse[0]
    for c in range(1, coarse.shape[0]):
        near = near + coarse[c]
    terms[...] = near.astype(jnp.bfloat16).astype(jnp.float32) * valid[...] + pooled[...]
    for k in range(lay.rows + 5):
        base = MARGIN + k * lay.wide
        i = k - 3
        own, following = (i + UPSCALE) // UPSCALE, (i + 1 + UPSCALE) // UPSCALE

        def spread(block_row, block_col, rows):
            return jnp.broadcast_to(
                terms[block_row, block_col : block_col + 1], (rows, width)
            )

        if i >= -2:
            if i < 0:
                row = top[i + 2]
            elif i < lay.rows:
                row = main[i]
            else:
                row = bottom[i - lay.rows]
            added = jnp.concatenate([spread(own, b + 2, UPSCALE) for b in range(blocks)], 0)
            flat[base : base + lay.cols] = (row.astype(jnp.float32) + added).astype(jnp.bfloat16)
        zero = jnp.zeros((RIM, width), jnp.float32)
        right = spread(own, blocks + 2, RIM) if i >= -2 else zero
        left = spread(following, 1, RIM) if i + 1 < lay.rows + 2 else zero
        flat[base + lay.cols : base + lay.wide] = (
            strip[k].astype(jnp.float32) + jnp.concatenate([right, left], 0)
        ).astype(jnp.bfloat16)
    arrive()
    put_square(square, weight, False)
    taps_matmul(flat, square, (z0, z1, z2), lay, False)

    def step(r, sums):
        begin = pl.multiple_of(r * lay.wide, 16)
        value = taken((z0, z1, z2), begin, lay.wide, False)
        act_out[pl.ds(begin, lay.wide)] = value
        mine = ((r >= 2) & (r < lay.rows + 2)).astype(jnp.float32)
        own_value = value[: lay.cols] * mine
        return sums[0] + folded(own_value), sums[1] + folded(own_value * own_value)

    zero = jnp.zeros((8, width), jnp.float32)
    sums = lax.fori_loop(0, lay.out_rows, step, (zero, zero))
    send_stats(stats, *sums)


def act_moments(stats, pixel_total):
    sums = jnp.sum(stats[...], 0)
    mean = sums[0:1] / pixel_total
    return mean, lax.rsqrt(sums[1:2] / pixel_total - mean * mean + norm_eps)


def inside_masks(lay, width, row_devices, col_devices):
    my_row, my_col = lax.axis_index("rows"), lax.axis_index("cols")
    column = lax.broadcasted_iota(jnp.int32, (lay.wide, width), 0)
    has_right = (my_col < col_devices - 1).astype(jnp.float32)
    has_left = (my_col > 0).astype(jnp.float32)
    near = jnp.where(
        column < lay.cols, 1.0, jnp.where(column < lay.cols + RIM, has_right, 0.0)
    )
    following = jnp.where(column >= lay.cols + RIM, has_left, 0.0)

    def row_inside(i):
        row = my_row * lay.rows + i
        return ((row >= 0) & (row < lay.rows * row_devices)).astype(jnp.float32)

    return lambda r: near * row_inside(r - 2) + following * row_inside(r - 1)


def norm_kernel(
    act, stats, act_grad, activated, grad_out, grad_stats, *, lay, grid, pixel_total
):
    width = act.shape[1]
    mean, inverse = act_moments(stats, pixel_total)
    mask = inside_masks(lay, width, *grid)
    activated[...] = jnp.zeros_like(activated)

    def step(r, sums):
        begin = pl.multiple_of(r * lay.wide, 16)
        normed = (act[pl.ds(begin, lay.wide)] - mean) * inverse
        gate = 1.0 / (1.0 + jnp.exp(-normed))
        inside = mask(r)
        activated[pl.ds(pl.multiple_of(begin + MARGIN + lay.wide, 16), lay.wide)] = (
            normed * gate * inside
        ).astype(jnp.bfloat16)
        grad = act_grad[pl.ds(begin, lay.wide)] * gate * (1.0 + normed * (1.0 - gate))
        grad_out[pl.ds(begin, lay.wide)] = grad
        mine = ((r >= 2) & (r < lay.rows + 2)).astype(jnp.float32)
        own_grad = grad[: lay.cols] * mine
        return sums[0] + folded(own_grad), sums[1] + folded(own_grad * normed[: lay.cols])

    zero = jnp.zeros((8, width), jnp.float32)
    sums = lax.fori_loop(0, lay.out_rows, step, (zero, zero))
    send_stats(grad_stats, *sums)


def weight_matmul(flat_ref, own_ref, total_ref, sent_ref, lay, chunk):
    count = lay.own
    first = MARGIN + 3 * lay.wide - MARGIN
    chunks = 3
    step = count // chunks
    width = own_ref.shape[1]
    total = None
    for c in range(chunks):
        begin = c * step
        left = jnp.concatenate(
            [
                flat_ref[first + begin + a * lay.wide : first + begin + a * lay.wide + step]
                for a in (-1, 0, 1)
            ],
            1,
        )
        right = jnp.concatenate(
            [
                own_ref[MARGIN + begin - b : MARGIN + begin - b + step].astype(jnp.bfloat16)
                for b in (-1, 0, 1)
            ],
            1,
        )
        part = lax.dot_general(
            left, right, (((0,), (0,)), ((), ())), preferred_element_type=jnp.float32
        )
        total = part if total is None else total + part
    for a in range(3):
        for b in range(3):
            total_ref[(a * 3 + b) * width : (a * 3 + b + 1) * width] = total[
                a * width : (a + 1) * width, b * width : (b + 1) * width
            ]
    padded = sent_ref.shape[1]
    for d in range(9 * width // chunk):
        sent_ref[d] = total_ref[d * chunk : d * chunk + padded].astype(jnp.bfloat16)


def second_kernel(
    activated, mixed, main, weight, enhanced, sent, square, z0, z1, z2, own, total, *, lay, chunk,
    arrive
):
    put_square(square, weight, False)
    taps_matmul(activated, square, (z0, z1, z2), lay, False)
    arrive()

    @pl.loop(0, lay.rows)
    def _(i):
        begin = pl.multiple_of((i + 2) * lay.wide, 16)
        value = taken((z0, z1, z2), begin, lay.cols, False)
        place = pl.multiple_of((i + 3) * lay.wide + MARGIN, 16)
        enhanced[i] = (mixed[pl.ds(place, lay.cols)].astype(jnp.float32) + value).astype(
            jnp.bfloat16
        )

    own[...] = jnp.zeros_like(own)

    @pl.loop(0, lay.rows)
    def _(i):
        place = pl.multiple_of(i * lay.wide + 2 * MARGIN, 16)
        own[pl.ds(place, lay.cols)] = main[i].astype(jnp.float32)

    weight_matmul(activated, own, total, sent, lay, chunk)


def first_kernel(
    stats, grad_stats, act, grad_ref, mixed, second, sent, kept, own, total, *, lay, grid,
    chunk, pixel_total, arrive
):
    width = act.shape[1]
    mean, inverse = act_moments(stats, pixel_total)
    sums = jnp.sum(grad_stats[...], 0)
    grad_mean, cross_mean = sums[0:1] / pixel_total, sums[1:2] / pixel_total
    mask = inside_masks(lay, width, *grid)
    own[...] = jnp.zeros_like(own)
    kept[...] = jnp.zeros_like(kept)

    @pl.loop(0, lay.out_rows)
    def _(r):
        begin = pl.multiple_of(r * lay.wide, 16)
        value = inverse * (
            grad_ref[pl.ds(begin, lay.wide)]
            - grad_mean
            - (act[pl.ds(begin, lay.wide)] - mean) * inverse * cross_mean
        )
        value = (value * mask(r)).astype(jnp.bfloat16)
        kept[pl.ds(begin, lay.wide)] = value

        @pl.when((r >= 2) & (r < lay.rows + 2))
        def _():
            place = pl.multiple_of((r - 2) * lay.wide + 2 * MARGIN, 16)
            own[pl.ds(place, lay.cols)] = value[: lay.cols].astype(jnp.float32)

    arrive()
    weight_matmul(mixed, own, total, sent, lay, chunk)
    for d in range(second.shape[0]):
        sent[second.shape[0] + d] = second[d]


def coarse_kernel(kept, picked, main, weight, out, *, lay):
    width = weight.shape[2]
    windows = jnp.dot(picked[...], kept[...], preferred_element_type=jnp.float32)
    block_rows, block_cols = lay.rows // UPSCALE, lay.cols // UPSCALE
    blocks = block_rows * block_cols
    summed = jnp.zeros((blocks, width), jnp.float32)
    for tap in range(9):
        summed = summed + lax.dot_general(
            windows[tap * blocks : (tap + 1) * blocks],
            weight[tap // 3, tap % 3].astype(jnp.float32),
            (((1,), (1,)), ((), ())),
            precision=lax.Precision.HIGHEST,
            preferred_element_type=jnp.float32,
        )
    for bi in range(block_rows):
        rows = jnp.zeros((lay.cols, width), jnp.float32)
        for i in range(UPSCALE):
            rows = rows + main[bi * UPSCALE + i].astype(jnp.float32)
        for bj in range(block_cols):
            k = bi * block_cols + bj
            cot = jnp.sum(rows[bj * UPSCALE : (bj + 1) * UPSCALE], 0, keepdims=True)
            out[k : k + 1] = (cot + summed[k : k + 1]) / UPSCALE


def share_kernel(received, sent, *, rescale):
    total = received[0].astype(jnp.float32)
    for d in range(1, received.shape[0]):
        total = total + received[d].astype(jnp.float32)
    total = (total * rescale).astype(jnp.bfloat16)
    for d in range(sent.shape[0]):
        sent[d] = total


def join_kernel(mine, other, first, second, *, chunk, grid):
    row_devices, col_devices = grid
    half, pairs = row_devices * col_devices // 2, col_devices // 2
    core = lax.axis_index("cols") & 1
    for k in range(2):

        @pl.when(core == k)
        def _():
            for source, side in ((mine, k), (other, 1 - k)):
                for d in range(half):
                    owner = d // pairs * col_devices + d % pairs * 2 + side
                    out = first if owner < half else second
                    begin = owner % half * chunk
                    out[begin : begin + chunk] = source[d].astype(jnp.float32)[:chunk]


def window_picks(lay):
    place = np.arange(lay.kept)
    slot, column = place // lay.wide + 1, place % lay.wide
    behind = column >= lay.cols + RIM
    i = np.where(behind, slot - 2, slot - 3)
    j = np.where(behind, column - lay.wide, column)
    rows = []
    for a in range(3):
        for b in range(3):
            y, x = i + a - 1, j + b - 1
            for bi in range(lay.rows // UPSCALE):
                for bj in range(lay.cols // UPSCALE):
                    rows.append((y // UPSCALE == bi) & (x // UPSCALE == bj) & (place < lay.out))
    return jnp.asarray(np.stack(rows), jnp.bfloat16)


def to_all(payload, axis):
    return lax.all_to_all(payload, axis, 0, 0)


def among_cores(payload, row_devices, col_devices):
    groups = [
        [r * col_devices + 2 * h + k for r in range(row_devices) for h in range(col_devices // 2)]
        for k in range(2)
    ]
    return lax.all_to_all(payload, BOTH, 0, 0, axis_index_groups=groups)


def core_swap(array, col_devices):
    return lax.ppermute(array, "cols", [(c, c ^ 1) for c in range(col_devices)])


def pieces(array):
    high = array.astype(jnp.bfloat16)
    rest = array - high.astype(jnp.float32)
    middle = rest.astype(jnp.bfloat16)
    return high, middle, (rest - middle.astype(jnp.float32)).astype(jnp.bfloat16)


def lane_roll(value, shift):
    return pltpu.roll(value, shift % value.shape[1], 1)


def pack_kernel(features, labels, band, sent, sums):
    encoder_width, tile_rows, tile_cols = features.shape
    block_rows, block_cols = tile_rows // UPSCALE, tile_cols // UPSCALE
    blocks = block_rows * block_cols
    sums[...] = jnp.zeros_like(sums)
    slot = lax.broadcasted_iota(jnp.int32, (blocks, tile_cols), 0)
    column = lax.broadcasted_iota(jnp.int32, (blocks, tile_cols), 1)
    total = jnp.zeros((blocks, 128), jnp.float32)
    for r in range(block_rows):
        sums[0:encoder_width] = jnp.sum(features[:, r * UPSCALE : (r + 1) * UPSCALE], 1)
        sums[encoder_width : encoder_width + 1] = (
            labels[r * UPSCALE : r * UPSCALE + 1].astype(jnp.float32) / UPSCALE
        )
        low = (slot - r * block_cols) * UPSCALE
        picked = ((column >= low) & (column < low + UPSCALE)).astype(jnp.float32)
        total = total + lax.dot_general(
            picked,
            sums[...],
            (((1,), (1,)), ((), ())),
            precision=lax.Precision.HIGHEST,
            preferred_element_type=jnp.float32,
        )
    high, middle, low = pieces(total)
    packed = (
        high.astype(jnp.float32)
        + lane_roll(middle.astype(jnp.float32), 32)
        + lane_roll(low.astype(jnp.float32), 64)
    )
    value = jnp.concatenate([band[...].astype(jnp.float32), packed], 0).astype(jnp.bfloat16)
    for d in range(sent.shape[0]):
        sent[d] = value


def pool_kernel(mine_ref, other_ref, places, weight, pooled, valid, table, *, near, coarse):
    block_rows, block_cols = near
    coarse_rows, coarse_cols = coarse
    encoder_width = weight.shape[0]
    half, rows, _ = mine_ref.shape
    devices = 2 * half
    lane = lax.broadcasted_iota(jnp.int32, (8, 128), 1)
    for d in range(devices):
        part = mine_ref[d] if d < half else other_ref[d - half]
        packed = part.astype(jnp.float32)[rows - 8 :]
        value = packed + lane_roll(packed, -32) + lane_roll(packed, -64)
        table[d * 8 : (d + 1) * 8] = jnp.where(lane <= encoder_width, value, 0.0)
    exact = dict(precision=lax.Precision.HIGHEST, preferred_element_type=jnp.float32)
    row0 = lax.axis_index("rows") * block_rows - 1
    col0 = lax.axis_index("cols") * block_cols - 2

    def position(shape):
        q = lax.broadcasted_iota(jnp.int32, shape, 0)
        return row0 + (q >> 3), col0 + (q & 7)

    count = pooled.shape[0]
    row, col = position((count, devices * 8))
    core = lax.axis_index("cols") & 1
    column = places[1:2] + block_cols * jnp.where(places[2:3] == 1, core, 1 - core)
    chosen = ((row == places[0:1]) & (col == column)).astype(jnp.float32)
    mine = jnp.dot(chosen, table[...], **exact)[:, encoder_width : encoder_width + 1]
    pick = (lane == encoder_width).astype(jnp.float32)
    every = lax.dot_general(pick, table[...], (((1,), (1,)), ((), ())), **exact)[0:1]
    same = (mine == every).astype(jnp.float32)
    sums = jnp.dot(same, table[...], **exact)
    members = jnp.sum(same, 1, keepdims=True) * float(UPSCALE * UPSCALE)
    averages = sums / jnp.maximum(members, 1.0)
    result = jnp.dot(averages[:, :encoder_width], weight[...], **exact)
    row, col = position(pooled.shape)
    inside = (row >= 0) & (row < coarse_rows) & (col >= 0) & (col < coarse_cols)
    pooled[...] = jnp.where(inside, result, 0.0)
    valid[...] = inside.astype(jnp.float32)


def channel_conv(rows_ref, weight, shifted, out_rows, cols):
    width = weight.shape[3]
    count = out_rows * cols
    sums = None
    for a in range(3):
        left = rows_ref[a * cols : a * cols + count]
        if width % 128:
            part = [
                jnp.dot(left, weight[a, b], preferred_element_type=jnp.float32) for b in range(3)
            ]
        else:
            right = jnp.concatenate([weight[a, b] for b in range(3)], 1)
            part = jnp.dot(left, right, preferred_element_type=jnp.float32)
            part = [part[:, b * width : (b + 1) * width] for b in range(3)]
        sums = part if sums is None else [s + p for s, p in zip(sums, part)]
    shifted[...] = jnp.zeros_like(shifted)
    total = sums[1]
    for b in (0, 2):
        shifted[:, 8 : 8 + cols] = sums[b].reshape(out_rows, cols, width)
        total = total + shifted[:, 7 + b : 7 + b + cols].reshape(count, width)
    return total


def hidden_kernel(mine, other, weight, sent, rows_ref, shifted, kept, *, grid, band, direct, arrive):
    row_devices, col_devices = grid
    band_rows, cols = band
    coarse_rows = row_devices * band_rows
    width = weight.shape[3]
    rows_ref[...] = jnp.zeros_like(rows_ref)
    if direct:
        pairs = col_devices // 2
        core = lax.axis_index("cols") & 1
        for source, side in ((mine, core), (other, 1 - core)):
            for d in range(row_devices * pairs):
                begin = (1 + d // pairs * band_rows) * cols
                lanes = pl.multiple_of((d % pairs * 2 + side) * width, width)
                rows_ref[begin : begin + band_rows * cols, pl.ds(lanes, width)] = source[
                    d, : band_rows * cols
                ]
    else:
        rows_ref[cols : cols + coarse_rows * cols] = mine[...]
    arrive()
    raw = channel_conv(rows_ref, weight, shifted, coarse_rows, cols)
    pixels = coarse_rows * cols
    mean = jnp.sum(raw, 0, keepdims=True) / pixels
    variance = jnp.sum(raw * raw, 0, keepdims=True) / pixels - mean * mean
    hidden = jnp.maximum((raw - mean) * lax.rsqrt(variance + norm_eps), 0.0)
    kept[...] = jnp.zeros_like(kept)
    kept[2 : 2 + coarse_rows] = hidden.astype(jnp.bfloat16).reshape(coarse_rows, cols, width)
    near = kept[pl.ds(lax.axis_index("rows") * band_rows, band_rows + 4)]
    near = near.reshape((band_rows + 4) * cols, width)
    for d in range(sent.shape[0]):
        sent[d] = near


def project_kernel(
    received, weight, source, project, sent, rows_ref, shifted, residual, spread, *, grid, band,
    direct, arrive
):
    row_devices, col_devices = grid
    band_rows, cols = band
    width = weight.shape[3]
    my_col = lax.axis_index("cols")
    for c in range(col_devices):
        rows_ref[:, c * width : (c + 1) * width] = received[c]
    arrive()
    raw = channel_conv(rows_ref, weight, shifted, band_rows + 2, cols)
    count = (band_rows + 2) * cols
    if direct:
        residual[...] = jnp.zeros_like(residual)
        for r in range(row_devices):
            piece = source[r * (col_devices // 2) + (my_col >> 1), : band_rows * cols]
            residual[1 + r * band_rows : 1 + (r + 1) * band_rows] = piece.reshape(
                band_rows, cols, width
            )
        base = residual[pl.ds(lax.axis_index("rows") * band_rows, band_rows + 2)]
        base = base.reshape(count, width)
    else:
        base = source[...]
    result = (base.astype(jnp.float32) + raw).astype(jnp.bfloat16)
    rows = project[pl.ds(pl.multiple_of(my_col * width, width), width)]
    partial = jnp.dot(result, rows, preferred_element_type=jnp.float32)
    spread[...] = jnp.zeros_like(spread)
    spread[:, 8 : 8 + cols] = partial.reshape(band_rows + 2, cols, partial.shape[1])
    step = cols // col_devices
    for j in range(col_devices):
        sent[j] = spread[:, 6 + j * step : 6 + j * step + sent.shape[2]]


def per_device(
    global_in,
    global_first,
    global_second,
    project_weight,
    enhancer_input,
    instance_map,
    encoder_features,
    instance_weight,
    enhancer_first,
    enhancer_second,
    output_cotangent,
):
    row_devices, col_devices = lax.axis_size("rows"), lax.axis_size("cols")
    devices = row_devices * col_devices
    my_row, my_col = lax.axis_index("rows"), lax.axis_index("cols")
    band_rows, band_cols, width_share = global_in.shape
    tile_rows, tile_cols, local_width = enhancer_input.shape
    coarse_rows = band_rows * row_devices
    block_rows = tile_rows // UPSCALE
    block_cols = tile_cols // UPSCALE
    blocks = block_rows * block_cols
    encoder_width = encoder_features.shape[0]

    lay = Layout(tile_rows, tile_cols)
    width = local_width
    grid = (row_devices, col_devices)
    band = (band_rows, band_cols)
    direct = width_share == 128
    main = global_in.reshape(-1, 128)
    main_rows = main.shape[0]
    sent_input = call(
        pack_kernel,
        jax.ShapeDtypeStruct((devices // 2, main_rows + 8, 128), jnp.bfloat16),
        (encoder_features, instance_map, main),
        [pltpu.VMEM((128, tile_cols), jnp.float32)],
        far={0: None, 1: None, 2: None},
    )
    mine = among_cores(sent_input, row_devices, col_devices)
    late_input, late_cotangent, _ = lax.optimization_barrier(
        (enhancer_input, output_cotangent, sent_input)
    )
    tops = jnp.stack([late_input[-2:], late_cotangent[-2:]])
    bottoms = jnp.stack([late_input[:2], late_cotangent[:2]])

    row_up = [(i, i + 1) for i in range(row_devices - 1)]
    row_down = [(j, i) for i, j in row_up]
    col_up = [(i, i + 1) for i in range(col_devices - 1)]
    col_down = [(j, i) for i, j in col_up]
    top = lax.ppermute(tops, "rows", row_up)
    bottom = lax.ppermute(bottoms, "rows", row_down)
    both = jnp.stack([late_input, late_cotangent])
    tall_last = jnp.concatenate([top[:, :, -RIM:], both[:, :, -RIM:], bottom[:, :, -RIM:]], 1)
    tall_first = jnp.concatenate([top[:, :, :RIM], both[:, :, :RIM], bottom[:, :, :RIM]], 1)
    mine, tall_last, tall_first = lax.optimization_barrier((mine, tall_last, tall_first))
    other = core_swap(mine, col_devices)
    pixel_total = float(tile_rows * tile_cols * devices)
    chunk = 18 * width // devices
    padded_chunk = -(-chunk // 8) * 8
    square = pltpu.VMEM((3 * width, 3 * width), jnp.bfloat16)
    z = [pltpu.VMEM((lay.z, width), jnp.float32)] * 3
    own = pltpu.VMEM((lay.own + 2 * MARGIN, width), jnp.float32)
    total = pltpu.VMEM((9 * width + 64, width), jnp.float32)
    flat_shape = jax.ShapeDtypeStruct((lay.flat, width), jnp.bfloat16)
    out_shape = jax.ShapeDtypeStruct((lay.out, width), jnp.float32)
    stats_shape = jax.ShapeDtypeStruct((devices, 8, width), jnp.float32)
    sent_shape = jax.ShapeDtypeStruct((devices, padded_chunk, width), jnp.bfloat16)
    half_shape = jax.ShapeDtypeStruct((devices // 2, padded_chunk, width), jnp.bfloat16)
    conv_flops = 18 * width * width * lay.out

    place = np.arange(devices * blocks)
    owner, slot = place // blocks % (devices // 2), place % blocks
    pairs = col_devices // 2
    places = np.zeros((8, devices * blocks), np.int32)
    places[0] = owner // pairs * block_rows + slot // block_cols
    places[1] = owner % pairs * 2 * block_cols + slot % block_cols
    places[2] = place // blocks < devices // 2
    near_shape = jax.ShapeDtypeStruct(((block_rows + 2) * 8, width), jnp.float32)
    pooled, valid = call(
        pool_kernel,
        (near_shape, near_shape),
        (mine, other, jnp.asarray(places), instance_weight),
        [pltpu.VMEM((devices * 8, 128), jnp.float32)],
        near=(block_rows, block_cols),
        coarse=(coarse_rows, band_cols),
    )
    channels = width_share * col_devices
    if direct:
        sources, base = (mine, other), mine
    else:
        even = my_col % 2 == 0
        sides = [jnp.where(even, mine, other), jnp.where(even, other, mine)]
        gathered = jnp.stack([side[:, :main_rows] for side in sides], 1).reshape(
            row_devices, col_devices, band_rows, band_cols, width_share
        )
        source = gathered.transpose(0, 2, 3, 1, 4).reshape(coarse_rows * band_cols, channels)
        sources = (source, source)
        column = lax.dynamic_index_in_dim(gathered, my_col, 1, keepdims=False)
        column = jnp.pad(
            column.reshape(coarse_rows, band_cols, width_share), ((1, 1), (0, 0), (0, 0))
        )
        base = lax.dynamic_slice_in_dim(column, my_row * band_rows, band_rows + 2, 0)
        base = base.reshape(-1, width_share)
    near_rows = band_rows + 4
    sent_hidden = call(
        hidden_kernel,
        jax.ShapeDtypeStruct((col_devices, near_rows * band_cols, width_share), jnp.bfloat16),
        (*sources, global_first),
        [
            pltpu.VMEM(((coarse_rows + 2) * band_cols, channels), jnp.bfloat16),
            pltpu.VMEM((coarse_rows, band_cols + 16, width_share), jnp.float32),
            pltpu.VMEM((coarse_rows + 4, band_cols, width_share), jnp.bfloat16),
        ],
        18 * coarse_rows * band_cols * channels * width_share,
        far={2: None},
        late=(2,),
        far_out=(0,),
        grid=grid,
        band=band,
        direct=direct,
    )
    near_hidden = to_all(sent_hidden, "cols")
    tall_last, tall_first, _ = lax.optimization_barrier((tall_last, tall_first, sent_hidden))
    left = lax.ppermute(tall_last, "cols", col_up)
    right = lax.ppermute(tall_first, "cols", col_down)
    strip = jnp.concatenate(
        [
            jnp.pad(right, ((0, 0), (1, 0), (0, 0), (0, 0))),
            jnp.pad(left, ((0, 0), (0, 1), (0, 0), (0, 0))),
        ],
        2,
    )
    act_grad = call(
        cot_kernel,
        out_shape,
        (output_cotangent, top, bottom, strip, enhancer_second),
        [pltpu.VMEM((lay.flat, width), jnp.bfloat16), square, *z],
        conv_flops,
        far={0: None, 1: 1, 2: 1, 3: 1, 4: None},
        far_out=(0,),
        lay=lay,
    )

    sent_coarse = call(
        project_kernel,
        jax.ShapeDtypeStruct((col_devices, band_rows + 2, 8, width), jnp.float32),
        (near_hidden, global_second, base, project_weight),
        [
            pltpu.VMEM((near_rows * band_cols, channels), jnp.bfloat16),
            pltpu.VMEM((band_rows + 2, band_cols + 16, width_share), jnp.float32),
            pltpu.VMEM((coarse_rows + 2, band_cols, width_share), jnp.bfloat16),
            pltpu.VMEM((band_rows + 2, band_cols + 16, width), jnp.float32),
        ],
        18 * (band_rows + 2) * band_cols * channels * width_share,
        far={1: None, 2: None, 3: None},
        late=(1, 2, 3),
        far_out=(0,),
        grid=grid,
        band=band,
        direct=direct,
    )
    near_coarse = to_all(sent_coarse, "cols")
    terms = (near_coarse, pooled.reshape(-1, 8, width), valid.reshape(-1, 8, width))

    mixed, first_act, stats = call(
        mixed_kernel,
        (flat_shape, out_shape, stats_shape),
        (enhancer_input, top, bottom, strip, *terms, enhancer_first),
        [square, pltpu.VMEM((block_rows + 2, 8, width), jnp.float32), *z],
        conv_flops,
        far={0: None, 1: 0, 2: 0, 3: 0, 5: None, 6: None, 7: None},
        late=(7,),
        far_out=(0, 1, 2),
        lay=lay,
    )
    stats = to_all(stats, BOTH)
    activated, normed_grad, grad_stats = call(
        norm_kernel,
        (flat_shape, out_shape, stats_shape),
        (first_act, stats, act_grad),
        far={0: None, 2: None},
        far_out=(0, 1, 2),
        lay=lay,
        grid=grid,
        pixel_total=pixel_total,
    )
    grad_stats = to_all(grad_stats, BOTH)
    enhanced, second_sent = call(
        second_kernel,
        (jax.ShapeDtypeStruct((tile_rows, tile_cols, width), jnp.bfloat16), half_shape),
        (activated, mixed, output_cotangent, enhancer_second),
        [square, *z, own, total],
        2 * conv_flops,
        far={0: None, 1: None, 2: None, 3: None},
        late=(1, 2),
        far_out=(1,),
        lay=lay,
        chunk=chunk,
    )
    sent_both, kept = call(
        first_kernel,
        (sent_shape, jax.ShapeDtypeStruct((lay.kept, width), jnp.bfloat16)),
        (stats, grad_stats, first_act, normed_grad, mixed, second_sent),
        [own, total],
        conv_flops,
        far={2: None, 3: None, 4: None, 5: None},
        late=(4, 5),
        far_out=(1,),
        lay=lay,
        grid=grid,
        chunk=chunk,
        pixel_total=pixel_total,
    )
    part = to_all(sent_both, BOTH)
    rescale = 1.0 / math.sqrt(pixel_total)
    global_gradient = call(
        coarse_kernel,
        jax.ShapeDtypeStruct((blocks, width), jnp.float32),
        (kept, window_picks(lay), output_cotangent, enhancer_first),
        far={0: None, 1: None, 2: None, 3: None},
        lay=lay,
    )
    part, global_gradient = lax.optimization_barrier((part, global_gradient))
    share = call(share_kernel, half_shape, (part,), rescale=rescale)
    share = among_cores(share, row_devices, col_devices)
    shares = (share, core_swap(share, col_devices))
    whole_shape = jax.ShapeDtypeStruct((9 * width, width), jnp.float32)
    first_total, second_total = call(
        join_kernel, (whole_shape, whole_shape), shares, chunk=chunk, grid=grid
    )
    return (
        enhanced,
        first_total.reshape(3, 3, width, width),
        second_total.reshape(3, 3, width, width),
        global_gradient.reshape(block_rows, block_cols, width),
    )


def solution(mesh):
    return jax.shard_map(
        per_device,
        mesh=mesh,
        in_specs=(
            P("rows", None, "cols"),
            P(None, None, None, "cols"),
            P(None, None, None, "cols"),
            P(),
            P("rows", "cols", None),
            P("rows", "cols"),
            P(None, "rows", "cols"),
            P(),
            P(),
            P(),
            P("rows", "cols", None),
        ),
        out_specs=(P("rows", "cols", None), P(), P(), P("rows", "cols", None)),
        check_vma=False,
    )
```

```python
import math

import jax
import jax.numpy as jnp
import numpy as np
from jax import lax
from jax.experimental import pallas as pl
from jax.experimental.pallas import tpu as pltpu
from jax.sharding import PartitionSpec as P

INSTANCES = 256
UPSCALE = 16
BOTH = ("rows", "cols")

norm_eps = 1e-05


RIM = 8
MARGIN = 16
KERNEL_VMEM = 20 * 1024 * 1024


class Layout:
    def __init__(self, tile_rows, tile_cols):
        self.rows, self.cols = tile_rows, tile_cols
        self.wide = tile_cols + 2 * RIM
        self.flat = (tile_rows + 6) * self.wide + 2 * MARGIN
        self.out_rows = tile_rows + 3
        self.out = self.out_rows * self.wide
        self.z = self.out + 2 * MARGIN
        self.own = tile_rows * self.wide + 2 * MARGIN
        self.kept = -(-self.out // 128) * 128


def call(
    body, outs, ins, scratch=(), flops=0, far=(), pick=None, far_out=(), limit=KERNEL_VMEM, **fixed
):
    pick = pick or {}
    single = not isinstance(outs, tuple)
    outs = (outs,) if single else outs
    n_in, n_out, n_own = len(ins), len(outs), len(scratch)
    near = pl.BlockSpec(memory_space=pltpu.VMEM)
    hbm = pl.BlockSpec(memory_space=pltpu.MemorySpace.HBM)
    landing = [pltpu.VMEM(ins[i].shape, ins[i].dtype) for i in far]
    leaving = [pltpu.VMEM(outs[j].shape, outs[j].dtype) for j in far_out]

    def kernel(*refs):
        in_refs, out_refs = list(refs[:n_in]), list(refs[n_in : n_in + n_out])
        rest = refs[n_in + n_out :]
        own, rest = rest[:n_own], rest[n_own:]
        buffers, sems = rest[: len(far) + len(far_out)], rest[len(far) + len(far_out) :]
        starts, results = [], []
        for slot, i in enumerate(far):
            starts.append(pltpu.make_async_copy(in_refs[i], buffers[slot], sems[slot]))
            starts[-1].start()
            in_refs[i] = buffers[slot]
        for slot, j in enumerate(far_out, len(far)):
            results.append((buffers[slot], out_refs[j], sems[slot]))
            out_refs[j] = buffers[slot]
        for i, k in pick.items():
            in_refs[i] = in_refs[i].at[k]
        for copy in starts:
            copy.wait()
        body(*in_refs, *out_refs, *own, **fixed)
        ends = [pltpu.make_async_copy(*triple) for triple in results]
        for copy in ends:
            copy.start()
        for copy in ends:
            copy.wait()

    result = pl.pallas_call(
        kernel,
        out_shape=outs,
        in_specs=[hbm if i in far else near for i in range(n_in)],
        out_specs=tuple(hbm if j in far_out else near for j in range(n_out)),
        scratch_shapes=[
            *scratch,
            *landing,
            *leaving,
            *[pltpu.SemaphoreType.DMA] * (len(landing) + len(leaving)),
        ],
        compiler_params=pltpu.CompilerParams(vmem_limit_bytes=limit),
        cost_estimate=pl.CostEstimate(flops=flops, bytes_accessed=4 << 20, transcendentals=0),
        name=body.__name__,
    )(*ins)
    return result[0] if single else result


def put_tiles(flat_ref, lay, main_ref, top_ref, bottom_ref, strip_ref):
    flat_ref[...] = jnp.zeros_like(flat_ref)
    for k in range(lay.rows + 5):
        base = MARGIN + k * lay.wide
        i = k - 3
        if i >= -2:
            if i < 0:
                row = top_ref[i + 2]
            elif i < lay.rows:
                row = main_ref[i]
            else:
                row = bottom_ref[i - lay.rows]
            flat_ref[base : base + lay.cols] = row
        flat_ref[base + lay.cols : base + lay.wide] = strip_ref[k]


def taps_matmul(flat_ref, square_ref, z_refs, lay, turned):
    count = z_refs[0].shape[0]
    chunks = 3
    step = count // chunks
    width = z_refs[0].shape[1]

    @pl.loop(0, chunks)
    def _(c):
        begin = pl.multiple_of(c * step, 16)
        parts = [flat_ref[pl.ds(begin + shift, step)] for shift in (0, lay.wide, 2 * lay.wide)]
        if turned:
            left = jnp.concatenate(parts[::-1], 1)
            result = lax.dot_general(
                left, square_ref[...], (((1,), (1,)), ((), ())), preferred_element_type=jnp.float32
            )
        else:
            left = jnp.concatenate(parts, 1)
            result = jnp.dot(left, square_ref[...], preferred_element_type=jnp.float32)
        for b in range(3):
            z_refs[b][pl.ds(begin, step)] = result[:, b * width : (b + 1) * width]


def put_square(square_ref, weight_ref, turned):
    width = weight_ref.shape[2]
    for a in range(3):
        for b in range(3):
            r, c = (b, a) if turned else (a, b)
            square_ref[r * width : (r + 1) * width, c * width : (c + 1) * width] = weight_ref[a, b]


def taken(z_refs, begin, count, turned):
    early, late = (2, 0) if turned else (0, 2)
    return (
        z_refs[early][pl.ds(begin + MARGIN - 1, count)]
        + z_refs[1][pl.ds(begin + MARGIN, count)]
        + z_refs[late][pl.ds(begin + MARGIN + 1, count)]
    )


def folded(value):
    return value.reshape(-1, 8, value.shape[-1]).sum(0)


def send_stats(out_ref, first, second):
    sums = jnp.concatenate(
        [jnp.sum(first, 0, keepdims=True), jnp.sum(second, 0, keepdims=True)], 0
    )
    out_ref[...] = jnp.zeros_like(out_ref)
    for d in range(out_ref.shape[0]):
        out_ref[d, 0:2] = sums


def cot_kernel(main, top, bottom, strip, weight, grad_out, flat, square, z0, z1, z2, *, lay):
    put_tiles(flat, lay, main, top, bottom, strip)
    put_square(square, weight, True)
    taps_matmul(flat, square, (z0, z1, z2), lay, True)

    @pl.loop(0, lay.out_rows)
    def _(r):
        begin = pl.multiple_of(r * lay.wide, 16)
        value = taken((z0, z1, z2), begin, lay.wide, True)
        grad_out[pl.ds(begin, lay.wide)] = value.astype(jnp.bfloat16)


def mixed_kernel(
    main, top, bottom, strip, coarse, pooled, valid, weight, flat, act_out, stats, square, terms, z0,
    z1, z2, *, lay
):
    width = main.shape[2]
    flat[...] = jnp.zeros_like(flat)
    blocks = lay.cols // UPSCALE
    near = coarse[0]
    for c in range(1, coarse.shape[0]):
        near = near + coarse[c]
    terms[...] = near.astype(jnp.bfloat16).astype(jnp.float32) * valid[...] + pooled[...]
    for k in range(lay.rows + 5):
        base = MARGIN + k * lay.wide
        i = k - 3
        own, following = (i + UPSCALE) // UPSCALE, (i + 1 + UPSCALE) // UPSCALE

        def spread(block_row, block_col, rows):
            return jnp.broadcast_to(
                terms[block_row, block_col : block_col + 1], (rows, width)
            )

        if i >= -2:
            if i < 0:
                row = top[i + 2]
            elif i < lay.rows:
                row = main[i]
            else:
                row = bottom[i - lay.rows]
            added = jnp.concatenate([spread(own, b + 2, UPSCALE) for b in range(blocks)], 0)
            flat[base : base + lay.cols] = (row.astype(jnp.float32) + added).astype(jnp.bfloat16)
        zero = jnp.zeros((RIM, width), jnp.float32)
        right = spread(own, blocks + 2, RIM) if i >= -2 else zero
        left = spread(following, 1, RIM) if i + 1 < lay.rows + 2 else zero
        flat[base + lay.cols : base + lay.wide] = (
            strip[k].astype(jnp.float32) + jnp.concatenate([right, left], 0)
        ).astype(jnp.bfloat16)
    put_square(square, weight, False)
    taps_matmul(flat, square, (z0, z1, z2), lay, False)

    def step(r, sums):
        begin = pl.multiple_of(r * lay.wide, 16)
        value = taken((z0, z1, z2), begin, lay.wide, False)
        act_out[pl.ds(begin, lay.wide)] = value
        mine = ((r >= 2) & (r < lay.rows + 2)).astype(jnp.float32)
        own_value = value[: lay.cols] * mine
        return sums[0] + folded(own_value), sums[1] + folded(own_value * own_value)

    zero = jnp.zeros((8, width), jnp.float32)
    sums = lax.fori_loop(0, lay.out_rows, step, (zero, zero))
    send_stats(stats, *sums)


def act_moments(stats, pixel_total):
    sums = jnp.sum(stats[...], 0)
    mean = sums[0:1] / pixel_total
    return mean, lax.rsqrt(sums[1:2] / pixel_total - mean * mean + norm_eps)


def inside_masks(lay, width, row_devices, col_devices):
    my_row, my_col = lax.axis_index("rows"), lax.axis_index("cols")
    column = lax.broadcasted_iota(jnp.int32, (lay.wide, width), 0)
    has_right = (my_col < col_devices - 1).astype(jnp.float32)
    has_left = (my_col > 0).astype(jnp.float32)
    near = jnp.where(
        column < lay.cols, 1.0, jnp.where(column < lay.cols + RIM, has_right, 0.0)
    )
    following = jnp.where(column >= lay.cols + RIM, has_left, 0.0)

    def row_inside(i):
        row = my_row * lay.rows + i
        return ((row >= 0) & (row < lay.rows * row_devices)).astype(jnp.float32)

    return lambda r: near * row_inside(r - 2) + following * row_inside(r - 1)


def gated(value):
    gate = 1.0 / (1.0 + jnp.exp(-value))
    return gate, gate * (1.0 + value * (1.0 - gate))


def norm_kernel(act, stats, act_grad, grad_stats, *, lay, pixel_total):
    width = act.shape[1]
    mean, inverse = act_moments(stats, pixel_total)

    def step(i, sums):
        begin = pl.multiple_of((i + 2) * lay.wide, 16)
        normed = (act[pl.ds(begin, lay.cols)] - mean) * inverse
        _, slope = gated(normed)
        grad = act_grad[pl.ds(begin, lay.cols)].astype(jnp.float32) * slope
        return sums[0] + folded(grad), sums[1] + folded(grad * normed)

    zero = jnp.zeros((8, width), jnp.float32)
    sums = lax.fori_loop(0, lay.rows, step, (zero, zero))
    send_stats(grad_stats, *sums)


def weight_matmul(flat_ref, own_ref, total_ref, sent_ref, lay, chunk):
    count = lay.own
    first = MARGIN + 3 * lay.wide - MARGIN
    chunks = 3
    step = count // chunks
    width = own_ref.shape[1]
    total = None
    for c in range(chunks):
        begin = c * step
        left = jnp.concatenate(
            [
                flat_ref[first + begin + a * lay.wide : first + begin + a * lay.wide + step]
                for a in (-1, 0, 1)
            ],
            1,
        )
        right = jnp.concatenate(
            [
                own_ref[MARGIN + begin - b : MARGIN + begin - b + step].astype(jnp.bfloat16)
                for b in (-1, 0, 1)
            ],
            1,
        )
        part = lax.dot_general(
            left, right, (((0,), (0,)), ((), ())), preferred_element_type=jnp.float32
        )
        total = part if total is None else total + part
    for a in range(3):
        for b in range(3):
            total_ref[(a * 3 + b) * width : (a * 3 + b + 1) * width] = total[
                a * width : (a + 1) * width, b * width : (b + 1) * width
            ]
    padded = sent_ref.shape[1]
    for d in range(9 * width // chunk):
        sent_ref[d] = total_ref[d * chunk : d * chunk + padded].astype(jnp.bfloat16)


def second_kernel(
    act, stats, mixed, main, weight, enhanced, sent, activated, square, z0, z1, z2, own, total, *, lay, chunk,
    grid, pixel_total
):
    width = act.shape[1]
    mean, inverse = act_moments(stats, pixel_total)
    mask = inside_masks(lay, width, *grid)
    activated[...] = jnp.zeros_like(activated)

    @pl.loop(0, lay.out_rows)
    def _(r):
        begin = pl.multiple_of(r * lay.wide, 16)
        normed = (act[pl.ds(begin, lay.wide)] - mean) * inverse
        gate, _ = gated(normed)
        activated[pl.ds(pl.multiple_of(begin + MARGIN + lay.wide, 16), lay.wide)] = (
            normed * gate * mask(r)
        ).astype(jnp.bfloat16)

    put_square(square, weight, False)
    taps_matmul(activated, square, (z0, z1, z2), lay, False)

    @pl.loop(0, lay.rows)
    def _(i):
        begin = pl.multiple_of((i + 2) * lay.wide, 16)
        value = taken((z0, z1, z2), begin, lay.cols, False)
        place = pl.multiple_of((i + 3) * lay.wide + MARGIN, 16)
        enhanced[i] = (mixed[pl.ds(place, lay.cols)].astype(jnp.float32) + value).astype(
            jnp.bfloat16
        )

    own[...] = jnp.zeros_like(own)

    @pl.loop(0, lay.rows)
    def _(i):
        place = pl.multiple_of(i * lay.wide + 2 * MARGIN, 16)
        own[pl.ds(place, lay.cols)] = main[i].astype(jnp.float32)

    weight_matmul(activated, own, total, sent, lay, chunk)


def first_kernel(
    stats, grad_stats, act, act_grad, mixed, second, sent, kept, own, total, *, lay, grid,
    chunk, pixel_total
):
    width = act.shape[1]
    mean, inverse = act_moments(stats, pixel_total)
    sums = jnp.sum(grad_stats[...], 0)
    grad_mean, cross_mean = sums[0:1] / pixel_total, sums[1:2] / pixel_total
    mask = inside_masks(lay, width, *grid)
    own[...] = jnp.zeros_like(own)
    kept[...] = jnp.zeros_like(kept)

    @pl.loop(0, lay.out_rows)
    def _(r):
        begin = pl.multiple_of(r * lay.wide, 16)
        normed = (act[pl.ds(begin, lay.wide)] - mean) * inverse
        _, slope = gated(normed)
        grad = act_grad[pl.ds(begin, lay.wide)].astype(jnp.float32) * slope
        value = inverse * (grad - grad_mean - normed * cross_mean)
        value = (value * mask(r)).astype(jnp.bfloat16)
        kept[pl.ds(begin, lay.wide)] = value

        @pl.when((r >= 2) & (r < lay.rows + 2))
        def _():
            place = pl.multiple_of((r - 2) * lay.wide + 2 * MARGIN, 16)
            own[pl.ds(place, lay.cols)] = value[: lay.cols].astype(jnp.float32)

    weight_matmul(mixed, own, total, sent, lay, chunk)
    for d in range(second.shape[0]):
        sent[second.shape[0] + d] = second[d]


def coarse_kernel(kept, picked, main, weight, out, *, lay):
    width = weight.shape[2]
    windows = jnp.dot(picked[...], kept[...], preferred_element_type=jnp.float32)
    block_rows, block_cols = lay.rows // UPSCALE, lay.cols // UPSCALE
    blocks = block_rows * block_cols
    summed = jnp.zeros((blocks, width), jnp.float32)
    for tap in range(9):
        summed = summed + lax.dot_general(
            windows[tap * blocks : (tap + 1) * blocks],
            weight[tap // 3, tap % 3].astype(jnp.float32),
            (((1,), (1,)), ((), ())),
            precision=lax.Precision.HIGHEST,
            preferred_element_type=jnp.float32,
        )
    for bi in range(block_rows):
        rows = jnp.zeros((lay.cols, width), jnp.float32)
        for i in range(UPSCALE):
            rows = rows + main[bi * UPSCALE + i].astype(jnp.float32)
        for bj in range(block_cols):
            k = bi * block_cols + bj
            cot = jnp.sum(rows[bj * UPSCALE : (bj + 1) * UPSCALE], 0, keepdims=True)
            out[k : k + 1] = (cot + summed[k : k + 1]) / UPSCALE


def share_kernel(received, sent, *, rescale):
    total = received[0].astype(jnp.float32)
    for d in range(1, received.shape[0]):
        total = total + received[d].astype(jnp.float32)
    total = (total * rescale).astype(jnp.bfloat16)
    for d in range(sent.shape[0]):
        sent[d] = total


def join_kernel(mine, other, first, second, *, chunk, grid):
    row_devices, col_devices = grid
    half, pairs = row_devices * col_devices // 2, col_devices // 2
    core = lax.axis_index("cols") & 1
    for k in range(2):

        @pl.when(core == k)
        def _():
            for source, side in ((mine, k), (other, 1 - k)):
                for d in range(half):
                    owner = d // pairs * col_devices + d % pairs * 2 + side
                    out = first if owner < half else second
                    begin = owner % half * chunk
                    out[begin : begin + chunk] = source[d].astype(jnp.float32)[:chunk]


def window_picks(lay):
    place = np.arange(lay.kept)
    slot, column = place // lay.wide + 1, place % lay.wide
    behind = column >= lay.cols + RIM
    i = np.where(behind, slot - 2, slot - 3)
    j = np.where(behind, column - lay.wide, column)
    rows = []
    for a in range(3):
        for b in range(3):
            y, x = i + a - 1, j + b - 1
            for bi in range(lay.rows // UPSCALE):
                for bj in range(lay.cols // UPSCALE):
                    rows.append((y // UPSCALE == bi) & (x // UPSCALE == bj) & (place < lay.out))
    return jnp.asarray(np.stack(rows), jnp.bfloat16)


def to_all(payload, axis):
    return lax.all_to_all(payload, axis, 0, 0)


def among_cores(payload, row_devices, col_devices):
    groups = [
        [r * col_devices + 2 * h + k for r in range(row_devices) for h in range(col_devices // 2)]
        for k in range(2)
    ]
    return lax.all_to_all(payload, BOTH, 0, 0, axis_index_groups=groups)


def core_swap(array, col_devices):
    return lax.ppermute(array, "cols", [(c, c ^ 1) for c in range(col_devices)])


def pieces(array):
    high = array.astype(jnp.bfloat16)
    rest = array - high.astype(jnp.float32)
    middle = rest.astype(jnp.bfloat16)
    return high, middle, (rest - middle.astype(jnp.float32)).astype(jnp.bfloat16)


def lane_roll(value, shift):
    return pltpu.roll(value, shift % value.shape[1], 1)


def pack_kernel(features, labels, band, sent, sums):
    encoder_width, tile_rows, tile_cols = features.shape
    block_rows, block_cols = tile_rows // UPSCALE, tile_cols // UPSCALE
    blocks = block_rows * block_cols
    sums[...] = jnp.zeros_like(sums)
    slot = lax.broadcasted_iota(jnp.int32, (blocks, tile_cols), 0)
    column = lax.broadcasted_iota(jnp.int32, (blocks, tile_cols), 1)
    total = jnp.zeros((blocks, 128), jnp.float32)
    for r in range(block_rows):
        sums[0:encoder_width] = jnp.sum(features[:, r * UPSCALE : (r + 1) * UPSCALE], 1)
        sums[encoder_width : encoder_width + 1] = (
            labels[r * UPSCALE : r * UPSCALE + 1].astype(jnp.float32) / UPSCALE
        )
        low = (slot - r * block_cols) * UPSCALE
        picked = ((column >= low) & (column < low + UPSCALE)).astype(jnp.float32)
        total = total + lax.dot_general(
            picked,
            sums[...],
            (((1,), (1,)), ((), ())),
            precision=lax.Precision.HIGHEST,
            preferred_element_type=jnp.float32,
        )
    high, middle, low = pieces(total)
    packed = (
        high.astype(jnp.float32)
        + lane_roll(middle.astype(jnp.float32), 32)
        + lane_roll(low.astype(jnp.float32), 64)
    )
    value = jnp.concatenate([band[...].astype(jnp.float32), packed], 0).astype(jnp.bfloat16)
    for d in range(sent.shape[0]):
        sent[d] = value


def pool_kernel(mine_ref, other_ref, places, weight, pooled, valid, table, *, near, coarse):
    block_rows, block_cols = near
    coarse_rows, coarse_cols = coarse
    encoder_width = weight.shape[0]
    half, rows, _ = mine_ref.shape
    devices = 2 * half
    lane = lax.broadcasted_iota(jnp.int32, (8, 128), 1)
    for d in range(devices):
        part = mine_ref[d] if d < half else other_ref[d - half]
        packed = part.astype(jnp.float32)[rows - 8 :]
        value = packed + lane_roll(packed, -32) + lane_roll(packed, -64)
        table[d * 8 : (d + 1) * 8] = jnp.where(lane <= encoder_width, value, 0.0)
    exact = dict(precision=lax.Precision.HIGHEST, preferred_element_type=jnp.float32)
    row0 = lax.axis_index("rows") * block_rows - 1
    col0 = lax.axis_index("cols") * block_cols - 2

    def position(shape):
        q = lax.broadcasted_iota(jnp.int32, shape, 0)
        return row0 + (q >> 3), col0 + (q & 7)

    count = pooled.shape[0]
    row, col = position((count, devices * 8))
    core = lax.axis_index("cols") & 1
    column = places[1:2] + block_cols * jnp.where(places[2:3] == 1, core, 1 - core)
    chosen = ((row == places[0:1]) & (col == column)).astype(jnp.float32)
    mine = jnp.dot(chosen, table[...], **exact)[:, encoder_width : encoder_width + 1]
    pick = (lane == encoder_width).astype(jnp.float32)
    every = lax.dot_general(pick, table[...], (((1,), (1,)), ((), ())), **exact)[0:1]
    same = (mine == every).astype(jnp.float32)
    sums = jnp.dot(same, table[...], **exact)
    members = jnp.sum(same, 1, keepdims=True) * float(UPSCALE * UPSCALE)
    averages = sums / jnp.maximum(members, 1.0)
    result = jnp.dot(averages[:, :encoder_width], weight[...], **exact)
    row, col = position(pooled.shape)
    inside = (row >= 0) & (row < coarse_rows) & (col >= 0) & (col < coarse_cols)
    pooled[...] = jnp.where(inside, result, 0.0)
    valid[...] = inside.astype(jnp.float32)


def channel_conv(rows_ref, weight, shifted, out_rows, cols):
    width = weight.shape[3]
    count = out_rows * cols
    sums = None
    for a in range(3):
        left = rows_ref[a * cols : a * cols + count]
        if width % 128:
            part = [
                jnp.dot(left, weight[a, b], preferred_element_type=jnp.float32) for b in range(3)
            ]
        else:
            right = jnp.concatenate([weight[a, b] for b in range(3)], 1)
            part = jnp.dot(left, right, preferred_element_type=jnp.float32)
            part = [part[:, b * width : (b + 1) * width] for b in range(3)]
        sums = part if sums is None else [s + p for s, p in zip(sums, part)]
    shifted[...] = jnp.zeros_like(shifted)
    total = sums[1]
    for b in (0, 2):
        shifted[:, 8 : 8 + cols] = sums[b].reshape(out_rows, cols, width)
        total = total + shifted[:, 7 + b : 7 + b + cols].reshape(count, width)
    return total


def hidden_kernel(mine, other, weight, sent, rows_ref, shifted, kept, *, grid, band, direct):
    row_devices, col_devices = grid
    band_rows, cols = band
    coarse_rows = row_devices * band_rows
    width = weight.shape[3]
    rows_ref[...] = jnp.zeros_like(rows_ref)
    if direct:
        pairs = col_devices // 2
        core = lax.axis_index("cols") & 1
        for source, side in ((mine, core), (other, 1 - core)):
            for d in range(row_devices * pairs):
                begin = (1 + d // pairs * band_rows) * cols
                lanes = pl.multiple_of((d % pairs * 2 + side) * width, width)
                rows_ref[begin : begin + band_rows * cols, pl.ds(lanes, width)] = source[
                    d, : band_rows * cols
                ]
    else:
        rows_ref[cols : cols + coarse_rows * cols] = mine[...]
    raw = channel_conv(rows_ref, weight, shifted, coarse_rows, cols)
    pixels = coarse_rows * cols
    mean = jnp.sum(raw, 0, keepdims=True) / pixels
    variance = jnp.sum(raw * raw, 0, keepdims=True) / pixels - mean * mean
    hidden = jnp.maximum((raw - mean) * lax.rsqrt(variance + norm_eps), 0.0)
    kept[...] = jnp.zeros_like(kept)
    kept[2 : 2 + coarse_rows] = hidden.astype(jnp.bfloat16).reshape(coarse_rows, cols, width)
    near = kept[pl.ds(lax.axis_index("rows") * band_rows, band_rows + 4)]
    near = near.reshape((band_rows + 4) * cols, width)
    for d in range(sent.shape[0]):
        sent[d] = near


def project_kernel(
    received, weight, source, project, sent, rows_ref, shifted, residual, spread, *, grid, band,
    direct
):
    row_devices, col_devices = grid
    band_rows, cols = band
    width = weight.shape[3]
    my_col = lax.axis_index("cols")
    for c in range(col_devices):
        rows_ref[:, c * width : (c + 1) * width] = received[c]
    raw = channel_conv(rows_ref, weight, shifted, band_rows + 2, cols)
    count = (band_rows + 2) * cols
    if direct:
        residual[...] = jnp.zeros_like(residual)
        for r in range(row_devices):
            piece = source[r * (col_devices // 2) + (my_col >> 1), : band_rows * cols]
            residual[1 + r * band_rows : 1 + (r + 1) * band_rows] = piece.reshape(
                band_rows, cols, width
            )
        base = residual[pl.ds(lax.axis_index("rows") * band_rows, band_rows + 2)]
        base = base.reshape(count, width)
    else:
        base = source[...]
    result = (base.astype(jnp.float32) + raw).astype(jnp.bfloat16)
    rows = project[pl.ds(pl.multiple_of(my_col * width, width), width)]
    partial = jnp.dot(result, rows, preferred_element_type=jnp.float32)
    spread[...] = jnp.zeros_like(spread)
    spread[:, 8 : 8 + cols] = partial.reshape(band_rows + 2, cols, partial.shape[1])
    step = cols // col_devices
    for j in range(col_devices):
        sent[j] = spread[:, 6 + j * step : 6 + j * step + sent.shape[2]]


def per_device(
    global_in,
    global_first,
    global_second,
    project_weight,
    enhancer_input,
    instance_map,
    encoder_features,
    instance_weight,
    enhancer_first,
    enhancer_second,
    output_cotangent,
):
    row_devices, col_devices = lax.axis_size("rows"), lax.axis_size("cols")
    devices = row_devices * col_devices
    my_row, my_col = lax.axis_index("rows"), lax.axis_index("cols")
    band_rows, band_cols, width_share = global_in.shape
    tile_rows, tile_cols, local_width = enhancer_input.shape
    coarse_rows = band_rows * row_devices
    block_rows = tile_rows // UPSCALE
    block_cols = tile_cols // UPSCALE
    blocks = block_rows * block_cols
    encoder_width = encoder_features.shape[0]

    lay = Layout(tile_rows, tile_cols)
    width = local_width
    grid = (row_devices, col_devices)
    band = (band_rows, band_cols)
    direct = width_share == 128
    main = global_in.reshape(-1, 128)
    main_rows = main.shape[0]
    sent_input = call(
        pack_kernel,
        jax.ShapeDtypeStruct((devices // 2, main_rows + 8, 128), jnp.bfloat16),
        (encoder_features, instance_map, main),
        [pltpu.VMEM((128, tile_cols), jnp.float32)],
        far=(0, 1, 2),
        limit=62 * 1024 * 1024,
    )
    mine = among_cores(sent_input, row_devices, col_devices)
    late_input, late_cotangent, _ = lax.optimization_barrier(
        (enhancer_input, output_cotangent, sent_input)
    )
    tops = jnp.stack([late_input[-2:], late_cotangent[-2:]])
    bottoms = jnp.stack([late_input[:2], late_cotangent[:2]])

    row_up = [(i, i + 1) for i in range(row_devices - 1)]
    row_down = [(j, i) for i, j in row_up]
    col_up = [(i, i + 1) for i in range(col_devices - 1)]
    col_down = [(j, i) for i, j in col_up]
    top = lax.ppermute(tops, "rows", row_up)
    bottom = lax.ppermute(bottoms, "rows", row_down)
    both = jnp.stack([late_input, late_cotangent])
    tall_last = jnp.concatenate([top[:, :, -RIM:], both[:, :, -RIM:], bottom[:, :, -RIM:]], 1)
    tall_first = jnp.concatenate([top[:, :, :RIM], both[:, :, :RIM], bottom[:, :, :RIM]], 1)
    mine, tall_last, tall_first = lax.optimization_barrier((mine, tall_last, tall_first))
    other = core_swap(mine, col_devices)
    pixel_total = float(tile_rows * tile_cols * devices)
    chunk = 18 * width // devices
    padded_chunk = -(-chunk // 8) * 8
    square = pltpu.VMEM((3 * width, 3 * width), jnp.bfloat16)
    z = [pltpu.VMEM((lay.z, width), jnp.float32)] * 3
    own = pltpu.VMEM((lay.own + 2 * MARGIN, width), jnp.float32)
    total = pltpu.VMEM((9 * width + 64, width), jnp.float32)
    flat_shape = jax.ShapeDtypeStruct((lay.flat, width), jnp.bfloat16)
    out_shape = jax.ShapeDtypeStruct((lay.out, width), jnp.float32)
    stats_shape = jax.ShapeDtypeStruct((devices, 8, width), jnp.float32)
    sent_shape = jax.ShapeDtypeStruct((devices, padded_chunk, width), jnp.bfloat16)
    half_shape = jax.ShapeDtypeStruct((devices // 2, padded_chunk, width), jnp.bfloat16)
    conv_flops = 18 * width * width * lay.out

    place = np.arange(devices * blocks)
    owner, slot = place // blocks % (devices // 2), place % blocks
    pairs = col_devices // 2
    places = np.zeros((8, devices * blocks), np.int32)
    places[0] = owner // pairs * block_rows + slot // block_cols
    places[1] = owner % pairs * 2 * block_cols + slot % block_cols
    places[2] = place // blocks < devices // 2
    near_shape = jax.ShapeDtypeStruct(((block_rows + 2) * 8, width), jnp.float32)
    pooled, valid = call(
        pool_kernel,
        (near_shape, near_shape),
        (mine, other, jnp.asarray(places), instance_weight),
        [pltpu.VMEM((devices * 8, 128), jnp.float32)],
        near=(block_rows, block_cols),
        coarse=(coarse_rows, band_cols),
    )
    channels = width_share * col_devices
    if direct:
        sources, base = (mine, other), mine
    else:
        even = my_col % 2 == 0
        sides = [jnp.where(even, mine, other), jnp.where(even, other, mine)]
        gathered = jnp.stack([side[:, :main_rows] for side in sides], 1).reshape(
            row_devices, col_devices, band_rows, band_cols, width_share
        )
        source = gathered.transpose(0, 2, 3, 1, 4).reshape(coarse_rows * band_cols, channels)
        sources = (source, source)
        column = lax.dynamic_index_in_dim(gathered, my_col, 1, keepdims=False)
        column = jnp.pad(
            column.reshape(coarse_rows, band_cols, width_share), ((1, 1), (0, 0), (0, 0))
        )
        base = lax.dynamic_slice_in_dim(column, my_row * band_rows, band_rows + 2, 0)
        base = base.reshape(-1, width_share)
    near_rows = band_rows + 4
    sent_hidden = call(
        hidden_kernel,
        jax.ShapeDtypeStruct((col_devices, near_rows * band_cols, width_share), jnp.bfloat16),
        (*sources, global_first),
        [
            pltpu.VMEM(((coarse_rows + 2) * band_cols, channels), jnp.bfloat16),
            pltpu.VMEM((coarse_rows, band_cols + 16, width_share), jnp.float32),
            pltpu.VMEM((coarse_rows + 4, band_cols, width_share), jnp.bfloat16),
        ],
        18 * coarse_rows * band_cols * channels * width_share,
        far_out=(0,),
        grid=grid,
        band=band,
        direct=direct,
    )
    near_hidden = to_all(sent_hidden, "cols")
    tall_last, tall_first, _ = lax.optimization_barrier((tall_last, tall_first, sent_hidden))
    left = lax.ppermute(tall_last, "cols", col_up)
    right = lax.ppermute(tall_first, "cols", col_down)
    strip = jnp.concatenate(
        [
            jnp.pad(right, ((0, 0), (1, 0), (0, 0), (0, 0))),
            jnp.pad(left, ((0, 0), (0, 1), (0, 0), (0, 0))),
        ],
        2,
    )
    act_grad = call(
        cot_kernel,
        jax.ShapeDtypeStruct((lay.out, width), jnp.bfloat16),
        (output_cotangent, top, bottom, strip, enhancer_second),
        [pltpu.VMEM((lay.flat, width), jnp.bfloat16), square, *z],
        conv_flops,
        pick={1: 1, 2: 1, 3: 1},
        lay=lay,
    )

    sent_coarse = call(
        project_kernel,
        jax.ShapeDtypeStruct((col_devices, band_rows + 2, 8, width), jnp.float32),
        (near_hidden, global_second, base, project_weight),
        [
            pltpu.VMEM((near_rows * band_cols, channels), jnp.bfloat16),
            pltpu.VMEM((band_rows + 2, band_cols + 16, width_share), jnp.float32),
            pltpu.VMEM((coarse_rows + 2, band_cols, width_share), jnp.bfloat16),
            pltpu.VMEM((band_rows + 2, band_cols + 16, width), jnp.float32),
        ],
        18 * (band_rows + 2) * band_cols * channels * width_share,
        far_out=(0,),
        grid=grid,
        band=band,
        direct=direct,
    )
    near_coarse = to_all(sent_coarse, "cols")
    terms = (near_coarse, pooled.reshape(-1, 8, width), valid.reshape(-1, 8, width))

    mixed, first_act, stats = call(
        mixed_kernel,
        (flat_shape, out_shape, stats_shape),
        (enhancer_input, top, bottom, strip, *terms, enhancer_first),
        [square, pltpu.VMEM((block_rows + 2, 8, width), jnp.float32), *z],
        conv_flops,
        pick={1: 0, 2: 0, 3: 0},
        far_out=(2,),
        lay=lay,
    )
    stats = to_all(stats, BOTH)
    grad_stats = call(
        norm_kernel,
        stats_shape,
        (first_act, stats, act_grad),
        far_out=(0,),
        lay=lay,
        pixel_total=pixel_total,
    )
    grad_stats = to_all(grad_stats, BOTH)
    enhanced, second_sent = call(
        second_kernel,
        (jax.ShapeDtypeStruct((tile_rows, tile_cols, width), jnp.bfloat16), half_shape),
        (first_act, stats, mixed, output_cotangent, enhancer_second),
        [pltpu.VMEM((lay.flat, width), jnp.bfloat16), square, *z, own, total],
        2 * conv_flops,
        lay=lay,
        chunk=chunk,
        grid=grid,
        pixel_total=pixel_total,
    )
    sent_both, kept = call(
        first_kernel,
        (sent_shape, jax.ShapeDtypeStruct((lay.kept, width), jnp.bfloat16)),
        (stats, grad_stats, first_act, act_grad, mixed, second_sent),
        [own, total],
        conv_flops,
        far_out=(0,),
        lay=lay,
        grid=grid,
        chunk=chunk,
        pixel_total=pixel_total,
    )
    part = to_all(sent_both, BOTH)
    rescale = 1.0 / math.sqrt(pixel_total)
    global_gradient = call(
        coarse_kernel,
        jax.ShapeDtypeStruct((blocks, width), jnp.float32),
        (kept, window_picks(lay), output_cotangent, enhancer_first),
        (),
        lay=lay,
    )
    part, global_gradient = lax.optimization_barrier((part, global_gradient))
    share = call(share_kernel, half_shape, (part,), rescale=rescale)
    share = among_cores(share, row_devices, col_devices)
    shares = (share, core_swap(share, col_devices))
    whole_shape = jax.ShapeDtypeStruct((9 * width, width), jnp.float32)
    first_total, second_total = call(
        join_kernel, (whole_shape, whole_shape), shares, chunk=chunk, grid=grid
    )
    return (
        enhanced,
        first_total.reshape(3, 3, width, width),
        second_total.reshape(3, 3, width, width),
        global_gradient.reshape(block_rows, block_cols, width),
    )


def solution(mesh):
    return jax.shard_map(
        per_device,
        mesh=mesh,
        in_specs=(
            P("rows", None, "cols"),
            P(None, None, None, "cols"),
            P(None, None, None, "cols"),
            P(),
            P("rows", "cols", None),
            P("rows", "cols"),
            P(None, "rows", "cols"),
            P(),
            P(),
            P(),
            P("rows", "cols", None),
        ),
        out_specs=(P("rows", "cols", None), P(), P(), P("rows", "cols", None)),
        check_vma=False,
    )
```

```python
import math

import jax
import jax.numpy as jnp
import numpy as np
from jax import lax
from jax.experimental import pallas as pl
from jax.experimental.pallas import tpu as pltpu
from jax.sharding import PartitionSpec as P

INSTANCES = 256
UPSCALE = 16
BOTH = ("rows", "cols")

norm_eps = 1e-05


RIM = 8
MARGIN = 16
KERNEL_VMEM = 20 * 1024 * 1024


class Layout:
    def __init__(self, tile_rows, tile_cols):
        self.rows, self.cols = tile_rows, tile_cols
        self.wide = tile_cols + 2 * RIM
        self.flat = (tile_rows + 6) * self.wide + 2 * MARGIN
        self.out_rows = tile_rows + 3
        self.out = self.out_rows * self.wide
        self.z = self.out + 2 * MARGIN
        self.own = tile_rows * self.wide + 2 * MARGIN
        self.kept = -(-self.out // 128) * 128


def call(
    body, outs, ins, scratch=(), flops=0, far=(), stream=None, pick=None, far_out=(),
    limit=KERNEL_VMEM, **fixed
):
    pick = pick or {}
    single = not isinstance(outs, tuple)
    outs = (outs,) if single else outs
    n_in, n_out, n_own = len(ins), len(outs), len(scratch)
    near = pl.BlockSpec(memory_space=pltpu.VMEM)
    hbm = pl.BlockSpec(memory_space=pltpu.MemorySpace.HBM)
    landing = [pltpu.VMEM(ins[i].shape, ins[i].dtype) for i in far]
    flow = [] if stream is None else [pltpu.VMEM(ins[stream].shape, ins[stream].dtype)]
    parts = 0 if stream is None else ins[stream].shape[0]
    leaving = [pltpu.VMEM(outs[j].shape, outs[j].dtype) for j in far_out]

    def kernel(*refs):
        in_refs, out_refs = list(refs[:n_in]), list(refs[n_in : n_in + n_out])
        rest = refs[n_in + n_out :]
        own, rest = rest[:n_own], rest[n_own:]
        buffers, sems = rest[: len(far) + len(far_out)], rest[len(far) + len(far_out) :]
        sems, flow_sems = sems[: len(far) + len(far_out)], sems[len(far) + len(far_out) :]
        extra, flowing = {}, []
        if stream is not None:
            target, flow_sems = flow_sems[0], flow_sems[1:]
            for k in range(parts):
                flowing.append(
                    pltpu.make_async_copy(in_refs[stream].at[k], target.at[k], flow_sems[k])
                )
            in_refs[stream] = target
            extra["arrive"] = lambda k: flowing[k].wait()
        starts, results = [], []
        for slot, i in enumerate(far):
            starts.append(pltpu.make_async_copy(in_refs[i], buffers[slot], sems[slot]))
            starts[-1].start()
            in_refs[i] = buffers[slot]
        for copy in flowing:
            copy.start()
        for slot, j in enumerate(far_out, len(far)):
            results.append((buffers[slot], out_refs[j], sems[slot]))
            out_refs[j] = buffers[slot]
        for i, k in pick.items():
            in_refs[i] = in_refs[i].at[k]
        for copy in starts:
            copy.wait()
        body(*in_refs, *out_refs, *own, **fixed, **extra)
        ends = [pltpu.make_async_copy(*triple) for triple in results]
        for copy in ends:
            copy.start()
        for copy in ends:
            copy.wait()

    result = pl.pallas_call(
        kernel,
        out_shape=outs,
        in_specs=[hbm if i in far or i == stream else near for i in range(n_in)],
        out_specs=tuple(hbm if j in far_out else near for j in range(n_out)),
        scratch_shapes=[
            *scratch,
            *landing,
            *leaving,
            *[pltpu.SemaphoreType.DMA] * (len(landing) + len(leaving)),
            *flow,
            *[pltpu.SemaphoreType.DMA] * parts,
        ],
        compiler_params=pltpu.CompilerParams(vmem_limit_bytes=limit),
        cost_estimate=pl.CostEstimate(flops=flops, bytes_accessed=4 << 20, transcendentals=0),
        name=body.__name__,
    )(*ins)
    return result[0] if single else result


def put_tiles(flat_ref, lay, main_ref, top_ref, bottom_ref, strip_ref):
    flat_ref[...] = jnp.zeros_like(flat_ref)
    for k in range(lay.rows + 5):
        base = MARGIN + k * lay.wide
        i = k - 3
        if i >= -2:
            if i < 0:
                row = top_ref[i + 2]
            elif i < lay.rows:
                row = main_ref[i]
            else:
                row = bottom_ref[i - lay.rows]
            flat_ref[base : base + lay.cols] = row
        flat_ref[base + lay.cols : base + lay.wide] = strip_ref[k]


def taps_matmul(flat_ref, square_ref, z_refs, lay, turned):
    count = z_refs[0].shape[0]
    chunks = 3
    step = count // chunks
    width = z_refs[0].shape[1]

    @pl.loop(0, chunks)
    def _(c):
        begin = pl.multiple_of(c * step, 16)
        parts = [flat_ref[pl.ds(begin + shift, step)] for shift in (0, lay.wide, 2 * lay.wide)]
        if turned:
            left = jnp.concatenate(parts[::-1], 1)
            result = lax.dot_general(
                left, square_ref[...], (((1,), (1,)), ((), ())), preferred_element_type=jnp.float32
            )
        else:
            left = jnp.concatenate(parts, 1)
            result = jnp.dot(left, square_ref[...], preferred_element_type=jnp.float32)
        for b in range(3):
            z_refs[b][pl.ds(begin, step)] = result[:, b * width : (b + 1) * width]


def put_square(square_ref, weight_ref, turned):
    width = weight_ref.shape[2]
    for a in range(3):
        for b in range(3):
            r, c = (b, a) if turned else (a, b)
            square_ref[r * width : (r + 1) * width, c * width : (c + 1) * width] = weight_ref[a, b]


def taken(z_refs, begin, count, turned):
    early, late = (2, 0) if turned else (0, 2)
    return (
        z_refs[early][pl.ds(begin + MARGIN - 1, count)]
        + z_refs[1][pl.ds(begin + MARGIN, count)]
        + z_refs[late][pl.ds(begin + MARGIN + 1, count)]
    )


def folded(value):
    return value.reshape(-1, 8, value.shape[-1]).sum(0)


def send_stats(out_ref, first, second):
    sums = jnp.concatenate(
        [jnp.sum(first, 0, keepdims=True), jnp.sum(second, 0, keepdims=True)], 0
    )
    out_ref[...] = jnp.zeros_like(out_ref)
    for d in range(out_ref.shape[0]):
        out_ref[d, 0:2] = sums


def cot_kernel(main, top, bottom, strip, weight, grad_out, flat, square, z0, z1, z2, *, lay):
    put_tiles(flat, lay, main, top, bottom, strip)
    put_square(square, weight, True)
    taps_matmul(flat, square, (z0, z1, z2), lay, True)

    @pl.loop(0, lay.out_rows)
    def _(r):
        begin = pl.multiple_of(r * lay.wide, 16)
        value = taken((z0, z1, z2), begin, lay.wide, True)
        grad_out[pl.ds(begin, lay.wide)] = value.astype(jnp.bfloat16)


def mixed_kernel(
    main, top, bottom, strip, coarse, pooled, valid, weight, flat, act_out, stats, square, terms, z0,
    z1, z2, *, lay
):
    width = main.shape[2]
    flat[...] = jnp.zeros_like(flat)
    blocks = lay.cols // UPSCALE
    near = coarse[0]
    for c in range(1, coarse.shape[0]):
        near = near + coarse[c]
    terms[...] = near.astype(jnp.bfloat16).astype(jnp.float32) * valid[...] + pooled[...]
    for k in range(lay.rows + 5):
        base = MARGIN + k * lay.wide
        i = k - 3
        own, following = (i + UPSCALE) // UPSCALE, (i + 1 + UPSCALE) // UPSCALE

        def spread(block_row, block_col, rows):
            return jnp.broadcast_to(
                terms[block_row, block_col : block_col + 1], (rows, width)
            )

        if i >= -2:
            if i < 0:
                row = top[i + 2]
            elif i < lay.rows:
                row = main[i]
            else:
                row = bottom[i - lay.rows]
            added = jnp.concatenate([spread(own, b + 2, UPSCALE) for b in range(blocks)], 0)
            flat[base : base + lay.cols] = (row.astype(jnp.float32) + added).astype(jnp.bfloat16)
        zero = jnp.zeros((RIM, width), jnp.float32)
        right = spread(own, blocks + 2, RIM) if i >= -2 else zero
        left = spread(following, 1, RIM) if i + 1 < lay.rows + 2 else zero
        flat[base + lay.cols : base + lay.wide] = (
            strip[k].astype(jnp.float32) + jnp.concatenate([right, left], 0)
        ).astype(jnp.bfloat16)
    put_square(square, weight, False)
    taps_matmul(flat, square, (z0, z1, z2), lay, False)

    def step(r, sums):
        begin = pl.multiple_of(r * lay.wide, 16)
        value = taken((z0, z1, z2), begin, lay.wide, False)
        act_out[pl.ds(begin, lay.wide)] = value
        mine = ((r >= 2) & (r < lay.rows + 2)).astype(jnp.float32)
        own_value = value[: lay.cols] * mine
        return sums[0] + folded(own_value), sums[1] + folded(own_value * own_value)

    zero = jnp.zeros((8, width), jnp.float32)
    sums = lax.fori_loop(0, lay.out_rows, step, (zero, zero))
    send_stats(stats, *sums)


def act_moments(stats, pixel_total):
    sums = jnp.sum(stats[...], 0)
    mean = sums[0:1] / pixel_total
    return mean, lax.rsqrt(sums[1:2] / pixel_total - mean * mean + norm_eps)


def inside_masks(lay, width, row_devices, col_devices):
    my_row, my_col = lax.axis_index("rows"), lax.axis_index("cols")
    column = lax.broadcasted_iota(jnp.int32, (lay.wide, width), 0)
    has_right = (my_col < col_devices - 1).astype(jnp.float32)
    has_left = (my_col > 0).astype(jnp.float32)
    near = jnp.where(
        column < lay.cols, 1.0, jnp.where(column < lay.cols + RIM, has_right, 0.0)
    )
    following = jnp.where(column >= lay.cols + RIM, has_left, 0.0)

    def row_inside(i):
        row = my_row * lay.rows + i
        return ((row >= 0) & (row < lay.rows * row_devices)).astype(jnp.float32)

    return lambda r: near * row_inside(r - 2) + following * row_inside(r - 1)


def gated(value):
    gate = 1.0 / (1.0 + jnp.exp(-value))
    return gate, gate * (1.0 + value * (1.0 - gate))


def norm_kernel(act, stats, act_grad, grad_stats, *, lay, pixel_total):
    width = act.shape[1]
    mean, inverse = act_moments(stats, pixel_total)

    def step(i, sums):
        begin = pl.multiple_of((i + 2) * lay.wide, 16)
        normed = (act[pl.ds(begin, lay.cols)] - mean) * inverse
        _, slope = gated(normed)
        grad = act_grad[pl.ds(begin, lay.cols)].astype(jnp.float32) * slope
        return sums[0] + folded(grad), sums[1] + folded(grad * normed)

    zero = jnp.zeros((8, width), jnp.float32)
    sums = lax.fori_loop(0, lay.rows, step, (zero, zero))
    send_stats(grad_stats, *sums)


def weight_matmul(flat_ref, own_ref, total_ref, sent_ref, lay, chunk):
    count = lay.own
    first = MARGIN + 3 * lay.wide - MARGIN
    chunks = 3
    step = count // chunks
    width = own_ref.shape[1]
    total = None
    for c in range(chunks):
        begin = c * step
        left = jnp.concatenate(
            [
                flat_ref[first + begin + a * lay.wide : first + begin + a * lay.wide + step]
                for a in (-1, 0, 1)
            ],
            1,
        )
        right = jnp.concatenate(
            [
                own_ref[MARGIN + begin - b : MARGIN + begin - b + step].astype(jnp.bfloat16)
                for b in (-1, 0, 1)
            ],
            1,
        )
        part = lax.dot_general(
            left, right, (((0,), (0,)), ((), ())), preferred_element_type=jnp.float32
        )
        total = part if total is None else total + part
    for a in range(3):
        for b in range(3):
            total_ref[(a * 3 + b) * width : (a * 3 + b + 1) * width] = total[
                a * width : (a + 1) * width, b * width : (b + 1) * width
            ]
    padded = sent_ref.shape[1]
    for d in range(9 * width // chunk):
        sent_ref[d] = total_ref[d * chunk : d * chunk + padded].astype(jnp.bfloat16)


def activate(activated, act, stats, lay, grid, pixel_total):
    width = act.shape[1]
    mean, inverse = act_moments(stats, pixel_total)
    mask = inside_masks(lay, width, *grid)
    activated[...] = jnp.zeros_like(activated)

    @pl.loop(0, lay.out_rows)
    def _(r):
        begin = pl.multiple_of(r * lay.wide, 16)
        normed = (act[pl.ds(begin, lay.wide)] - mean) * inverse
        gate, _ = gated(normed)
        activated[pl.ds(pl.multiple_of(begin + MARGIN + lay.wide, 16), lay.wide)] = (
            normed * gate * mask(r)
        ).astype(jnp.bfloat16)


def second_kernel(
    act, stats, main, sent, activated, own, total, *, lay, chunk, grid, pixel_total
):
    activate(activated, act, stats, lay, grid, pixel_total)
    own[...] = jnp.zeros_like(own)

    @pl.loop(0, lay.rows)
    def _(i):
        place = pl.multiple_of(i * lay.wide + 2 * MARGIN, 16)
        own[pl.ds(place, lay.cols)] = main[i].astype(jnp.float32)

    weight_matmul(activated, own, total, sent, lay, chunk)


def enhanced_kernel(
    act, stats, mixed, weight, enhanced, activated, square, z0, z1, z2, *, lay, grid, pixel_total
):
    activate(activated, act, stats, lay, grid, pixel_total)
    put_square(square, weight, False)
    taps_matmul(activated, square, (z0, z1, z2), lay, False)

    @pl.loop(0, lay.rows)
    def _(i):
        begin = pl.multiple_of((i + 2) * lay.wide, 16)
        value = taken((z0, z1, z2), begin, lay.cols, False)
        place = pl.multiple_of((i + 3) * lay.wide + MARGIN, 16)
        enhanced[i] = (mixed[pl.ds(place, lay.cols)].astype(jnp.float32) + value).astype(
            jnp.bfloat16
        )


def first_kernel(
    stats, grad_stats, act, act_grad, mixed, second, sent, kept, own, total, *, lay, grid,
    chunk, pixel_total
):
    width = act.shape[1]
    mean, inverse = act_moments(stats, pixel_total)
    sums = jnp.sum(grad_stats[...], 0)
    grad_mean, cross_mean = sums[0:1] / pixel_total, sums[1:2] / pixel_total
    mask = inside_masks(lay, width, *grid)
    own[...] = jnp.zeros_like(own)
    kept[...] = jnp.zeros_like(kept)

    @pl.loop(0, lay.out_rows)
    def _(r):
        begin = pl.multiple_of(r * lay.wide, 16)
        normed = (act[pl.ds(begin, lay.wide)] - mean) * inverse
        _, slope = gated(normed)
        grad = act_grad[pl.ds(begin, lay.wide)].astype(jnp.float32) * slope
        value = inverse * (grad - grad_mean - normed * cross_mean)
        value = (value * mask(r)).astype(jnp.bfloat16)
        kept[pl.ds(begin, lay.wide)] = value

        @pl.when((r >= 2) & (r < lay.rows + 2))
        def _():
            place = pl.multiple_of((r - 2) * lay.wide + 2 * MARGIN, 16)
            own[pl.ds(place, lay.cols)] = value[: lay.cols].astype(jnp.float32)

    weight_matmul(mixed, own, total, sent, lay, chunk)
    for d in range(second.shape[0]):
        sent[second.shape[0] + d] = second[d]


def coarse_kernel(kept, picked, main, weight, out, *, lay):
    width = weight.shape[2]
    windows = jnp.dot(picked[...], kept[...], preferred_element_type=jnp.float32)
    block_rows, block_cols = lay.rows // UPSCALE, lay.cols // UPSCALE
    blocks = block_rows * block_cols
    summed = jnp.zeros((blocks, width), jnp.float32)
    for tap in range(9):
        summed = summed + lax.dot_general(
            windows[tap * blocks : (tap + 1) * blocks],
            weight[tap // 3, tap % 3].astype(jnp.float32),
            (((1,), (1,)), ((), ())),
            precision=lax.Precision.HIGHEST,
            preferred_element_type=jnp.float32,
        )
    for bi in range(block_rows):
        rows = jnp.zeros((lay.cols, width), jnp.float32)
        for i in range(UPSCALE):
            rows = rows + main[bi * UPSCALE + i].astype(jnp.float32)
        for bj in range(block_cols):
            k = bi * block_cols + bj
            cot = jnp.sum(rows[bj * UPSCALE : (bj + 1) * UPSCALE], 0, keepdims=True)
            out[k : k + 1] = (cot + summed[k : k + 1]) / UPSCALE


def share_kernel(received, sent, *, rescale):
    total = received[0].astype(jnp.float32)
    for d in range(1, received.shape[0]):
        total = total + received[d].astype(jnp.float32)
    total = (total * rescale).astype(jnp.bfloat16)
    for d in range(sent.shape[0]):
        sent[d] = total


def join_kernel(mine, other, first, second, *, chunk, grid):
    row_devices, col_devices = grid
    half, pairs = row_devices * col_devices // 2, col_devices // 2
    core = lax.axis_index("cols") & 1
    for k in range(2):

        @pl.when(core == k)
        def _():
            for source, side in ((mine, k), (other, 1 - k)):
                for d in range(half):
                    owner = d // pairs * col_devices + d % pairs * 2 + side
                    out = first if owner < half else second
                    begin = owner % half * chunk
                    out[begin : begin + chunk] = source[d].astype(jnp.float32)[:chunk]


def window_picks(lay):
    place = np.arange(lay.kept)
    slot, column = place // lay.wide + 1, place % lay.wide
    behind = column >= lay.cols + RIM
    i = np.where(behind, slot - 2, slot - 3)
    j = np.where(behind, column - lay.wide, column)
    rows = []
    for a in range(3):
        for b in range(3):
            y, x = i + a - 1, j + b - 1
            for bi in range(lay.rows // UPSCALE):
                for bj in range(lay.cols // UPSCALE):
                    rows.append((y // UPSCALE == bi) & (x // UPSCALE == bj) & (place < lay.out))
    return jnp.asarray(np.stack(rows), jnp.bfloat16)


def to_all(payload, axis):
    return lax.all_to_all(payload, axis, 0, 0)


def among_cores(payload, row_devices, col_devices):
    groups = [
        [r * col_devices + 2 * h + k for r in range(row_devices) for h in range(col_devices // 2)]
        for k in range(2)
    ]
    return lax.all_to_all(payload, BOTH, 0, 0, axis_index_groups=groups)


def core_swap(array, col_devices):
    return lax.ppermute(array, "cols", [(c, c ^ 1) for c in range(col_devices)])


def pieces(array):
    high = array.astype(jnp.bfloat16)
    rest = array - high.astype(jnp.float32)
    middle = rest.astype(jnp.bfloat16)
    return high, middle, (rest - middle.astype(jnp.float32)).astype(jnp.bfloat16)


def lane_roll(value, shift):
    return pltpu.roll(value, shift % value.shape[1], 1)


def pack_kernel(features, labels, band, sent, sums):
    encoder_width, tile_rows, tile_cols = features.shape
    block_rows, block_cols = tile_rows // UPSCALE, tile_cols // UPSCALE
    blocks = block_rows * block_cols
    sums[...] = jnp.zeros_like(sums)
    slot = lax.broadcasted_iota(jnp.int32, (blocks, tile_cols), 0)
    column = lax.broadcasted_iota(jnp.int32, (blocks, tile_cols), 1)
    total = jnp.zeros((blocks, 128), jnp.float32)
    for r in range(block_rows):
        sums[0:encoder_width] = jnp.sum(features[:, r * UPSCALE : (r + 1) * UPSCALE], 1)
        sums[encoder_width : encoder_width + 1] = (
            labels[r * UPSCALE : r * UPSCALE + 1].astype(jnp.float32) / UPSCALE
        )
        low = (slot - r * block_cols) * UPSCALE
        picked = ((column >= low) & (column < low + UPSCALE)).astype(jnp.float32)
        total = total + lax.dot_general(
            picked,
            sums[...],
            (((1,), (1,)), ((), ())),
            precision=lax.Precision.HIGHEST,
            preferred_element_type=jnp.float32,
        )
    high, middle, low = pieces(total)
    packed = (
        high.astype(jnp.float32)
        + lane_roll(middle.astype(jnp.float32), 32)
        + lane_roll(low.astype(jnp.float32), 64)
    )
    value = jnp.concatenate([band[...].astype(jnp.float32), packed], 0).astype(jnp.bfloat16)
    for d in range(sent.shape[0]):
        sent[d] = value


def pool_kernel(mine_ref, other_ref, places, weight, pooled, valid, table, *, near, coarse):
    block_rows, block_cols = near
    coarse_rows, coarse_cols = coarse
    encoder_width = weight.shape[0]
    half, rows, _ = mine_ref.shape
    devices = 2 * half
    lane = lax.broadcasted_iota(jnp.int32, (8, 128), 1)
    for d in range(devices):
        part = mine_ref[d] if d < half else other_ref[d - half]
        packed = part.astype(jnp.float32)[rows - 8 :]
        value = packed + lane_roll(packed, -32) + lane_roll(packed, -64)
        table[d * 8 : (d + 1) * 8] = jnp.where(lane <= encoder_width, value, 0.0)
    exact = dict(precision=lax.Precision.HIGHEST, preferred_element_type=jnp.float32)
    row0 = lax.axis_index("rows") * block_rows - 1
    col0 = lax.axis_index("cols") * block_cols - 2

    def position(shape):
        q = lax.broadcasted_iota(jnp.int32, shape, 0)
        return row0 + (q >> 3), col0 + (q & 7)

    count = pooled.shape[0]
    row, col = position((count, devices * 8))
    core = lax.axis_index("cols") & 1
    column = places[1:2] + block_cols * jnp.where(places[2:3] == 1, core, 1 - core)
    chosen = ((row == places[0:1]) & (col == column)).astype(jnp.float32)
    mine = jnp.dot(chosen, table[...], **exact)[:, encoder_width : encoder_width + 1]
    pick = (lane == encoder_width).astype(jnp.float32)
    every = lax.dot_general(pick, table[...], (((1,), (1,)), ((), ())), **exact)[0:1]
    same = (mine == every).astype(jnp.float32)
    sums = jnp.dot(same, table[...], **exact)
    members = jnp.sum(same, 1, keepdims=True) * float(UPSCALE * UPSCALE)
    averages = sums / jnp.maximum(members, 1.0)
    result = jnp.dot(averages[:, :encoder_width], weight[...], **exact)
    row, col = position(pooled.shape)
    inside = (row >= 0) & (row < coarse_rows) & (col >= 0) & (col < coarse_cols)
    pooled[...] = jnp.where(inside, result, 0.0)
    valid[...] = inside.astype(jnp.float32)


def channel_conv(rows_ref, weight, shifted, out_rows, cols, arrive=None):
    width = weight.shape[3]
    count = out_rows * cols
    sums = None
    for a in range(3):
        left = rows_ref[a * cols : a * cols + count]
        if arrive is not None:
            arrive(a)
        if width % 128:
            part = [
                jnp.dot(left, weight[a, b], preferred_element_type=jnp.float32) for b in range(3)
            ]
        else:
            right = jnp.concatenate([weight[a, b] for b in range(3)], 1)
            part = jnp.dot(left, right, preferred_element_type=jnp.float32)
            part = [part[:, b * width : (b + 1) * width] for b in range(3)]
        sums = part if sums is None else [s + p for s, p in zip(sums, part)]
    shifted[...] = jnp.zeros_like(shifted)
    total = sums[1]
    for b in (0, 2):
        shifted[:, 8 : 8 + cols] = sums[b].reshape(out_rows, cols, width)
        total = total + shifted[:, 7 + b : 7 + b + cols].reshape(count, width)
    return total


def hidden_kernel(mine, other, weight, sent, rows_ref, shifted, kept, *, grid, band, direct):
    row_devices, col_devices = grid
    band_rows, cols = band
    coarse_rows = row_devices * band_rows
    width = weight.shape[3]
    rows_ref[...] = jnp.zeros_like(rows_ref)
    if direct:
        pairs = col_devices // 2
        core = lax.axis_index("cols") & 1
        for source, side in ((mine, core), (other, 1 - core)):
            for d in range(row_devices * pairs):
                begin = (1 + d // pairs * band_rows) * cols
                lanes = pl.multiple_of((d % pairs * 2 + side) * width, width)
                rows_ref[begin : begin + band_rows * cols, pl.ds(lanes, width)] = source[
                    d, : band_rows * cols
                ]
    else:
        rows_ref[cols : cols + coarse_rows * cols] = mine[...]
    raw = channel_conv(rows_ref, weight, shifted, coarse_rows, cols)
    pixels = coarse_rows * cols
    mean = jnp.sum(raw, 0, keepdims=True) / pixels
    variance = jnp.sum(raw * raw, 0, keepdims=True) / pixels - mean * mean
    hidden = jnp.maximum((raw - mean) * lax.rsqrt(variance + norm_eps), 0.0)
    kept[...] = jnp.zeros_like(kept)
    kept[2 : 2 + coarse_rows] = hidden.astype(jnp.bfloat16).reshape(coarse_rows, cols, width)
    near = kept[pl.ds(lax.axis_index("rows") * band_rows, band_rows + 4)]
    near = near.reshape((band_rows + 4) * cols, width)
    for d in range(sent.shape[0]):
        sent[d] = near


def project_kernel(
    received, weight, source, project, sent, rows_ref, shifted, residual, spread, *, grid, band,
    direct, arrive
):
    row_devices, col_devices = grid
    band_rows, cols = band
    width = weight.shape[3]
    my_col = lax.axis_index("cols")
    for c in range(col_devices):
        rows_ref[:, c * width : (c + 1) * width] = received[c]
    raw = channel_conv(rows_ref, weight, shifted, band_rows + 2, cols, arrive)
    count = (band_rows + 2) * cols
    if direct:
        residual[...] = jnp.zeros_like(residual)
        for r in range(row_devices):
            piece = source[r * (col_devices // 2) + (my_col >> 1), : band_rows * cols]
            residual[1 + r * band_rows : 1 + (r + 1) * band_rows] = piece.reshape(
                band_rows, cols, width
            )
        base = residual[pl.ds(lax.axis_index("rows") * band_rows, band_rows + 2)]
        base = base.reshape(count, width)
    else:
        base = source[...]
    result = (base.astype(jnp.float32) + raw).astype(jnp.bfloat16)
    rows = project[pl.ds(pl.multiple_of(my_col * width, width), width)]
    partial = jnp.dot(result, rows, preferred_element_type=jnp.float32)
    spread[...] = jnp.zeros_like(spread)
    spread[:, 8 : 8 + cols] = partial.reshape(band_rows + 2, cols, partial.shape[1])
    step = cols // col_devices
    for j in range(col_devices):
        sent[j] = spread[:, 6 + j * step : 6 + j * step + sent.shape[2]]


def per_device(
    global_in,
    global_first,
    global_second,
    project_weight,
    enhancer_input,
    instance_map,
    encoder_features,
    instance_weight,
    enhancer_first,
    enhancer_second,
    output_cotangent,
):
    row_devices, col_devices = lax.axis_size("rows"), lax.axis_size("cols")
    devices = row_devices * col_devices
    my_row, my_col = lax.axis_index("rows"), lax.axis_index("cols")
    band_rows, band_cols, width_share = global_in.shape
    tile_rows, tile_cols, local_width = enhancer_input.shape
    coarse_rows = band_rows * row_devices
    block_rows = tile_rows // UPSCALE
    block_cols = tile_cols // UPSCALE
    blocks = block_rows * block_cols
    encoder_width = encoder_features.shape[0]

    lay = Layout(tile_rows, tile_cols)
    width = local_width
    grid = (row_devices, col_devices)
    band = (band_rows, band_cols)
    direct = width_share == 128
    main = global_in.reshape(-1, 128)
    main_rows = main.shape[0]
    sent_input = call(
        pack_kernel,
        jax.ShapeDtypeStruct((devices // 2, main_rows + 8, 128), jnp.bfloat16),
        (encoder_features, instance_map, main),
        [pltpu.VMEM((128, tile_cols), jnp.float32)],
        far=(0, 1, 2),
        limit=62 * 1024 * 1024,
    )
    mine = among_cores(sent_input, row_devices, col_devices)
    late_input, late_cotangent, _ = lax.optimization_barrier(
        (enhancer_input, output_cotangent, sent_input)
    )
    tops = jnp.stack([late_input[-2:], late_cotangent[-2:]])
    bottoms = jnp.stack([late_input[:2], late_cotangent[:2]])

    row_up = [(i, i + 1) for i in range(row_devices - 1)]
    row_down = [(j, i) for i, j in row_up]
    col_up = [(i, i + 1) for i in range(col_devices - 1)]
    col_down = [(j, i) for i, j in col_up]
    top = lax.ppermute(tops, "rows", row_up)
    bottom = lax.ppermute(bottoms, "rows", row_down)
    both = jnp.stack([late_input, late_cotangent])
    tall_last = jnp.concatenate([top[:, :, -RIM:], both[:, :, -RIM:], bottom[:, :, -RIM:]], 1)
    tall_first = jnp.concatenate([top[:, :, :RIM], both[:, :, :RIM], bottom[:, :, :RIM]], 1)
    mine, tall_last, tall_first = lax.optimization_barrier((mine, tall_last, tall_first))
    other = core_swap(mine, col_devices)
    pixel_total = float(tile_rows * tile_cols * devices)
    chunk = 18 * width // devices
    padded_chunk = -(-chunk // 8) * 8
    square = pltpu.VMEM((3 * width, 3 * width), jnp.bfloat16)
    z = [pltpu.VMEM((lay.z, width), jnp.float32)] * 3
    own = pltpu.VMEM((lay.own + 2 * MARGIN, width), jnp.float32)
    total = pltpu.VMEM((9 * width + 64, width), jnp.float32)
    flat_shape = jax.ShapeDtypeStruct((lay.flat, width), jnp.bfloat16)
    out_shape = jax.ShapeDtypeStruct((lay.out, width), jnp.float32)
    stats_shape = jax.ShapeDtypeStruct((devices, 8, width), jnp.float32)
    sent_shape = jax.ShapeDtypeStruct((devices, padded_chunk, width), jnp.bfloat16)
    half_shape = jax.ShapeDtypeStruct((devices // 2, padded_chunk, width), jnp.bfloat16)
    conv_flops = 18 * width * width * lay.out

    place = np.arange(devices * blocks)
    owner, slot = place // blocks % (devices // 2), place % blocks
    pairs = col_devices // 2
    places = np.zeros((8, devices * blocks), np.int32)
    places[0] = owner // pairs * block_rows + slot // block_cols
    places[1] = owner % pairs * 2 * block_cols + slot % block_cols
    places[2] = place // blocks < devices // 2
    near_shape = jax.ShapeDtypeStruct(((block_rows + 2) * 8, width), jnp.float32)
    pooled, valid = call(
        pool_kernel,
        (near_shape, near_shape),
        (mine, other, jnp.asarray(places), instance_weight),
        [pltpu.VMEM((devices * 8, 128), jnp.float32)],
        near=(block_rows, block_cols),
        coarse=(coarse_rows, band_cols),
    )
    channels = width_share * col_devices
    if direct:
        sources, base = (mine, other), mine
    else:
        even = my_col % 2 == 0
        sides = [jnp.where(even, mine, other), jnp.where(even, other, mine)]
        gathered = jnp.stack([side[:, :main_rows] for side in sides], 1).reshape(
            row_devices, col_devices, band_rows, band_cols, width_share
        )
        source = gathered.transpose(0, 2, 3, 1, 4).reshape(coarse_rows * band_cols, channels)
        sources = (source, source)
        column = lax.dynamic_index_in_dim(gathered, my_col, 1, keepdims=False)
        column = jnp.pad(
            column.reshape(coarse_rows, band_cols, width_share), ((1, 1), (0, 0), (0, 0))
        )
        base = lax.dynamic_slice_in_dim(column, my_row * band_rows, band_rows + 2, 0)
        base = base.reshape(-1, width_share)
    near_rows = band_rows + 4
    sent_hidden = call(
        hidden_kernel,
        jax.ShapeDtypeStruct((col_devices, near_rows * band_cols, width_share), jnp.bfloat16),
        (*sources, global_first),
        [
            pltpu.VMEM(((coarse_rows + 2) * band_cols, channels), jnp.bfloat16),
            pltpu.VMEM((coarse_rows, band_cols + 16, width_share), jnp.float32),
            pltpu.VMEM((coarse_rows + 4, band_cols, width_share), jnp.bfloat16),
        ],
        18 * coarse_rows * band_cols * channels * width_share,
        far_out=(0,),
        grid=grid,
        band=band,
        direct=direct,
    )
    near_hidden = to_all(sent_hidden, "cols")
    tall_last, tall_first, _ = lax.optimization_barrier((tall_last, tall_first, sent_hidden))
    left = lax.ppermute(tall_last, "cols", col_up)
    right = lax.ppermute(tall_first, "cols", col_down)
    strip = jnp.concatenate(
        [
            jnp.pad(right, ((0, 0), (1, 0), (0, 0), (0, 0))),
            jnp.pad(left, ((0, 0), (0, 1), (0, 0), (0, 0))),
        ],
        2,
    )
    act_grad = call(
        cot_kernel,
        jax.ShapeDtypeStruct((lay.out, width), jnp.bfloat16),
        (output_cotangent, top, bottom, strip, enhancer_second),
        [pltpu.VMEM((lay.flat, width), jnp.bfloat16), square, *z],
        conv_flops,
        pick={1: 1, 2: 1, 3: 1},
        lay=lay,
    )

    sent_coarse = call(
        project_kernel,
        jax.ShapeDtypeStruct((col_devices, band_rows + 2, 8, width), jnp.float32),
        (near_hidden, global_second, base, project_weight),
        [
            pltpu.VMEM((near_rows * band_cols, channels), jnp.bfloat16),
            pltpu.VMEM((band_rows + 2, band_cols + 16, width_share), jnp.float32),
            pltpu.VMEM((coarse_rows + 2, band_cols, width_share), jnp.bfloat16),
            pltpu.VMEM((band_rows + 2, band_cols + 16, width), jnp.float32),
        ],
        18 * (band_rows + 2) * band_cols * channels * width_share,
        far=(3,),
        stream=1,
        limit=63438848,
        far_out=(0,),
        grid=grid,
        band=band,
        direct=direct,
    )
    near_coarse = to_all(sent_coarse, "cols")
    terms = (near_coarse, pooled.reshape(-1, 8, width), valid.reshape(-1, 8, width))

    mixed, first_act, stats = call(
        mixed_kernel,
        (flat_shape, out_shape, stats_shape),
        (enhancer_input, top, bottom, strip, *terms, enhancer_first),
        [square, pltpu.VMEM((block_rows + 2, 8, width), jnp.float32), *z],
        conv_flops,
        pick={1: 0, 2: 0, 3: 0},
        far_out=(2,),
        lay=lay,
    )
    stats = to_all(stats, BOTH)
    grad_stats = call(
        norm_kernel,
        stats_shape,
        (first_act, stats, act_grad),
        far_out=(0,),
        lay=lay,
        pixel_total=pixel_total,
    )
    grad_stats = to_all(grad_stats, BOTH)
    flat_scratch = pltpu.VMEM((lay.flat, width), jnp.bfloat16)
    second_sent = call(
        second_kernel,
        half_shape,
        (first_act, stats, output_cotangent),
        [flat_scratch, own, total],
        conv_flops,
        lay=lay,
        chunk=chunk,
        grid=grid,
        pixel_total=pixel_total,
    )
    sent_both, kept = call(
        first_kernel,
        (sent_shape, jax.ShapeDtypeStruct((lay.kept, width), jnp.bfloat16)),
        (stats, grad_stats, first_act, act_grad, mixed, second_sent),
        [own, total],
        conv_flops,
        far_out=(0,),
        lay=lay,
        grid=grid,
        chunk=chunk,
        pixel_total=pixel_total,
    )
    part = to_all(sent_both, BOTH)
    late_stats, _ = lax.optimization_barrier((stats, sent_both))
    enhanced = call(
        enhanced_kernel,
        jax.ShapeDtypeStruct((tile_rows, tile_cols, width), jnp.bfloat16),
        (first_act, late_stats, mixed, enhancer_second),
        [flat_scratch, square, *z],
        conv_flops,
        lay=lay,
        grid=grid,
        pixel_total=pixel_total,
    )
    rescale = 1.0 / math.sqrt(pixel_total)
    global_gradient = call(
        coarse_kernel,
        jax.ShapeDtypeStruct((blocks, width), jnp.float32),
        (kept, window_picks(lay), output_cotangent, enhancer_first),
        (),
        lay=lay,
    )
    part, global_gradient, enhanced = lax.optimization_barrier((part, global_gradient, enhanced))
    share = call(share_kernel, half_shape, (part,), rescale=rescale)
    share = among_cores(share, row_devices, col_devices)
    shares = (share, core_swap(share, col_devices))
    whole_shape = jax.ShapeDtypeStruct((9 * width, width), jnp.float32)
    first_total, second_total = call(
        join_kernel, (whole_shape, whole_shape), shares, chunk=chunk, grid=grid
    )
    return (
        enhanced,
        first_total.reshape(3, 3, width, width),
        second_total.reshape(3, 3, width, width),
        global_gradient.reshape(block_rows, block_cols, width),
    )


def solution(mesh):
    return jax.shard_map(
        per_device,
        mesh=mesh,
        in_specs=(
            P("rows", None, "cols"),
            P(None, None, None, "cols"),
            P(None, None, None, "cols"),
            P(),
            P("rows", "cols", None),
            P("rows", "cols"),
            P(None, "rows", "cols"),
            P(),
            P(),
            P(),
            P("rows", "cols", None),
        ),
        out_specs=(P("rows", "cols", None), P(), P(), P("rows", "cols", None)),
        check_vma=False,
    )
```

```python
import math

import jax
import jax.numpy as jnp
import numpy as np
from jax import lax
from jax.experimental import pallas as pl
from jax.experimental.pallas import tpu as pltpu
from jax.sharding import PartitionSpec as P

INSTANCES = 256
UPSCALE = 16
BOTH = ("rows", "cols")

norm_eps = 1e-05


RIM = 8
MARGIN = 16
KERNEL_VMEM = 20 * 1024 * 1024


class Layout:
    def __init__(self, tile_rows, tile_cols):
        self.rows, self.cols = tile_rows, tile_cols
        self.wide = tile_cols + 2 * RIM
        self.flat = (tile_rows + 6) * self.wide + 2 * MARGIN
        self.out_rows = tile_rows + 3
        self.out = self.out_rows * self.wide
        self.z = self.out + 2 * MARGIN
        self.own = tile_rows * self.wide + 2 * MARGIN
        self.kept = -(-self.out // 128) * 128


def call(
    body, outs, ins, scratch=(), flops=0, far=(), pick=None, far_out=(), limit=KERNEL_VMEM, **fixed
):
    pick = pick or {}
    single = not isinstance(outs, tuple)
    outs = (outs,) if single else outs
    n_in, n_out, n_own = len(ins), len(outs), len(scratch)
    near = pl.BlockSpec(memory_space=pltpu.VMEM)
    hbm = pl.BlockSpec(memory_space=pltpu.MemorySpace.HBM)
    landing = [pltpu.VMEM(ins[i].shape, ins[i].dtype) for i in far]
    leaving = [pltpu.VMEM(outs[j].shape, outs[j].dtype) for j in far_out]

    def kernel(*refs):
        in_refs, out_refs = list(refs[:n_in]), list(refs[n_in : n_in + n_out])
        rest = refs[n_in + n_out :]
        own, rest = rest[:n_own], rest[n_own:]
        buffers, sems = rest[: len(far) + len(far_out)], rest[len(far) + len(far_out) :]
        starts, results = [], []
        for slot, i in enumerate(far):
            starts.append(pltpu.make_async_copy(in_refs[i], buffers[slot], sems[slot]))
            starts[-1].start()
            in_refs[i] = buffers[slot]
        for slot, j in enumerate(far_out, len(far)):
            results.append((buffers[slot], out_refs[j], sems[slot]))
            out_refs[j] = buffers[slot]
        for i, k in pick.items():
            in_refs[i] = in_refs[i].at[k]
        for copy in starts:
            copy.wait()
        body(*in_refs, *out_refs, *own, **fixed)
        ends = [pltpu.make_async_copy(*triple) for triple in results]
        for copy in ends:
            copy.start()
        for copy in ends:
            copy.wait()

    result = pl.pallas_call(
        kernel,
        out_shape=outs,
        in_specs=[hbm if i in far else near for i in range(n_in)],
        out_specs=tuple(hbm if j in far_out else near for j in range(n_out)),
        scratch_shapes=[
            *scratch,
            *landing,
            *leaving,
            *[pltpu.SemaphoreType.DMA] * (len(landing) + len(leaving)),
        ],
        compiler_params=pltpu.CompilerParams(vmem_limit_bytes=limit),
        cost_estimate=pl.CostEstimate(flops=flops, bytes_accessed=4 << 20, transcendentals=0),
        name=body.__name__,
    )(*ins)
    return result[0] if single else result


def put_tiles(flat_ref, lay, main_ref, top_ref, bottom_ref, strip_ref):
    flat_ref[...] = jnp.zeros_like(flat_ref)
    for k in range(lay.rows + 5):
        base = MARGIN + k * lay.wide
        i = k - 3
        if i >= -2:
            if i < 0:
                row = top_ref[i + 2]
            elif i < lay.rows:
                row = main_ref[i]
            else:
                row = bottom_ref[i - lay.rows]
            flat_ref[base : base + lay.cols] = row
        flat_ref[base + lay.cols : base + lay.wide] = strip_ref[k]


def taps_matmul(flat_ref, square_ref, z_refs, lay, turned):
    count = z_refs[0].shape[0]
    chunks = 3
    step = count // chunks
    width = z_refs[0].shape[1]

    @pl.loop(0, chunks)
    def _(c):
        begin = pl.multiple_of(c * step, 16)
        parts = [flat_ref[pl.ds(begin + shift, step)] for shift in (0, lay.wide, 2 * lay.wide)]
        if turned:
            left = jnp.concatenate(parts[::-1], 1)
            result = lax.dot_general(
                left, square_ref[...], (((1,), (1,)), ((), ())), preferred_element_type=jnp.float32
            )
        else:
            left = jnp.concatenate(parts, 1)
            result = jnp.dot(left, square_ref[...], preferred_element_type=jnp.float32)
        for b in range(3):
            z_refs[b][pl.ds(begin, step)] = result[:, b * width : (b + 1) * width]


def put_square(square_ref, weight_ref, turned):
    width = weight_ref.shape[2]
    for a in range(3):
        for b in range(3):
            r, c = (b, a) if turned else (a, b)
            square_ref[r * width : (r + 1) * width, c * width : (c + 1) * width] = weight_ref[a, b]


def taken(z_refs, begin, count, turned):
    early, late = (2, 0) if turned else (0, 2)
    return (
        z_refs[early][pl.ds(begin + MARGIN - 1, count)]
        + z_refs[1][pl.ds(begin + MARGIN, count)]
        + z_refs[late][pl.ds(begin + MARGIN + 1, count)]
    )


def folded(value):
    return value.reshape(-1, 8, value.shape[-1]).sum(0)


def send_stats(out_ref, first, second):
    sums = jnp.concatenate(
        [jnp.sum(first, 0, keepdims=True), jnp.sum(second, 0, keepdims=True)], 0
    )
    out_ref[...] = jnp.zeros_like(out_ref)
    for d in range(out_ref.shape[0]):
        out_ref[d, 0:2] = sums


def cot_kernel(main, top, bottom, strip, weight, grad_out, flat, square, z0, z1, z2, *, lay):
    put_tiles(flat, lay, main, top, bottom, strip)
    put_square(square, weight, True)
    taps_matmul(flat, square, (z0, z1, z2), lay, True)

    @pl.loop(0, lay.out_rows)
    def _(r):
        begin = pl.multiple_of(r * lay.wide, 16)
        value = taken((z0, z1, z2), begin, lay.wide, True)
        grad_out[pl.ds(begin, lay.wide)] = value.astype(jnp.bfloat16)


def mixed_kernel(
    main, top, bottom, strip, coarse, pooled, valid, weight, flat, act_out, stats, square, terms, z0,
    z1, z2, *, lay
):
    width = main.shape[2]
    flat[...] = jnp.zeros_like(flat)
    blocks = lay.cols // UPSCALE
    near = coarse[0]
    for c in range(1, coarse.shape[0]):
        near = near + coarse[c]
    terms[...] = near.astype(jnp.bfloat16).astype(jnp.float32) * valid[...] + pooled[...]
    for k in range(lay.rows + 5):
        base = MARGIN + k * lay.wide
        i = k - 3
        own, following = (i + UPSCALE) // UPSCALE, (i + 1 + UPSCALE) // UPSCALE

        def spread(block_row, block_col, rows):
            return jnp.broadcast_to(
                terms[block_row, block_col : block_col + 1], (rows, width)
            )

        if i >= -2:
            if i < 0:
                row = top[i + 2]
            elif i < lay.rows:
                row = main[i]
            else:
                row = bottom[i - lay.rows]
            added = jnp.concatenate([spread(own, b + 2, UPSCALE) for b in range(blocks)], 0)
            flat[base : base + lay.cols] = (row.astype(jnp.float32) + added).astype(jnp.bfloat16)
        zero = jnp.zeros((RIM, width), jnp.float32)
        right = spread(own, blocks + 2, RIM) if i >= -2 else zero
        left = spread(following, 1, RIM) if i + 1 < lay.rows + 2 else zero
        flat[base + lay.cols : base + lay.wide] = (
            strip[k].astype(jnp.float32) + jnp.concatenate([right, left], 0)
        ).astype(jnp.bfloat16)
    put_square(square, weight, False)
    taps_matmul(flat, square, (z0, z1, z2), lay, False)

    def step(r, sums):
        begin = pl.multiple_of(r * lay.wide, 16)
        value = taken((z0, z1, z2), begin, lay.wide, False)
        act_out[pl.ds(begin, lay.wide)] = value
        mine = ((r >= 2) & (r < lay.rows + 2)).astype(jnp.float32)
        own_value = value[: lay.cols] * mine
        return sums[0] + folded(own_value), sums[1] + folded(own_value * own_value)

    zero = jnp.zeros((8, width), jnp.float32)
    sums = lax.fori_loop(0, lay.out_rows, step, (zero, zero))
    send_stats(stats, *sums)


def act_moments(stats, pixel_total):
    sums = jnp.sum(stats[...], 0)
    mean = sums[0:1] / pixel_total
    return mean, lax.rsqrt(sums[1:2] / pixel_total - mean * mean + norm_eps)


def inside_masks(lay, width, row_devices, col_devices):
    my_row, my_col = lax.axis_index("rows"), lax.axis_index("cols")
    column = lax.broadcasted_iota(jnp.int32, (lay.wide, width), 0)
    has_right = (my_col < col_devices - 1).astype(jnp.float32)
    has_left = (my_col > 0).astype(jnp.float32)
    near = jnp.where(
        column < lay.cols, 1.0, jnp.where(column < lay.cols + RIM, has_right, 0.0)
    )
    following = jnp.where(column >= lay.cols + RIM, has_left, 0.0)

    def row_inside(i):
        row = my_row * lay.rows + i
        return ((row >= 0) & (row < lay.rows * row_devices)).astype(jnp.float32)

    return lambda r: near * row_inside(r - 2) + following * row_inside(r - 1)


def gated(value):
    gate = 1.0 / (1.0 + jnp.exp(-value))
    return gate, gate * (1.0 + value * (1.0 - gate))


def norm_kernel(act, stats, act_grad, grad_stats, *, lay, pixel_total):
    width = act.shape[1]
    mean, inverse = act_moments(stats, pixel_total)

    def step(i, sums):
        begin = pl.multiple_of((i + 2) * lay.wide, 16)
        normed = (act[pl.ds(begin, lay.cols)] - mean) * inverse
        _, slope = gated(normed)
        grad = act_grad[pl.ds(begin, lay.cols)].astype(jnp.float32) * slope
        return sums[0] + folded(grad), sums[1] + folded(grad * normed)

    zero = jnp.zeros((8, width), jnp.float32)
    sums = lax.fori_loop(0, lay.rows, step, (zero, zero))
    send_stats(grad_stats, *sums)


def weight_matmul(flat_ref, own_ref, total_ref, sent_ref, lay, chunk):
    count = lay.own
    first = MARGIN + 3 * lay.wide - MARGIN
    chunks = 3
    step = count // chunks
    width = own_ref.shape[1]
    total = None
    for c in range(chunks):
        begin = c * step
        left = jnp.concatenate(
            [
                flat_ref[first + begin + a * lay.wide : first + begin + a * lay.wide + step]
                for a in (-1, 0, 1)
            ],
            1,
        )
        right = jnp.concatenate(
            [
                own_ref[MARGIN + begin - b : MARGIN + begin - b + step].astype(jnp.bfloat16)
                for b in (-1, 0, 1)
            ],
            1,
        )
        part = lax.dot_general(
            left, right, (((0,), (0,)), ((), ())), preferred_element_type=jnp.float32
        )
        total = part if total is None else total + part
    for a in range(3):
        for b in range(3):
            total_ref[(a * 3 + b) * width : (a * 3 + b + 1) * width] = total[
                a * width : (a + 1) * width, b * width : (b + 1) * width
            ]
    padded = sent_ref.shape[1]
    for d in range(9 * width // chunk):
        sent_ref[d] = total_ref[d * chunk : d * chunk + padded].astype(jnp.bfloat16)


def activate(activated, act, stats, lay, grid, pixel_total):
    width = act.shape[1]
    mean, inverse = act_moments(stats, pixel_total)
    mask = inside_masks(lay, width, *grid)
    activated[...] = jnp.zeros_like(activated)

    @pl.loop(0, lay.out_rows)
    def _(r):
        begin = pl.multiple_of(r * lay.wide, 16)
        normed = (act[pl.ds(begin, lay.wide)] - mean) * inverse
        gate, _ = gated(normed)
        activated[pl.ds(pl.multiple_of(begin + MARGIN + lay.wide, 16), lay.wide)] = (
            normed * gate * mask(r)
        ).astype(jnp.bfloat16)


def second_kernel(
    act, stats, main, sent, activated, own, total, *, lay, chunk, grid, pixel_total
):
    activate(activated, act, stats, lay, grid, pixel_total)
    own[...] = jnp.zeros_like(own)

    @pl.loop(0, lay.rows)
    def _(i):
        place = pl.multiple_of(i * lay.wide + 2 * MARGIN, 16)
        own[pl.ds(place, lay.cols)] = main[i].astype(jnp.float32)

    weight_matmul(activated, own, total, sent, lay, chunk)


def enhanced_kernel(
    act, stats, mixed, weight, enhanced, activated, square, z0, z1, z2, *, lay, grid, pixel_total
):
    activate(activated, act, stats, lay, grid, pixel_total)
    put_square(square, weight, False)
    taps_matmul(activated, square, (z0, z1, z2), lay, False)

    @pl.loop(0, lay.rows)
    def _(i):
        begin = pl.multiple_of((i + 2) * lay.wide, 16)
        value = taken((z0, z1, z2), begin, lay.cols, False)
        place = pl.multiple_of((i + 3) * lay.wide + MARGIN, 16)
        enhanced[i] = (mixed[pl.ds(place, lay.cols)].astype(jnp.float32) + value).astype(
            jnp.bfloat16
        )


def first_gradient(act, act_grad, stats, grad_stats, pixel_total):
    mean, inverse = act_moments(stats, pixel_total)
    sums = jnp.sum(grad_stats[...], 0)
    grad_mean, cross_mean = sums[0:1] / pixel_total, sums[1:2] / pixel_total

    def value(begin, count):
        normed = (act[pl.ds(begin, count)] - mean) * inverse
        _, slope = gated(normed)
        grad = act_grad[pl.ds(begin, count)].astype(jnp.float32) * slope
        return inverse * (grad - grad_mean - normed * cross_mean)

    return value


def first_kernel(
    stats, grad_stats, act, act_grad, mixed, second, sent, own, total, *, lay, chunk, pixel_total
):
    value = first_gradient(act, act_grad, stats, grad_stats, pixel_total)
    own[...] = jnp.zeros_like(own)

    @pl.loop(0, lay.rows)
    def _(i):
        begin = pl.multiple_of((i + 2) * lay.wide, 16)
        place = pl.multiple_of(i * lay.wide + 2 * MARGIN, 16)
        own[pl.ds(place, lay.cols)] = value(begin, lay.cols)

    weight_matmul(mixed, own, total, sent, lay, chunk)
    for d in range(second.shape[0]):
        sent[second.shape[0] + d] = second[d]


def coarse_kernel(
    stats, grad_stats, act, act_grad, picked, main, weight, out, kept, *, lay, grid, pixel_total
):
    width = weight.shape[2]
    value = first_gradient(act, act_grad, stats, grad_stats, pixel_total)
    mask = inside_masks(lay, width, *grid)
    kept[...] = jnp.zeros_like(kept)

    @pl.loop(0, lay.out_rows)
    def _(r):
        begin = pl.multiple_of(r * lay.wide, 16)
        kept[pl.ds(begin, lay.wide)] = (value(begin, lay.wide) * mask(r)).astype(jnp.bfloat16)

    windows = jnp.dot(picked[...], kept[...], preferred_element_type=jnp.float32)
    block_rows, block_cols = lay.rows // UPSCALE, lay.cols // UPSCALE
    blocks = block_rows * block_cols
    summed = jnp.zeros((blocks, width), jnp.float32)
    for tap in range(9):
        summed = summed + lax.dot_general(
            windows[tap * blocks : (tap + 1) * blocks],
            weight[tap // 3, tap % 3].astype(jnp.float32),
            (((1,), (1,)), ((), ())),
            precision=lax.Precision.HIGHEST,
            preferred_element_type=jnp.float32,
        )
    for bi in range(block_rows):
        rows = jnp.zeros((lay.cols, width), jnp.float32)
        for i in range(UPSCALE):
            rows = rows + main[bi * UPSCALE + i].astype(jnp.float32)
        for bj in range(block_cols):
            k = bi * block_cols + bj
            cot = jnp.sum(rows[bj * UPSCALE : (bj + 1) * UPSCALE], 0, keepdims=True)
            out[k : k + 1] = (cot + summed[k : k + 1]) / UPSCALE


def share_kernel(received, sent, *, rescale):
    total = received[0].astype(jnp.float32)
    for d in range(1, received.shape[0]):
        total = total + received[d].astype(jnp.float32)
    total = (total * rescale).astype(jnp.bfloat16)
    for d in range(sent.shape[0]):
        sent[d] = total


def join_kernel(mine, other, first, second, *, chunk, grid):
    row_devices, col_devices = grid
    half, pairs = row_devices * col_devices // 2, col_devices // 2
    core = lax.axis_index("cols") & 1
    for k in range(2):

        @pl.when(core == k)
        def _():
            for source, side in ((mine, k), (other, 1 - k)):
                for d in range(half):
                    owner = d // pairs * col_devices + d % pairs * 2 + side
                    out = first if owner < half else second
                    begin = owner % half * chunk
                    out[begin : begin + chunk] = source[d].astype(jnp.float32)[:chunk]


def window_picks(lay):
    place = np.arange(lay.kept)
    slot, column = place // lay.wide + 1, place % lay.wide
    behind = column >= lay.cols + RIM
    i = np.where(behind, slot - 2, slot - 3)
    j = np.where(behind, column - lay.wide, column)
    rows = []
    for a in range(3):
        for b in range(3):
            y, x = i + a - 1, j + b - 1
            for bi in range(lay.rows // UPSCALE):
                for bj in range(lay.cols // UPSCALE):
                    rows.append((y // UPSCALE == bi) & (x // UPSCALE == bj) & (place < lay.out))
    return jnp.asarray(np.stack(rows), jnp.bfloat16)


def to_all(payload, axis):
    return lax.all_to_all(payload, axis, 0, 0)


def among_cores(payload, row_devices, col_devices):
    groups = [
        [r * col_devices + 2 * h + k for r in range(row_devices) for h in range(col_devices // 2)]
        for k in range(2)
    ]
    return lax.all_to_all(payload, BOTH, 0, 0, axis_index_groups=groups)


def core_swap(array, col_devices):
    return lax.ppermute(array, "cols", [(c, c ^ 1) for c in range(col_devices)])


def pieces(array):
    high = array.astype(jnp.bfloat16)
    rest = array - high.astype(jnp.float32)
    middle = rest.astype(jnp.bfloat16)
    return high, middle, (rest - middle.astype(jnp.float32)).astype(jnp.bfloat16)


def lane_roll(value, shift):
    return pltpu.roll(value, shift % value.shape[1], 1)


def pack_kernel(features, labels, band, sent, sums):
    encoder_width, tile_rows, tile_cols = features.shape
    block_rows, block_cols = tile_rows // UPSCALE, tile_cols // UPSCALE
    blocks = block_rows * block_cols
    sums[...] = jnp.zeros_like(sums)
    slot = lax.broadcasted_iota(jnp.int32, (blocks, tile_cols), 0)
    column = lax.broadcasted_iota(jnp.int32, (blocks, tile_cols), 1)
    total = jnp.zeros((blocks, 128), jnp.float32)
    for r in range(block_rows):
        sums[0:encoder_width] = jnp.sum(features[:, r * UPSCALE : (r + 1) * UPSCALE], 1)
        sums[encoder_width : encoder_width + 1] = (
            labels[r * UPSCALE : r * UPSCALE + 1].astype(jnp.float32) / UPSCALE
        )
        low = (slot - r * block_cols) * UPSCALE
        picked = ((column >= low) & (column < low + UPSCALE)).astype(jnp.float32)
        total = total + lax.dot_general(
            picked,
            sums[...],
            (((1,), (1,)), ((), ())),
            precision=lax.Precision.HIGHEST,
            preferred_element_type=jnp.float32,
        )
    high, middle, low = pieces(total)
    packed = (
        high.astype(jnp.float32)
        + lane_roll(middle.astype(jnp.float32), 32)
        + lane_roll(low.astype(jnp.float32), 64)
    )
    value = jnp.concatenate([band[...].astype(jnp.float32), packed], 0).astype(jnp.bfloat16)
    for d in range(sent.shape[0]):
        sent[d] = value


def pool_kernel(mine_ref, other_ref, places, weight, pooled, valid, table, *, near, coarse):
    block_rows, block_cols = near
    coarse_rows, coarse_cols = coarse
    encoder_width = weight.shape[0]
    half, rows, _ = mine_ref.shape
    devices = 2 * half
    lane = lax.broadcasted_iota(jnp.int32, (8, 128), 1)
    for d in range(devices):
        part = mine_ref[d] if d < half else other_ref[d - half]
        packed = part.astype(jnp.float32)[rows - 8 :]
        value = packed + lane_roll(packed, -32) + lane_roll(packed, -64)
        table[d * 8 : (d + 1) * 8] = jnp.where(lane <= encoder_width, value, 0.0)
    exact = dict(precision=lax.Precision.HIGHEST, preferred_element_type=jnp.float32)
    row0 = lax.axis_index("rows") * block_rows - 1
    col0 = lax.axis_index("cols") * block_cols - 2

    def position(shape):
        q = lax.broadcasted_iota(jnp.int32, shape, 0)
        return row0 + (q >> 3), col0 + (q & 7)

    count = pooled.shape[0]
    row, col = position((count, devices * 8))
    core = lax.axis_index("cols") & 1
    column = places[1:2] + block_cols * jnp.where(places[2:3] == 1, core, 1 - core)
    chosen = ((row == places[0:1]) & (col == column)).astype(jnp.float32)
    mine = jnp.dot(chosen, table[...], **exact)[:, encoder_width : encoder_width + 1]
    pick = (lane == encoder_width).astype(jnp.float32)
    every = lax.dot_general(pick, table[...], (((1,), (1,)), ((), ())), **exact)[0:1]
    same = (mine == every).astype(jnp.float32)
    sums = jnp.dot(same, table[...], **exact)
    members = jnp.sum(same, 1, keepdims=True) * float(UPSCALE * UPSCALE)
    averages = sums / jnp.maximum(members, 1.0)
    result = jnp.dot(averages[:, :encoder_width], weight[...], **exact)
    row, col = position(pooled.shape)
    inside = (row >= 0) & (row < coarse_rows) & (col >= 0) & (col < coarse_cols)
    pooled[...] = jnp.where(inside, result, 0.0)
    valid[...] = inside.astype(jnp.float32)


def channel_conv(rows_ref, weight, shifted, out_rows, cols):
    width = weight.shape[3]
    count = out_rows * cols
    sums = None
    for a in range(3):
        left = rows_ref[a * cols : a * cols + count]
        if width % 128:
            part = [
                jnp.dot(left, weight[a, b], preferred_element_type=jnp.float32) for b in range(3)
            ]
        else:
            right = jnp.concatenate([weight[a, b] for b in range(3)], 1)
            part = jnp.dot(left, right, preferred_element_type=jnp.float32)
            part = [part[:, b * width : (b + 1) * width] for b in range(3)]
        sums = part if sums is None else [s + p for s, p in zip(sums, part)]
    shifted[...] = jnp.zeros_like(shifted)
    total = sums[1]
    for b in (0, 2):
        shifted[:, 8 : 8 + cols] = sums[b].reshape(out_rows, cols, width)
        total = total + shifted[:, 7 + b : 7 + b + cols].reshape(count, width)
    return total


def hidden_kernel(mine, other, weight, sent, rows_ref, shifted, kept, *, grid, band, direct):
    row_devices, col_devices = grid
    band_rows, cols = band
    coarse_rows = row_devices * band_rows
    width = weight.shape[3]
    rows_ref[...] = jnp.zeros_like(rows_ref)
    if direct:
        pairs = col_devices // 2
        core = lax.axis_index("cols") & 1
        for source, side in ((mine, core), (other, 1 - core)):
            for d in range(row_devices * pairs):
                begin = (1 + d // pairs * band_rows) * cols
                lanes = pl.multiple_of((d % pairs * 2 + side) * width, width)
                rows_ref[begin : begin + band_rows * cols, pl.ds(lanes, width)] = source[
                    d, : band_rows * cols
                ]
    else:
        rows_ref[cols : cols + coarse_rows * cols] = mine[...]
    raw = channel_conv(rows_ref, weight, shifted, coarse_rows, cols)
    pixels = coarse_rows * cols
    mean = jnp.sum(raw, 0, keepdims=True) / pixels
    variance = jnp.sum(raw * raw, 0, keepdims=True) / pixels - mean * mean
    hidden = jnp.maximum((raw - mean) * lax.rsqrt(variance + norm_eps), 0.0)
    kept[...] = jnp.zeros_like(kept)
    kept[2 : 2 + coarse_rows] = hidden.astype(jnp.bfloat16).reshape(coarse_rows, cols, width)
    near = kept[pl.ds(lax.axis_index("rows") * band_rows, band_rows + 4)]
    near = near.reshape((band_rows + 4) * cols, width)
    for d in range(sent.shape[0]):
        sent[d] = near


def project_kernel(
    received, weight, source, project, sent, rows_ref, shifted, residual, spread, *, grid, band,
    direct
):
    row_devices, col_devices = grid
    band_rows, cols = band
    width = weight.shape[3]
    my_col = lax.axis_index("cols")
    for c in range(col_devices):
        rows_ref[:, c * width : (c + 1) * width] = received[c]
    raw = channel_conv(rows_ref, weight, shifted, band_rows + 2, cols)
    count = (band_rows + 2) * cols
    if direct:
        residual[...] = jnp.zeros_like(residual)
        for r in range(row_devices):
            piece = source[r * (col_devices // 2) + (my_col >> 1), : band_rows * cols]
            residual[1 + r * band_rows : 1 + (r + 1) * band_rows] = piece.reshape(
                band_rows, cols, width
            )
        base = residual[pl.ds(lax.axis_index("rows") * band_rows, band_rows + 2)]
        base = base.reshape(count, width)
    else:
        base = source[...]
    result = (base.astype(jnp.float32) + raw).astype(jnp.bfloat16)
    rows = project[pl.ds(pl.multiple_of(my_col * width, width), width)]
    partial = jnp.dot(result, rows, preferred_element_type=jnp.float32)
    spread[...] = jnp.zeros_like(spread)
    spread[:, 8 : 8 + cols] = partial.reshape(band_rows + 2, cols, partial.shape[1])
    step = cols // col_devices
    for j in range(col_devices):
        sent[j] = spread[:, 6 + j * step : 6 + j * step + sent.shape[2]]


def per_device(
    global_in,
    global_first,
    global_second,
    project_weight,
    enhancer_input,
    instance_map,
    encoder_features,
    instance_weight,
    enhancer_first,
    enhancer_second,
    output_cotangent,
):
    row_devices, col_devices = lax.axis_size("rows"), lax.axis_size("cols")
    devices = row_devices * col_devices
    my_row, my_col = lax.axis_index("rows"), lax.axis_index("cols")
    band_rows, band_cols, width_share = global_in.shape
    tile_rows, tile_cols, local_width = enhancer_input.shape
    coarse_rows = band_rows * row_devices
    block_rows = tile_rows // UPSCALE
    block_cols = tile_cols // UPSCALE
    blocks = block_rows * block_cols
    encoder_width = encoder_features.shape[0]

    lay = Layout(tile_rows, tile_cols)
    width = local_width
    grid = (row_devices, col_devices)
    band = (band_rows, band_cols)
    direct = width_share == 128
    main = global_in.reshape(-1, 128)
    main_rows = main.shape[0]
    sent_input = call(
        pack_kernel,
        jax.ShapeDtypeStruct((devices // 2, main_rows + 8, 128), jnp.bfloat16),
        (encoder_features, instance_map, main),
        [pltpu.VMEM((128, tile_cols), jnp.float32)],
        far=(0, 1, 2),
        limit=62 * 1024 * 1024,
    )
    mine = among_cores(sent_input, row_devices, col_devices)
    late_input, late_cotangent, _ = lax.optimization_barrier(
        (enhancer_input, output_cotangent, sent_input)
    )
    tops = jnp.stack([late_input[-2:], late_cotangent[-2:]])
    bottoms = jnp.stack([late_input[:2], late_cotangent[:2]])

    row_up = [(i, i + 1) for i in range(row_devices - 1)]
    row_down = [(j, i) for i, j in row_up]
    col_up = [(i, i + 1) for i in range(col_devices - 1)]
    col_down = [(j, i) for i, j in col_up]
    top = lax.ppermute(tops, "rows", row_up)
    bottom = lax.ppermute(bottoms, "rows", row_down)
    both = jnp.stack([late_input, late_cotangent])
    tall_last = jnp.concatenate([top[:, :, -RIM:], both[:, :, -RIM:], bottom[:, :, -RIM:]], 1)
    tall_first = jnp.concatenate([top[:, :, :RIM], both[:, :, :RIM], bottom[:, :, :RIM]], 1)
    mine, tall_last, tall_first = lax.optimization_barrier((mine, tall_last, tall_first))
    other = core_swap(mine, col_devices)
    pixel_total = float(tile_rows * tile_cols * devices)
    chunk = 18 * width // devices
    padded_chunk = -(-chunk // 8) * 8
    square = pltpu.VMEM((3 * width, 3 * width), jnp.bfloat16)
    z = [pltpu.VMEM((lay.z, width), jnp.float32)] * 3
    own = pltpu.VMEM((lay.own + 2 * MARGIN, width), jnp.float32)
    total = pltpu.VMEM((9 * width + 64, width), jnp.float32)
    flat_shape = jax.ShapeDtypeStruct((lay.flat, width), jnp.bfloat16)
    out_shape = jax.ShapeDtypeStruct((lay.out, width), jnp.float32)
    stats_shape = jax.ShapeDtypeStruct((devices, 8, width), jnp.float32)
    sent_shape = jax.ShapeDtypeStruct((devices, padded_chunk, width), jnp.bfloat16)
    half_shape = jax.ShapeDtypeStruct((devices // 2, padded_chunk, width), jnp.bfloat16)
    conv_flops = 18 * width * width * lay.out

    place = np.arange(devices * blocks)
    owner, slot = place // blocks % (devices // 2), place % blocks
    pairs = col_devices // 2
    places = np.zeros((8, devices * blocks), np.int32)
    places[0] = owner // pairs * block_rows + slot // block_cols
    places[1] = owner % pairs * 2 * block_cols + slot % block_cols
    places[2] = place // blocks < devices // 2
    near_shape = jax.ShapeDtypeStruct(((block_rows + 2) * 8, width), jnp.float32)
    pooled, valid = call(
        pool_kernel,
        (near_shape, near_shape),
        (mine, other, jnp.asarray(places), instance_weight),
        [pltpu.VMEM((devices * 8, 128), jnp.float32)],
        near=(block_rows, block_cols),
        coarse=(coarse_rows, band_cols),
    )
    channels = width_share * col_devices
    if direct:
        sources, base = (mine, other), mine
    else:
        even = my_col % 2 == 0
        sides = [jnp.where(even, mine, other), jnp.where(even, other, mine)]
        gathered = jnp.stack([side[:, :main_rows] for side in sides], 1).reshape(
            row_devices, col_devices, band_rows, band_cols, width_share
        )
        source = gathered.transpose(0, 2, 3, 1, 4).reshape(coarse_rows * band_cols, channels)
        sources = (source, source)
        column = lax.dynamic_index_in_dim(gathered, my_col, 1, keepdims=False)
        column = jnp.pad(
            column.reshape(coarse_rows, band_cols, width_share), ((1, 1), (0, 0), (0, 0))
        )
        base = lax.dynamic_slice_in_dim(column, my_row * band_rows, band_rows + 2, 0)
        base = base.reshape(-1, width_share)
    near_rows = band_rows + 4
    sent_hidden = call(
        hidden_kernel,
        jax.ShapeDtypeStruct((col_devices, near_rows * band_cols, width_share), jnp.bfloat16),
        (*sources, global_first),
        [
            pltpu.VMEM(((coarse_rows + 2) * band_cols, channels), jnp.bfloat16),
            pltpu.VMEM((coarse_rows, band_cols + 16, width_share), jnp.float32),
            pltpu.VMEM((coarse_rows + 4, band_cols, width_share), jnp.bfloat16),
        ],
        18 * coarse_rows * band_cols * channels * width_share,
        far_out=(0,),
        grid=grid,
        band=band,
        direct=direct,
    )
    near_hidden = to_all(sent_hidden, "cols")
    tall_last, tall_first, _ = lax.optimization_barrier((tall_last, tall_first, sent_hidden))
    left = lax.ppermute(tall_last, "cols", col_up)
    right = lax.ppermute(tall_first, "cols", col_down)
    strip = jnp.concatenate(
        [
            jnp.pad(right, ((0, 0), (1, 0), (0, 0), (0, 0))),
            jnp.pad(left, ((0, 0), (0, 1), (0, 0), (0, 0))),
        ],
        2,
    )
    act_grad = call(
        cot_kernel,
        jax.ShapeDtypeStruct((lay.out, width), jnp.bfloat16),
        (output_cotangent, top, bottom, strip, enhancer_second),
        [pltpu.VMEM((lay.flat, width), jnp.bfloat16), square, *z],
        conv_flops,
        pick={1: 1, 2: 1, 3: 1},
        lay=lay,
    )

    sent_coarse = call(
        project_kernel,
        jax.ShapeDtypeStruct((col_devices, band_rows + 2, 8, width), jnp.float32),
        (near_hidden, global_second, base, project_weight),
        [
            pltpu.VMEM((near_rows * band_cols, channels), jnp.bfloat16),
            pltpu.VMEM((band_rows + 2, band_cols + 16, width_share), jnp.float32),
            pltpu.VMEM((coarse_rows + 2, band_cols, width_share), jnp.bfloat16),
            pltpu.VMEM((band_rows + 2, band_cols + 16, width), jnp.float32),
        ],
        18 * (band_rows + 2) * band_cols * channels * width_share,
        far_out=(0,),
        grid=grid,
        band=band,
        direct=direct,
    )
    near_coarse = to_all(sent_coarse, "cols")
    terms = (near_coarse, pooled.reshape(-1, 8, width), valid.reshape(-1, 8, width))

    mixed, first_act, stats = call(
        mixed_kernel,
        (flat_shape, out_shape, stats_shape),
        (enhancer_input, top, bottom, strip, *terms, enhancer_first),
        [square, pltpu.VMEM((block_rows + 2, 8, width), jnp.float32), *z],
        conv_flops,
        pick={1: 0, 2: 0, 3: 0},
        far_out=(2,),
        lay=lay,
    )
    stats = to_all(stats, BOTH)
    grad_stats = call(
        norm_kernel,
        stats_shape,
        (first_act, stats, act_grad),
        far_out=(0,),
        lay=lay,
        pixel_total=pixel_total,
    )
    grad_stats = to_all(grad_stats, BOTH)
    flat_scratch = pltpu.VMEM((lay.flat, width), jnp.bfloat16)
    second_sent = call(
        second_kernel,
        half_shape,
        (first_act, stats, output_cotangent),
        [flat_scratch, own, total],
        conv_flops,
        lay=lay,
        chunk=chunk,
        grid=grid,
        pixel_total=pixel_total,
    )
    sent_both = call(
        first_kernel,
        sent_shape,
        (stats, grad_stats, first_act, act_grad, mixed, second_sent),
        [own, total],
        conv_flops,
        far_out=(0,),
        lay=lay,
        chunk=chunk,
        pixel_total=pixel_total,
    )
    part = to_all(sent_both, BOTH)
    late_stats, late_grad_stats, _ = lax.optimization_barrier((stats, grad_stats, sent_both))
    enhanced = call(
        enhanced_kernel,
        jax.ShapeDtypeStruct((tile_rows, tile_cols, width), jnp.bfloat16),
        (first_act, late_stats, mixed, enhancer_second),
        [flat_scratch, square, *z],
        conv_flops,
        lay=lay,
        grid=grid,
        pixel_total=pixel_total,
    )
    rescale = 1.0 / math.sqrt(pixel_total)
    global_gradient = call(
        coarse_kernel,
        jax.ShapeDtypeStruct((blocks, width), jnp.float32),
        (
            late_stats,
            late_grad_stats,
            first_act,
            act_grad,
            window_picks(lay),
            output_cotangent,
            enhancer_first,
        ),
        [pltpu.VMEM((lay.kept, width), jnp.bfloat16)],
        lay=lay,
        grid=grid,
        pixel_total=pixel_total,
    )
    part, global_gradient, enhanced = lax.optimization_barrier((part, global_gradient, enhanced))
    share = call(share_kernel, half_shape, (part,), rescale=rescale)
    share = among_cores(share, row_devices, col_devices)
    shares = (share, core_swap(share, col_devices))
    whole_shape = jax.ShapeDtypeStruct((9 * width, width), jnp.float32)
    first_total, second_total = call(
        join_kernel, (whole_shape, whole_shape), shares, chunk=chunk, grid=grid
    )
    return (
        enhanced,
        first_total.reshape(3, 3, width, width),
        second_total.reshape(3, 3, width, width),
        global_gradient.reshape(block_rows, block_cols, width),
    )


def solution(mesh):
    return jax.shard_map(
        per_device,
        mesh=mesh,
        in_specs=(
            P("rows", None, "cols"),
            P(None, None, None, "cols"),
            P(None, None, None, "cols"),
            P(),
            P("rows", "cols", None),
            P("rows", "cols"),
            P(None, "rows", "cols"),
            P(),
            P(),
            P(),
            P("rows", "cols", None),
        ),
        out_specs=(P("rows", "cols", None), P(), P(), P("rows", "cols", None)),
        check_vma=False,
    )
```

```python
import math

import jax
import jax.numpy as jnp
import numpy as np
from jax import lax
from jax.experimental import pallas as pl
from jax.experimental.pallas import tpu as pltpu
from jax.sharding import PartitionSpec as P

INSTANCES = 256
UPSCALE = 16
BOTH = ("rows", "cols")

norm_eps = 1e-05


RIM = 8
MARGIN = 16
KERNEL_VMEM = 20 * 1024 * 1024


class Layout:
    def __init__(self, tile_rows, tile_cols):
        self.rows, self.cols = tile_rows, tile_cols
        self.wide = tile_cols + 2 * RIM
        self.flat = (tile_rows + 6) * self.wide + 2 * MARGIN
        self.out_rows = tile_rows + 3
        self.out = self.out_rows * self.wide
        self.z = self.out + 2 * MARGIN
        self.own = tile_rows * self.wide + 2 * MARGIN
        self.kept = -(-self.out // 128) * 128


def call(
    body, outs, ins, scratch=(), flops=0, far=(), pick=None, far_out=(), limit=KERNEL_VMEM, **fixed
):
    pick = pick or {}
    single = not isinstance(outs, tuple)
    outs = (outs,) if single else outs
    n_in, n_out, n_own = len(ins), len(outs), len(scratch)
    near = pl.BlockSpec(memory_space=pltpu.VMEM)
    hbm = pl.BlockSpec(memory_space=pltpu.MemorySpace.HBM)
    landing = [pltpu.VMEM(ins[i].shape, ins[i].dtype) for i in far]
    leaving = [pltpu.VMEM(outs[j].shape, outs[j].dtype) for j in far_out]

    def kernel(*refs):
        in_refs, out_refs = list(refs[:n_in]), list(refs[n_in : n_in + n_out])
        rest = refs[n_in + n_out :]
        own, rest = rest[:n_own], rest[n_own:]
        buffers, sems = rest[: len(far) + len(far_out)], rest[len(far) + len(far_out) :]
        starts, results = [], []
        for slot, i in enumerate(far):
            starts.append(pltpu.make_async_copy(in_refs[i], buffers[slot], sems[slot]))
            starts[-1].start()
            in_refs[i] = buffers[slot]
        for slot, j in enumerate(far_out, len(far)):
            results.append((buffers[slot], out_refs[j], sems[slot]))
            out_refs[j] = buffers[slot]
        for i, k in pick.items():
            in_refs[i] = in_refs[i].at[k]
        for copy in starts:
            copy.wait()
        body(*in_refs, *out_refs, *own, **fixed)
        ends = [pltpu.make_async_copy(*triple) for triple in results]
        for copy in ends:
            copy.start()
        for copy in ends:
            copy.wait()

    result = pl.pallas_call(
        kernel,
        out_shape=outs,
        in_specs=[hbm if i in far else near for i in range(n_in)],
        out_specs=tuple(hbm if j in far_out else near for j in range(n_out)),
        scratch_shapes=[
            *scratch,
            *landing,
            *leaving,
            *[pltpu.SemaphoreType.DMA] * (len(landing) + len(leaving)),
        ],
        compiler_params=pltpu.CompilerParams(vmem_limit_bytes=limit),
        cost_estimate=pl.CostEstimate(flops=flops, bytes_accessed=4 << 20, transcendentals=0),
        name=body.__name__,
    )(*ins)
    return result[0] if single else result


def put_tiles(flat_ref, lay, main_ref, top_ref, bottom_ref, strip_ref):
    flat_ref[...] = jnp.zeros_like(flat_ref)
    for k in range(lay.rows + 5):
        base = MARGIN + k * lay.wide
        i = k - 3
        if i >= -2:
            if i < 0:
                row = top_ref[i + 2]
            elif i < lay.rows:
                row = main_ref[i]
            else:
                row = bottom_ref[i - lay.rows]
            flat_ref[base : base + lay.cols] = row
        flat_ref[base + lay.cols : base + lay.wide] = strip_ref[k]


def taps_matmul(flat_ref, square_ref, z_refs, lay, turned):
    count = z_refs[0].shape[0]
    chunks = 3
    step = count // chunks
    width = z_refs[0].shape[1]

    @pl.loop(0, chunks)
    def _(c):
        begin = pl.multiple_of(c * step, 16)
        parts = [flat_ref[pl.ds(begin + shift, step)] for shift in (0, lay.wide, 2 * lay.wide)]
        if turned:
            left = jnp.concatenate(parts[::-1], 1)
            result = lax.dot_general(
                left, square_ref[...], (((1,), (1,)), ((), ())), preferred_element_type=jnp.float32
            )
        else:
            left = jnp.concatenate(parts, 1)
            result = jnp.dot(left, square_ref[...], preferred_element_type=jnp.float32)
        for b in range(3):
            z_refs[b][pl.ds(begin, step)] = result[:, b * width : (b + 1) * width]


def put_square(square_ref, weight_ref, turned):
    width = weight_ref.shape[2]
    for a in range(3):
        for b in range(3):
            r, c = (b, a) if turned else (a, b)
            square_ref[r * width : (r + 1) * width, c * width : (c + 1) * width] = weight_ref[a, b]


def taken(z_refs, begin, count, turned):
    early, late = (2, 0) if turned else (0, 2)
    return (
        z_refs[early][pl.ds(begin + MARGIN - 1, count)]
        + z_refs[1][pl.ds(begin + MARGIN, count)]
        + z_refs[late][pl.ds(begin + MARGIN + 1, count)]
    )


def folded(value):
    return value.reshape(-1, 8, value.shape[-1]).sum(0)


def send_stats(out_ref, first, second):
    sums = jnp.concatenate(
        [jnp.sum(first, 0, keepdims=True), jnp.sum(second, 0, keepdims=True)], 0
    )
    out_ref[...] = jnp.zeros_like(out_ref)
    for d in range(out_ref.shape[0]):
        out_ref[d, 0:2] = sums


def cot_kernel(main, top, bottom, strip, weight, grad_out, flat, square, z0, z1, z2, *, lay):
    put_tiles(flat, lay, main, top, bottom, strip)
    put_square(square, weight, True)
    taps_matmul(flat, square, (z0, z1, z2), lay, True)

    @pl.loop(0, lay.out_rows)
    def _(r):
        begin = pl.multiple_of(r * lay.wide, 16)
        value = taken((z0, z1, z2), begin, lay.wide, True)
        grad_out[pl.ds(begin, lay.wide)] = value.astype(jnp.bfloat16)


def mixed_kernel(
    main, top, bottom, strip, coarse, pooled, valid, weight, flat, act_out, stats, square, terms, z0,
    z1, z2, *, lay
):
    width = main.shape[2]
    flat[...] = jnp.zeros_like(flat)
    blocks = lay.cols // UPSCALE
    near = coarse[0]
    for c in range(1, coarse.shape[0]):
        near = near + coarse[c]
    terms[...] = near.astype(jnp.bfloat16).astype(jnp.float32) * valid[...] + pooled[...]
    for k in range(lay.rows + 5):
        base = MARGIN + k * lay.wide
        i = k - 3
        own, following = (i + UPSCALE) // UPSCALE, (i + 1 + UPSCALE) // UPSCALE

        def spread(block_row, block_col, rows):
            return jnp.broadcast_to(
                terms[block_row, block_col : block_col + 1], (rows, width)
            )

        if i >= -2:
            if i < 0:
                row = top[i + 2]
            elif i < lay.rows:
                row = main[i]
            else:
                row = bottom[i - lay.rows]
            added = jnp.concatenate([spread(own, b + 2, UPSCALE) for b in range(blocks)], 0)
            flat[base : base + lay.cols] = (row.astype(jnp.float32) + added).astype(jnp.bfloat16)
        zero = jnp.zeros((RIM, width), jnp.float32)
        right = spread(own, blocks + 2, RIM) if i >= -2 else zero
        left = spread(following, 1, RIM) if i + 1 < lay.rows + 2 else zero
        flat[base + lay.cols : base + lay.wide] = (
            strip[k].astype(jnp.float32) + jnp.concatenate([right, left], 0)
        ).astype(jnp.bfloat16)
    put_square(square, weight, False)
    taps_matmul(flat, square, (z0, z1, z2), lay, False)

    def step(r, sums):
        begin = pl.multiple_of(r * lay.wide, 16)
        value = taken((z0, z1, z2), begin, lay.wide, False)
        act_out[pl.ds(begin, lay.wide)] = value
        mine = ((r >= 2) & (r < lay.rows + 2)).astype(jnp.float32)
        own_value = value[: lay.cols] * mine
        return sums[0] + folded(own_value), sums[1] + folded(own_value * own_value)

    zero = jnp.zeros((8, width), jnp.float32)
    sums = lax.fori_loop(0, lay.out_rows, step, (zero, zero))
    send_stats(stats, *sums)


def act_moments(stats, pixel_total):
    sums = jnp.sum(stats[...], 0)
    mean = sums[0:1] / pixel_total
    return mean, lax.rsqrt(sums[1:2] / pixel_total - mean * mean + norm_eps)


def inside_masks(lay, width, row_devices, col_devices):
    my_row, my_col = lax.axis_index("rows"), lax.axis_index("cols")
    column = lax.broadcasted_iota(jnp.int32, (lay.wide, width), 0)
    has_right = (my_col < col_devices - 1).astype(jnp.float32)
    has_left = (my_col > 0).astype(jnp.float32)
    near = jnp.where(
        column < lay.cols, 1.0, jnp.where(column < lay.cols + RIM, has_right, 0.0)
    )
    following = jnp.where(column >= lay.cols + RIM, has_left, 0.0)

    def row_inside(i):
        row = my_row * lay.rows + i
        return ((row >= 0) & (row < lay.rows * row_devices)).astype(jnp.float32)

    return lambda r: near * row_inside(r - 2) + following * row_inside(r - 1)


def gated(value):
    gate = 1.0 / (1.0 + jnp.exp(-value))
    return gate, gate * (1.0 + value * (1.0 - gate))


def norm_kernel(act, stats, act_grad, grad_stats, *, lay, pixel_total):
    width = act.shape[1]
    mean, inverse = act_moments(stats, pixel_total)

    def step(i, sums):
        begin = pl.multiple_of((i + 2) * lay.wide, 16)
        normed = (act[pl.ds(begin, lay.cols)] - mean) * inverse
        _, slope = gated(normed)
        grad = act_grad[pl.ds(begin, lay.cols)].astype(jnp.float32) * slope
        return sums[0] + folded(grad), sums[1] + folded(grad * normed)

    zero = jnp.zeros((8, width), jnp.float32)
    sums = lax.fori_loop(0, lay.rows, step, (zero, zero))
    send_stats(grad_stats, *sums)


def weight_matmul(flat_ref, own_ref, total_ref, sent_ref, lay, chunk):
    count = lay.own
    first = MARGIN + 3 * lay.wide - MARGIN
    chunks = 3
    step = count // chunks
    width = own_ref.shape[1]
    total = None
    for c in range(chunks):
        begin = c * step
        left = jnp.concatenate(
            [
                flat_ref[first + begin + a * lay.wide : first + begin + a * lay.wide + step]
                for a in (-1, 0, 1)
            ],
            1,
        )
        right = jnp.concatenate(
            [
                own_ref[MARGIN + begin - b : MARGIN + begin - b + step].astype(jnp.bfloat16)
                for b in (-1, 0, 1)
            ],
            1,
        )
        part = lax.dot_general(
            left, right, (((0,), (0,)), ((), ())), preferred_element_type=jnp.float32
        )
        total = part if total is None else total + part
    for a in range(3):
        for b in range(3):
            total_ref[(a * 3 + b) * width : (a * 3 + b + 1) * width] = total[
                a * width : (a + 1) * width, b * width : (b + 1) * width
            ]
    padded = sent_ref.shape[1]
    for d in range(9 * width // chunk):
        sent_ref[d] = total_ref[d * chunk : d * chunk + padded].astype(jnp.bfloat16)


def activate(activated, act, stats, lay, grid, pixel_total):
    width = act.shape[1]
    mean, inverse = act_moments(stats, pixel_total)
    mask = inside_masks(lay, width, *grid)
    activated[...] = jnp.zeros_like(activated)

    @pl.loop(0, lay.out_rows)
    def _(r):
        begin = pl.multiple_of(r * lay.wide, 16)
        normed = (act[pl.ds(begin, lay.wide)] - mean) * inverse
        gate, _ = gated(normed)
        activated[pl.ds(pl.multiple_of(begin + MARGIN + lay.wide, 16), lay.wide)] = (
            normed * gate * mask(r)
        ).astype(jnp.bfloat16)


def second_kernel(
    act, stats, main, sent, activated, own, total, *, lay, chunk, grid, pixel_total
):
    activate(activated, act, stats, lay, grid, pixel_total)
    own[...] = jnp.zeros_like(own)

    @pl.loop(0, lay.rows)
    def _(i):
        place = pl.multiple_of(i * lay.wide + 2 * MARGIN, 16)
        own[pl.ds(place, lay.cols)] = main[i].astype(jnp.float32)

    weight_matmul(activated, own, total, sent, lay, chunk)


def enhanced_kernel(
    act, stats, mixed, weight, enhanced, activated, square, z0, z1, z2, *, lay, grid, pixel_total
):
    activate(activated, act, stats, lay, grid, pixel_total)
    put_square(square, weight, False)
    taps_matmul(activated, square, (z0, z1, z2), lay, False)

    @pl.loop(0, lay.rows)
    def _(i):
        begin = pl.multiple_of((i + 2) * lay.wide, 16)
        value = taken((z0, z1, z2), begin, lay.cols, False)
        place = pl.multiple_of((i + 3) * lay.wide + MARGIN, 16)
        enhanced[i] = (mixed[pl.ds(place, lay.cols)].astype(jnp.float32) + value).astype(
            jnp.bfloat16
        )


def first_gradient(act, act_grad, stats, grad_stats, pixel_total):
    mean, inverse = act_moments(stats, pixel_total)
    sums = jnp.sum(grad_stats[...], 0)
    grad_mean, cross_mean = sums[0:1] / pixel_total, sums[1:2] / pixel_total

    def value(begin, count):
        normed = (act[pl.ds(begin, count)] - mean) * inverse
        _, slope = gated(normed)
        grad = act_grad[pl.ds(begin, count)].astype(jnp.float32) * slope
        return inverse * (grad - grad_mean - normed * cross_mean)

    return value


def first_kernel(
    stats, grad_stats, act, act_grad, mixed, sent, own, total, *, lay, chunk, pixel_total
):
    value = first_gradient(act, act_grad, stats, grad_stats, pixel_total)
    own[...] = jnp.zeros_like(own)

    @pl.loop(0, lay.rows)
    def _(i):
        begin = pl.multiple_of((i + 2) * lay.wide, 16)
        place = pl.multiple_of(i * lay.wide + 2 * MARGIN, 16)
        own[pl.ds(place, lay.cols)] = value(begin, lay.cols)

    weight_matmul(mixed, own, total, sent, lay, chunk)


def coarse_kernel(
    stats, grad_stats, act, act_grad, picked, main, weight, out, kept, *, lay, grid, pixel_total
):
    width = weight.shape[2]
    value = first_gradient(act, act_grad, stats, grad_stats, pixel_total)
    mask = inside_masks(lay, width, *grid)
    kept[...] = jnp.zeros_like(kept)

    @pl.loop(0, lay.out_rows)
    def _(r):
        begin = pl.multiple_of(r * lay.wide, 16)
        kept[pl.ds(begin, lay.wide)] = (value(begin, lay.wide) * mask(r)).astype(jnp.bfloat16)

    windows = jnp.dot(picked[...], kept[...], preferred_element_type=jnp.float32)
    block_rows, block_cols = lay.rows // UPSCALE, lay.cols // UPSCALE
    blocks = block_rows * block_cols
    summed = jnp.zeros((blocks, width), jnp.float32)
    for tap in range(9):
        summed = summed + lax.dot_general(
            windows[tap * blocks : (tap + 1) * blocks],
            weight[tap // 3, tap % 3].astype(jnp.float32),
            (((1,), (1,)), ((), ())),
            precision=lax.Precision.HIGHEST,
            preferred_element_type=jnp.float32,
        )
    for bi in range(block_rows):
        rows = jnp.zeros((lay.cols, width), jnp.float32)
        for i in range(UPSCALE):
            rows = rows + main[bi * UPSCALE + i].astype(jnp.float32)
        for bj in range(block_cols):
            k = bi * block_cols + bj
            cot = jnp.sum(rows[bj * UPSCALE : (bj + 1) * UPSCALE], 0, keepdims=True)
            out[k : k + 1] = (cot + summed[k : k + 1]) / UPSCALE


def pair_kernel(first, moved_first, second, moved_second, sent):
    core = lax.axis_index("cols") & 1
    for k, (mine, other) in enumerate(((first, moved_first), (second, moved_second))):

        @pl.when(core == k)
        def _():
            for d in range(sent.shape[0]):
                total = mine[d].astype(jnp.float32) + other[d].astype(jnp.float32)
                sent[d] = total.astype(jnp.bfloat16)


def share_kernel(received, sent, *, rescale):
    total = received[0].astype(jnp.float32)
    for d in range(1, received.shape[0]):
        total = total + received[d].astype(jnp.float32)
    total = (total * rescale).astype(jnp.bfloat16)
    for d in range(sent.shape[0]):
        sent[d] = total


def join_kernel(mine, other, first, second, *, chunk):
    core = lax.axis_index("cols") & 1
    for k, (near, far) in enumerate(((first, second), (second, first))):

        @pl.when(core == k)
        def _():
            for source, out in ((mine, near), (other, far)):
                for d in range(source.shape[0]):
                    out[d * chunk : (d + 1) * chunk] = source[d].astype(jnp.float32)[:chunk]


def window_picks(lay):
    place = np.arange(lay.kept)
    slot, column = place // lay.wide + 1, place % lay.wide
    behind = column >= lay.cols + RIM
    i = np.where(behind, slot - 2, slot - 3)
    j = np.where(behind, column - lay.wide, column)
    rows = []
    for a in range(3):
        for b in range(3):
            y, x = i + a - 1, j + b - 1
            for bi in range(lay.rows // UPSCALE):
                for bj in range(lay.cols // UPSCALE):
                    rows.append((y // UPSCALE == bi) & (x // UPSCALE == bj) & (place < lay.out))
    return jnp.asarray(np.stack(rows), jnp.bfloat16)


def to_all(payload, axis):
    return lax.all_to_all(payload, axis, 0, 0)


def among_cores(payload, row_devices, col_devices):
    groups = [
        [r * col_devices + 2 * h + k for r in range(row_devices) for h in range(col_devices // 2)]
        for k in range(2)
    ]
    return lax.all_to_all(payload, BOTH, 0, 0, axis_index_groups=groups)


def core_swap(array, col_devices):
    return lax.ppermute(array, "cols", [(c, c ^ 1) for c in range(col_devices)])


def pieces(array):
    high = array.astype(jnp.bfloat16)
    rest = array - high.astype(jnp.float32)
    middle = rest.astype(jnp.bfloat16)
    return high, middle, (rest - middle.astype(jnp.float32)).astype(jnp.bfloat16)


def lane_roll(value, shift):
    return pltpu.roll(value, shift % value.shape[1], 1)


def pack_kernel(features, labels, band, sent, sums):
    encoder_width, tile_rows, tile_cols = features.shape
    block_rows, block_cols = tile_rows // UPSCALE, tile_cols // UPSCALE
    blocks = block_rows * block_cols
    sums[...] = jnp.zeros_like(sums)
    slot = lax.broadcasted_iota(jnp.int32, (blocks, tile_cols), 0)
    column = lax.broadcasted_iota(jnp.int32, (blocks, tile_cols), 1)
    total = jnp.zeros((blocks, 128), jnp.float32)
    for r in range(block_rows):
        sums[0:encoder_width] = jnp.sum(features[:, r * UPSCALE : (r + 1) * UPSCALE], 1)
        sums[encoder_width : encoder_width + 1] = (
            labels[r * UPSCALE : r * UPSCALE + 1].astype(jnp.float32) / UPSCALE
        )
        low = (slot - r * block_cols) * UPSCALE
        picked = ((column >= low) & (column < low + UPSCALE)).astype(jnp.float32)
        total = total + lax.dot_general(
            picked,
            sums[...],
            (((1,), (1,)), ((), ())),
            precision=lax.Precision.HIGHEST,
            preferred_element_type=jnp.float32,
        )
    high, middle, low = pieces(total)
    packed = (
        high.astype(jnp.float32)
        + lane_roll(middle.astype(jnp.float32), 32)
        + lane_roll(low.astype(jnp.float32), 64)
    )
    value = jnp.concatenate([band[...].astype(jnp.float32), packed], 0).astype(jnp.bfloat16)
    for d in range(sent.shape[0]):
        sent[d] = value


def pool_kernel(mine_ref, other_ref, places, weight, pooled, valid, table, *, near, coarse):
    block_rows, block_cols = near
    coarse_rows, coarse_cols = coarse
    encoder_width = weight.shape[0]
    half, rows, _ = mine_ref.shape
    devices = 2 * half
    lane = lax.broadcasted_iota(jnp.int32, (8, 128), 1)
    for d in range(devices):
        part = mine_ref[d] if d < half else other_ref[d - half]
        packed = part.astype(jnp.float32)[rows - 8 :]
        value = packed + lane_roll(packed, -32) + lane_roll(packed, -64)
        table[d * 8 : (d + 1) * 8] = jnp.where(lane <= encoder_width, value, 0.0)
    exact = dict(precision=lax.Precision.HIGHEST, preferred_element_type=jnp.float32)
    row0 = lax.axis_index("rows") * block_rows - 1
    col0 = lax.axis_index("cols") * block_cols - 2

    def position(shape):
        q = lax.broadcasted_iota(jnp.int32, shape, 0)
        return row0 + (q >> 3), col0 + (q & 7)

    count = pooled.shape[0]
    row, col = position((count, devices * 8))
    core = lax.axis_index("cols") & 1
    column = places[1:2] + block_cols * jnp.where(places[2:3] == 1, core, 1 - core)
    chosen = ((row == places[0:1]) & (col == column)).astype(jnp.float32)
    mine = jnp.dot(chosen, table[...], **exact)[:, encoder_width : encoder_width + 1]
    pick = (lane == encoder_width).astype(jnp.float32)
    every = lax.dot_general(pick, table[...], (((1,), (1,)), ((), ())), **exact)[0:1]
    same = (mine == every).astype(jnp.float32)
    sums = jnp.dot(same, table[...], **exact)
    members = jnp.sum(same, 1, keepdims=True) * float(UPSCALE * UPSCALE)
    averages = sums / jnp.maximum(members, 1.0)
    result = jnp.dot(averages[:, :encoder_width], weight[...], **exact)
    row, col = position(pooled.shape)
    inside = (row >= 0) & (row < coarse_rows) & (col >= 0) & (col < coarse_cols)
    pooled[...] = jnp.where(inside, result, 0.0)
    valid[...] = inside.astype(jnp.float32)


def channel_conv(rows_ref, weight, shifted, out_rows, cols):
    width = weight.shape[3]
    count = out_rows * cols
    sums = None
    for a in range(3):
        left = rows_ref[a * cols : a * cols + count]
        if width % 128:
            part = [
                jnp.dot(left, weight[a, b], preferred_element_type=jnp.float32) for b in range(3)
            ]
        else:
            right = jnp.concatenate([weight[a, b] for b in range(3)], 1)
            part = jnp.dot(left, right, preferred_element_type=jnp.float32)
            part = [part[:, b * width : (b + 1) * width] for b in range(3)]
        sums = part if sums is None else [s + p for s, p in zip(sums, part)]
    shifted[...] = jnp.zeros_like(shifted)
    total = sums[1]
    for b in (0, 2):
        shifted[:, 8 : 8 + cols] = sums[b].reshape(out_rows, cols, width)
        total = total + shifted[:, 7 + b : 7 + b + cols].reshape(count, width)
    return total


def hidden_kernel(mine, other, weight, sent, rows_ref, shifted, kept, *, grid, band, direct):
    row_devices, col_devices = grid
    band_rows, cols = band
    coarse_rows = row_devices * band_rows
    width = weight.shape[3]
    rows_ref[...] = jnp.zeros_like(rows_ref)
    if direct:
        pairs = col_devices // 2
        core = lax.axis_index("cols") & 1
        for source, side in ((mine, core), (other, 1 - core)):
            for d in range(row_devices * pairs):
                begin = (1 + d // pairs * band_rows) * cols
                lanes = pl.multiple_of((d % pairs * 2 + side) * width, width)
                rows_ref[begin : begin + band_rows * cols, pl.ds(lanes, width)] = source[
                    d, : band_rows * cols
                ]
    else:
        rows_ref[cols : cols + coarse_rows * cols] = mine[...]
    raw = channel_conv(rows_ref, weight, shifted, coarse_rows, cols)
    pixels = coarse_rows * cols
    mean = jnp.sum(raw, 0, keepdims=True) / pixels
    variance = jnp.sum(raw * raw, 0, keepdims=True) / pixels - mean * mean
    hidden = jnp.maximum((raw - mean) * lax.rsqrt(variance + norm_eps), 0.0)
    kept[...] = jnp.zeros_like(kept)
    kept[2 : 2 + coarse_rows] = hidden.astype(jnp.bfloat16).reshape(coarse_rows, cols, width)
    near = kept[pl.ds(lax.axis_index("rows") * band_rows, band_rows + 4)]
    near = near.reshape((band_rows + 4) * cols, width)
    for d in range(sent.shape[0]):
        sent[d] = near


def project_kernel(
    received, weight, source, project, sent, rows_ref, shifted, residual, spread, *, grid, band,
    direct
):
    row_devices, col_devices = grid
    band_rows, cols = band
    width = weight.shape[3]
    my_col = lax.axis_index("cols")
    for c in range(col_devices):
        rows_ref[:, c * width : (c + 1) * width] = received[c]
    raw = channel_conv(rows_ref, weight, shifted, band_rows + 2, cols)
    count = (band_rows + 2) * cols
    if direct:
        residual[...] = jnp.zeros_like(residual)
        for r in range(row_devices):
            piece = source[r * (col_devices // 2) + (my_col >> 1), : band_rows * cols]
            residual[1 + r * band_rows : 1 + (r + 1) * band_rows] = piece.reshape(
                band_rows, cols, width
            )
        base = residual[pl.ds(lax.axis_index("rows") * band_rows, band_rows + 2)]
        base = base.reshape(count, width)
    else:
        base = source[...]
    result = (base.astype(jnp.float32) + raw).astype(jnp.bfloat16)
    rows = project[pl.ds(pl.multiple_of(my_col * width, width), width)]
    partial = jnp.dot(result, rows, preferred_element_type=jnp.float32)
    spread[...] = jnp.zeros_like(spread)
    spread[:, 8 : 8 + cols] = partial.reshape(band_rows + 2, cols, partial.shape[1])
    step = cols // col_devices
    for j in range(col_devices):
        sent[j] = spread[:, 6 + j * step : 6 + j * step + sent.shape[2]]


def per_device(
    global_in,
    global_first,
    global_second,
    project_weight,
    enhancer_input,
    instance_map,
    encoder_features,
    instance_weight,
    enhancer_first,
    enhancer_second,
    output_cotangent,
):
    row_devices, col_devices = lax.axis_size("rows"), lax.axis_size("cols")
    devices = row_devices * col_devices
    my_row, my_col = lax.axis_index("rows"), lax.axis_index("cols")
    band_rows, band_cols, width_share = global_in.shape
    tile_rows, tile_cols, local_width = enhancer_input.shape
    coarse_rows = band_rows * row_devices
    block_rows = tile_rows // UPSCALE
    block_cols = tile_cols // UPSCALE
    blocks = block_rows * block_cols
    encoder_width = encoder_features.shape[0]

    lay = Layout(tile_rows, tile_cols)
    width = local_width
    grid = (row_devices, col_devices)
    band = (band_rows, band_cols)
    direct = width_share == 128
    main = global_in.reshape(-1, 128)
    main_rows = main.shape[0]
    sent_input = call(
        pack_kernel,
        jax.ShapeDtypeStruct((devices // 2, main_rows + 8, 128), jnp.bfloat16),
        (encoder_features, instance_map, main),
        [pltpu.VMEM((128, tile_cols), jnp.float32)],
        far=(0, 1, 2),
        limit=62 * 1024 * 1024,
    )
    mine = among_cores(sent_input, row_devices, col_devices)
    late_input, late_cotangent, _ = lax.optimization_barrier(
        (enhancer_input, output_cotangent, sent_input)
    )
    tops = jnp.stack([late_input[-2:], late_cotangent[-2:]])
    bottoms = jnp.stack([late_input[:2], late_cotangent[:2]])

    row_up = [(i, i + 1) for i in range(row_devices - 1)]
    row_down = [(j, i) for i, j in row_up]
    col_up = [(i, i + 1) for i in range(col_devices - 1)]
    col_down = [(j, i) for i, j in col_up]
    top = lax.ppermute(tops, "rows", row_up)
    bottom = lax.ppermute(bottoms, "rows", row_down)
    both = jnp.stack([late_input, late_cotangent])
    tall_last = jnp.concatenate([top[:, :, -RIM:], both[:, :, -RIM:], bottom[:, :, -RIM:]], 1)
    tall_first = jnp.concatenate([top[:, :, :RIM], both[:, :, :RIM], bottom[:, :, :RIM]], 1)
    mine, tall_last, tall_first = lax.optimization_barrier((mine, tall_last, tall_first))
    other = core_swap(mine, col_devices)
    pixel_total = float(tile_rows * tile_cols * devices)
    chunk = 18 * width // devices
    padded_chunk = -(-chunk // 8) * 8
    square = pltpu.VMEM((3 * width, 3 * width), jnp.bfloat16)
    z = [pltpu.VMEM((lay.z, width), jnp.float32)] * 3
    own = pltpu.VMEM((lay.own + 2 * MARGIN, width), jnp.float32)
    total = pltpu.VMEM((9 * width + 64, width), jnp.float32)
    flat_shape = jax.ShapeDtypeStruct((lay.flat, width), jnp.bfloat16)
    out_shape = jax.ShapeDtypeStruct((lay.out, width), jnp.float32)
    stats_shape = jax.ShapeDtypeStruct((devices, 8, width), jnp.float32)
    half_shape = jax.ShapeDtypeStruct((devices // 2, padded_chunk, width), jnp.bfloat16)
    conv_flops = 18 * width * width * lay.out

    place = np.arange(devices * blocks)
    owner, slot = place // blocks % (devices // 2), place % blocks
    pairs = col_devices // 2
    places = np.zeros((8, devices * blocks), np.int32)
    places[0] = owner // pairs * block_rows + slot // block_cols
    places[1] = owner % pairs * 2 * block_cols + slot % block_cols
    places[2] = place // blocks < devices // 2
    near_shape = jax.ShapeDtypeStruct(((block_rows + 2) * 8, width), jnp.float32)
    pooled, valid = call(
        pool_kernel,
        (near_shape, near_shape),
        (mine, other, jnp.asarray(places), instance_weight),
        [pltpu.VMEM((devices * 8, 128), jnp.float32)],
        near=(block_rows, block_cols),
        coarse=(coarse_rows, band_cols),
    )
    channels = width_share * col_devices
    if direct:
        sources, base = (mine, other), mine
    else:
        even = my_col % 2 == 0
        sides = [jnp.where(even, mine, other), jnp.where(even, other, mine)]
        gathered = jnp.stack([side[:, :main_rows] for side in sides], 1).reshape(
            row_devices, col_devices, band_rows, band_cols, width_share
        )
        source = gathered.transpose(0, 2, 3, 1, 4).reshape(coarse_rows * band_cols, channels)
        sources = (source, source)
        column = lax.dynamic_index_in_dim(gathered, my_col, 1, keepdims=False)
        column = jnp.pad(
            column.reshape(coarse_rows, band_cols, width_share), ((1, 1), (0, 0), (0, 0))
        )
        base = lax.dynamic_slice_in_dim(column, my_row * band_rows, band_rows + 2, 0)
        base = base.reshape(-1, width_share)
    near_rows = band_rows + 4
    sent_hidden = call(
        hidden_kernel,
        jax.ShapeDtypeStruct((col_devices, near_rows * band_cols, width_share), jnp.bfloat16),
        (*sources, global_first),
        [
            pltpu.VMEM(((coarse_rows + 2) * band_cols, channels), jnp.bfloat16),
            pltpu.VMEM((coarse_rows, band_cols + 16, width_share), jnp.float32),
            pltpu.VMEM((coarse_rows + 4, band_cols, width_share), jnp.bfloat16),
        ],
        18 * coarse_rows * band_cols * channels * width_share,
        far_out=(0,),
        grid=grid,
        band=band,
        direct=direct,
    )
    near_hidden = to_all(sent_hidden, "cols")
    tall_last, tall_first, _ = lax.optimization_barrier((tall_last, tall_first, sent_hidden))
    left = lax.ppermute(tall_last, "cols", col_up)
    right = lax.ppermute(tall_first, "cols", col_down)
    strip = jnp.concatenate(
        [
            jnp.pad(right, ((0, 0), (1, 0), (0, 0), (0, 0))),
            jnp.pad(left, ((0, 0), (0, 1), (0, 0), (0, 0))),
        ],
        2,
    )
    act_grad = call(
        cot_kernel,
        jax.ShapeDtypeStruct((lay.out, width), jnp.bfloat16),
        (output_cotangent, top, bottom, strip, enhancer_second),
        [pltpu.VMEM((lay.flat, width), jnp.bfloat16), square, *z],
        conv_flops,
        pick={1: 1, 2: 1, 3: 1},
        lay=lay,
    )

    sent_coarse = call(
        project_kernel,
        jax.ShapeDtypeStruct((col_devices, band_rows + 2, 8, width), jnp.float32),
        (near_hidden, global_second, base, project_weight),
        [
            pltpu.VMEM((near_rows * band_cols, channels), jnp.bfloat16),
            pltpu.VMEM((band_rows + 2, band_cols + 16, width_share), jnp.float32),
            pltpu.VMEM((coarse_rows + 2, band_cols, width_share), jnp.bfloat16),
            pltpu.VMEM((band_rows + 2, band_cols + 16, width), jnp.float32),
        ],
        18 * (band_rows + 2) * band_cols * channels * width_share,
        far_out=(0,),
        grid=grid,
        band=band,
        direct=direct,
    )
    near_coarse = to_all(sent_coarse, "cols")
    terms = (near_coarse, pooled.reshape(-1, 8, width), valid.reshape(-1, 8, width))

    mixed, first_act, stats = call(
        mixed_kernel,
        (flat_shape, out_shape, stats_shape),
        (enhancer_input, top, bottom, strip, *terms, enhancer_first),
        [square, pltpu.VMEM((block_rows + 2, 8, width), jnp.float32), *z],
        conv_flops,
        pick={1: 0, 2: 0, 3: 0},
        far_out=(2,),
        lay=lay,
    )
    stats = to_all(stats, BOTH)
    grad_stats = call(
        norm_kernel,
        stats_shape,
        (first_act, stats, act_grad),
        far_out=(0,),
        lay=lay,
        pixel_total=pixel_total,
    )
    grad_stats = to_all(grad_stats, BOTH)
    flat_scratch = pltpu.VMEM((lay.flat, width), jnp.bfloat16)
    second_sent = call(
        second_kernel,
        half_shape,
        (first_act, stats, output_cotangent),
        [flat_scratch, own, total],
        conv_flops,
        lay=lay,
        chunk=chunk,
        grid=grid,
        pixel_total=pixel_total,
    )
    moved_second = lax.ppermute(
        second_sent, "cols", [(c, c + 1) for c in range(0, col_devices, 2)]
    )
    first_sent = call(
        first_kernel,
        half_shape,
        (stats, grad_stats, first_act, act_grad, mixed),
        [own, total],
        conv_flops,
        lay=lay,
        chunk=chunk,
        pixel_total=pixel_total,
    )
    moved_first = lax.ppermute(
        first_sent, "cols", [(c + 1, c) for c in range(0, col_devices, 2)]
    )
    pair = call(
        pair_kernel, half_shape, (first_sent, moved_first, second_sent, moved_second)
    )
    part = among_cores(pair, row_devices, col_devices)
    late_stats, late_grad_stats, _ = lax.optimization_barrier((stats, grad_stats, pair))
    enhanced = call(
        enhanced_kernel,
        jax.ShapeDtypeStruct((tile_rows, tile_cols, width), jnp.bfloat16),
        (first_act, late_stats, mixed, enhancer_second),
        [flat_scratch, square, *z],
        conv_flops,
        lay=lay,
        grid=grid,
        pixel_total=pixel_total,
    )
    rescale = 1.0 / math.sqrt(pixel_total)
    global_gradient = call(
        coarse_kernel,
        jax.ShapeDtypeStruct((blocks, width), jnp.float32),
        (
            late_stats,
            late_grad_stats,
            first_act,
            act_grad,
            window_picks(lay),
            output_cotangent,
            enhancer_first,
        ),
        [pltpu.VMEM((lay.kept, width), jnp.bfloat16)],
        lay=lay,
        grid=grid,
        pixel_total=pixel_total,
    )
    part, global_gradient, enhanced = lax.optimization_barrier((part, global_gradient, enhanced))
    share = call(share_kernel, half_shape, (part,), rescale=rescale)
    share = among_cores(share, row_devices, col_devices)
    shares = (share, core_swap(share, col_devices))
    whole_shape = jax.ShapeDtypeStruct((9 * width, width), jnp.float32)
    first_total, second_total = call(
        join_kernel, (whole_shape, whole_shape), shares, chunk=chunk
    )
    return (
        enhanced,
        first_total.reshape(3, 3, width, width),
        second_total.reshape(3, 3, width, width),
        global_gradient.reshape(block_rows, block_cols, width),
    )


def solution(mesh):
    return jax.shard_map(
        per_device,
        mesh=mesh,
        in_specs=(
            P("rows", None, "cols"),
            P(None, None, None, "cols"),
            P(None, None, None, "cols"),
            P(),
            P("rows", "cols", None),
            P("rows", "cols"),
            P(None, "rows", "cols"),
            P(),
            P(),
            P(),
            P("rows", "cols", None),
        ),
        out_specs=(P("rows", "cols", None), P(), P(), P("rows", "cols", None)),
        check_vma=False,
    )
```
